128 devices in a mesh: dp: 8 (over z, x_lo), graph: 16 (over x_hi, y, core).
Axes of the slice: x: 4 (x_hi: 2, x_lo: 2; x = x_hi * 2 + x_lo), y: 4, z: 4, core: 2. Of those that a mesh axis runs over, the one named last changes fastest.
Arguments:
- node_feat: bfloat16 [8, 384, 6272], P('dp', 'graph'), may hold values from -6 to 6
- radial: bfloat16 [8, 12288, 128], P('dp', 'graph'), may hold values from -6 to 6
- src_node: int32 [8, 12288], P('dp', 'graph'), may hold values from 0 to 383, as said below
- dst_node: int32 [8, 12288], P('dp', 'graph'), may hold values from 0 to 383, as said below
- w_query: bfloat16 [128, 128], replicated, may hold values from -0.5 to 0.5
- w_key: bfloat16 [128, 128], replicated, may hold values from -0.5 to 0.5
- w_radial: bfloat16 [128, 896], replicated, may hold values from -0.5 to 0.5
- w_degree: bfloat16 [7, 128, 128], replicated, may hold values from -0.5 to 0.5
- cotangent: bfloat16 [8, 384, 6272], P('dp', 'graph'), may hold values from -6 to 6
Outputs:
- updated: bfloat16 [8, 384, 6272], P('dp', 'graph')
- grad_node: bfloat16 [8, 384, 6272], P('dp', 'graph')
- grad_query: float32 [128, 128], replicated
- grad_key: float32 [128, 128], replicated
- grad_radial: float32 [128, 896], replicated
- grad_degree: float32 [7, 128, 128], replicated
The draws below stay inside these ranges and needn't reach their ends.
Inputs may be any that keep to these rules, and one draw needn't show every extreme that they name: `src_node`: any atom of the structure. `dst_node`: edges at positions k * 768 to (k + 1) * 768 - 1 target atoms k * 24 to (k + 1) * 24 - 1.
All inputs are finite; a program needn't handle non-finite values.
Results may differ from the reference program's by a relative error of at most 0.015.
Values may be sent and summed in bfloat16 or wider, within the bound.
A program may use at most 256 MiB of HBM per device.

```python
import math
import jax
import jax.numpy as jnp
import numpy as np
from jax import lax

C = 128
HEADS = 8
R = 128
NODE_DEV = 24
LMAX1 = 7
LMC = 6272
EDGE_DEV = 768
NODES = 384
EDGES = 12288
STRUCTS = 8
N_GRAPH = 16


def draw_src_node(key, part):
    key = jax.random.fold_in(key, 11)
    chosen = jax.random.randint(key, (STRUCTS, EDGES), 0, NODES, dtype=jnp.int32)
    chosen = chosen.at[:, 0].set(NODES - 1)
    return chosen.at[:, 1].set(0)


def draw_dst_node(key, part):
    key = jax.random.fold_in(key, 23)
    owner_rank = jnp.arange(EDGES, dtype=jnp.int32) // EDGE_DEV
    offset = jax.random.randint(key, (STRUCTS, EDGES), 0, NODE_DEV, dtype=jnp.int32)
    offset = offset.at[:, 0].set(0)
    offset = offset.at[:, EDGES - 1].set(NODE_DEV - 1)
    return owner_rank[None, :] * NODE_DEV + offset


def block_levels(own_key, extent, shards, least, high):
    def one(dim, parts):
        steps = jax.random.uniform(jax.random.fold_in(jax.random.fold_in(own_key, 6), dim), (parts,), jnp.float32, least / len(shards), high / len(shards))
        return jnp.repeat(jnp.exp(steps), extent[dim] // parts).reshape((-1,) + (1,) * (len(extent) - dim - 1))

    gain = one(*shards[0])
    for cut in shards[1:]:
        gain = gain * one(*cut)
    return gain


def bell_draw(key, extent, scale, most, shards=(), held_as=jnp.bfloat16):
    gain = block_levels(key, extent, shards, -0.22, 0.18) if shards else 1.0
    entries = jax.random.normal(key, extent, jnp.float32) * scale * gain
    return jnp.minimum(jnp.maximum(entries, -most), most).astype(held_as)


def setup_inputs(seed: int = 0) -> dict:
    arg_keys = jax.random.split(jax.random.key(seed), 10)
    node_feat = bell_draw(arg_keys[0], (STRUCTS, NODES, LMC), 1.0, 6.0, ((0, 8), (1, 16)))
    radial = bell_draw(arg_keys[1], (STRUCTS, EDGES, R), 1.0, 6.0, ((0, 8), (1, 16)))
    src_node = draw_src_node(jax.random.fold_in(arg_keys[9], 71), 0)
    dst_node = draw_dst_node(jax.random.fold_in(arg_keys[9], 71), 0)
    w_query = bell_draw(arg_keys[4], (C, C), C ** -0.5, 0.5)
    w_key = bell_draw(arg_keys[5], (C, C), C ** -0.5, 0.5)
    w_radial = bell_draw(arg_keys[6], (R, LMAX1 * C), R ** -0.5, 0.5)
    w_degree = bell_draw(arg_keys[7], (LMAX1, C, C), C ** -0.5, 0.5)
    cotangent = bell_draw(arg_keys[8], (STRUCTS, NODES, LMC), 1.0, 6.0, ((0, 8), (1, 16)))
    return dict(node_feat=node_feat, radial=radial, src_node=src_node, dst_node=dst_node, w_query=w_query, w_key=w_key, w_radial=w_radial, w_degree=w_degree, cotangent=cotangent)


def degree_of(count):
    return np.floor(np.sqrt(np.arange(count) + 0.5)).astype(np.int32)

def per_degree(block_fn, packed, levels, channels):
    pieces = []
    for degree in range(levels):
        first_col = degree * degree * channels
        last_col = (degree + 1) * (degree + 1) * channels
        row_block = packed[:, first_col:last_col].reshape(-1, channels)
        pieces.append(block_fn(degree, row_block).reshape(packed.shape[0], -1))
    return jnp.concatenate(pieces, axis=1)

def reference(node_feat, radial, src_node, dst_node, w_query, w_key, w_radial, w_degree, cotangent):
    channels = w_query.shape[0]
    levels = w_degree.shape[0]
    coeffs = levels * levels
    packed_width = coeffs * channels
    head_size = channels // HEADS
    logit_scale = 1.0 / math.sqrt(head_size)
    table = degree_of(coeffs)
    fold_table = jnp.asarray((table[:, None] == np.arange(levels)[None, :]).astype(np.float32))
    highest = lax.Precision.HIGHEST
    key_float = w_key.astype(jnp.float32)
    query_float = w_query.astype(jnp.float32)
    total_query = jnp.zeros((channels, channels), jnp.float32)
    total_key = jnp.zeros((channels, channels), jnp.float32)
    total_radial = jnp.zeros(w_radial.shape, jnp.float32)
    total_degree = jnp.zeros(w_degree.shape, jnp.float32)
    updated_list = []
    grad_list = []
    for member in range(STRUCTS):
        node_rows = node_feat[member]
        upstream = cotangent[member]
        src_blocks = src_node[member].reshape(N_GRAPH, EDGE_DEV)
        dst_blocks = dst_node[member].reshape(N_GRAPH, EDGE_DEV)
        rad_blocks = radial[member].reshape(N_GRAPH, EDGE_DEV, -1)
        query = jnp.dot(node_rows[:, :channels], w_query, preferred_element_type=jnp.float32)

        def edge_state(src_blk, dst_blk, rad_blk):
            edge_x = jnp.take(node_rows, src_blk, axis=0)
            edge_count = edge_x.shape[0]
            pre_gate = jnp.dot(rad_blk, w_radial, preferred_element_type=jnp.float32)
            gate_full = jax.nn.silu(pre_gate).reshape(edge_count, levels, channels)[:, table, :]
            query_edge = jnp.take(query, dst_blk, axis=0)
            key_edge = jnp.dot(edge_x[:, :channels], w_key, preferred_element_type=jnp.float32)
            logits = (query_edge * key_edge).reshape(edge_count, HEADS, head_size).sum(-1) * logit_scale
            attention = jax.nn.sigmoid(logits)
            attn_full = jnp.repeat(attention, head_size, axis=1)
            edge_x3 = edge_x.reshape(edge_count, coeffs, channels).astype(jnp.float32)
            return (edge_x, edge_x3, pre_gate, gate_full, query_edge, key_edge, attention, attn_full)

        def forward_step(carry, blocks):
            src_blk, dst_blk, rad_blk = blocks
            edge_x, edge_x3, pre_gate, gate_full, query_edge, key_edge, attention, attn_full = edge_state(src_blk, dst_blk, rad_blk)
            message = (edge_x3 * gate_full * attn_full[:, None, :]).astype(jnp.bfloat16).reshape(edge_x.shape[0], packed_width)
            return (carry + jax.ops.segment_sum(message.astype(jnp.float32), dst_blk, num_segments=NODES), None)
        summed_msg, ignored = lax.scan(forward_step, jnp.zeros((NODES, packed_width), jnp.float32), (src_blocks, dst_blocks, rad_blocks))
        gathered_sum = summed_msg.astype(jnp.bfloat16)
        mixed = per_degree(lambda degree, row_block: jnp.dot(row_block, w_degree[degree], preferred_element_type=jnp.float32), gathered_sum, levels, channels)
        updated_list.append((node_rows.astype(jnp.float32) + mixed).astype(jnp.bfloat16))
        degree_grads = []
        for degree in range(levels):
            first_col = degree * degree * channels
            last_col = (degree + 1) * (degree + 1) * channels
            left_rows = gathered_sum[:, first_col:last_col].reshape(-1, channels)
            right_rows = upstream[:, first_col:last_col].reshape(-1, channels)
            degree_grads.append(jnp.dot(left_rows.T, right_rows, preferred_element_type=jnp.float32))
        total_degree = total_degree + jnp.stack(degree_grads)
        upstream_sum = per_degree(lambda degree, row_block: jnp.dot(row_block, w_degree[degree].T, preferred_element_type=jnp.float32), upstream, levels, channels).astype(jnp.bfloat16)

        def backward_step(carry, blocks):
            spread, query_node, grad_key_sum, grad_radial_sum = carry
            src_blk, dst_blk, rad_blk = blocks
            edge_x, edge_x3, pre_gate, gate_full, query_edge, key_edge, attention, attn_full = edge_state(src_blk, dst_blk, rad_blk)
            edge_count = edge_x.shape[0]
            edge_grad = jnp.take(upstream_sum, dst_blk, axis=0).astype(jnp.float32).reshape(edge_count, coeffs, channels)
            grad_gate = jnp.einsum('ekc,kl->elc', edge_grad * edge_x3 * attn_full[:, None, :], fold_table, precision=highest)
            grad_attn = lax.optimization_barrier(jnp.sum(edge_grad * edge_x3 * gate_full, axis=1))
            grad_logit = grad_attn.reshape(edge_count, HEADS, head_size).sum(-1) * attention * (1.0 - attention) * logit_scale
            logit_full = jnp.repeat(grad_logit, head_size, axis=1)
            grad_key_edge = logit_full * query_edge
            grad_query_edge = logit_full * key_edge
            grad_key_sum = grad_key_sum + jnp.dot(edge_x[:, :channels].astype(jnp.float32).T, grad_key_edge, precision=highest)
            query_node = query_node + jax.ops.segment_sum(grad_query_edge, dst_blk, num_segments=NODES)
            sigma = jax.nn.sigmoid(pre_gate)
            grad_pre = grad_gate.reshape(edge_count, levels * channels) * sigma * (1.0 + pre_gate * (1.0 - sigma))
            grad_radial_sum = grad_radial_sum + jnp.dot(rad_blk.astype(jnp.float32).T, grad_pre, precision=highest)
            edge_back = (edge_grad * gate_full * attn_full[:, None, :]).reshape(edge_count, packed_width)
            key_back = jnp.dot(grad_key_edge, key_float.T, precision=highest)
            edge_back = jnp.concatenate([edge_back[:, :channels] + key_back, edge_back[:, channels:]], axis=1).astype(jnp.bfloat16)
            block_part = jax.ops.segment_sum(edge_back.astype(jnp.float32), src_blk, num_segments=NODES).astype(jnp.bfloat16)
            block_part = lax.optimization_barrier(block_part)
            spread = spread + block_part.astype(jnp.float32)
            return ((spread, query_node, grad_key_sum, grad_radial_sum), None)
        start_carry = (jnp.zeros((NODES, packed_width), jnp.float32), jnp.zeros((NODES, channels), jnp.float32), jnp.zeros((channels, channels), jnp.float32), jnp.zeros(w_radial.shape, jnp.float32))
        finals, ignored = lax.scan(backward_step, start_carry, (src_blocks, dst_blocks, rad_blocks))
        spread, query_node, grad_key_sum, grad_radial_sum = finals
        total_key = total_key + grad_key_sum
        total_radial = total_radial + grad_radial_sum
        total_query = total_query + jnp.dot(node_rows[:, :channels].astype(jnp.float32).T, query_node, precision=highest)
        query_back = jnp.dot(query_node, query_float.T, precision=highest)
        grad_own = upstream.astype(jnp.float32) + spread
        grad_own = jnp.concatenate([grad_own[:, :channels] + query_back, grad_own[:, channels:]], axis=1)
        grad_list.append(grad_own.astype(jnp.bfloat16))
    return (jnp.stack(updated_list), jnp.stack(grad_list), total_query, total_key, total_radial, total_degree)
```

```python
import functools
import math

import jax
import jax.numpy as jnp
from jax import lax
from jax.experimental import pallas as pl
from jax.experimental.pallas import tpu as pltpu
from jax.sharding import PartitionSpec as P

HEADS = 8
C = 128
LEVELS = 7
NODE_DEV = 24
PAD = 32
EDGE_DEV = 768
NODES = 384
CHIP_ROWS = 48
N_GRAPH = 16
N_DP = 8
HALF_PAIRS = 12
CHUNK = 2
CHUNKS = HALF_PAIRS // CHUNK
ROW_BLOCK = 256
GRAD_ROWS = 2048
GRAD_PIECE = GRAD_ROWS // N_GRAPH
MESH = pl.DeviceIdType.MESH
F32 = jnp.float32
BF16 = jnp.bfloat16

X_OWN, UP_OWN, DOWN_OWN, FAR_OWN, UP_RELAY, DOWN_RELAY, X_RELAY, TO_SIB = range(8)
SUM_SIB, PART_UP, PART_DOWN, PART_X, OWN_UP, OWN_DOWN, TOTAL_X, TOTAL_FAR, LAST_SIB = range(9)


def mm(a, b):
    return jnp.dot(a, b, preferred_element_type=F32)


def mm_nt(a, b):
    return lax.dot_general(a, b, (((1,), (1,)), ((), ())), preferred_element_type=F32)


def mm_tn(a, b):
    return lax.dot_general(a, b, (((0,), (0,)), ((), ())), preferred_element_type=F32)


def two_parts(a):
    high = a.astype(BF16)
    return high, (a - high.astype(F32)).astype(BF16)


def degree_of(k):
    total = 0
    for degree in range(1, LEVELS):
        total = total + (k + 64 - degree * degree) // 64
    return total


def columns(k, count=1):
    return pl.ds(pl.multiple_of(k * C, C), count * C)


def kernel(
    x_ref, rad_ref, src_ref, dst_ref, wq_ref, wk_ref, wr_ref, wd_ref, cot_ref,
    upd_ref, gn_ref, gw_ref,
    xs, sibx, xall, x0all, x0, src_hot, src_t, dst_hot, dst_t,
    gs, g0, gate, slope, scaled, fold, fwd, msg, back,
    part, from_sib, in_part, in_total, last, last_in, p0, in0,
    wpart, win1, win2, wall,
    qe, key, att, ex0, gm0,
    sib_sems, x0_send, x0_recv, ag_send, ag_recv, rs_send, rs_recv,
    r0_send, r0_recv, w1_send, w1_recv, w2_send, w2_recv, w3_send, w3_recv,
):
    dp = lax.axis_index("dp")
    graph = lax.axis_index("graph")
    core = lax.rem(graph, 2)
    chip = graph // 2
    x_hi = chip // 4
    y = lax.rem(chip, 4)
    other = 1 - core

    def chip_at(dx, dy):
        return lax.rem(x_hi + dx, 2) * 4 + lax.rem(y + dy, 4)

    def at(dx, dy):
        return (dp, chip_at(dx, dy) * 2 + core)

    sibling = (dp, chip * 2 + other)

    def rows_of(which):
        return pl.ds(pl.multiple_of(which * CHIP_ROWS, 16), CHIP_ROWS)

    def remote(src, dst, send, recv, device):
        return pltpu.make_async_remote_copy(
            src_ref=src, dst_ref=dst, send_sem=send, recv_sem=recv,
            device_id=device, device_id_type=MESH,
        )

    barrier = pltpu.get_barrier_semaphore()

    @pl.loop(1, N_GRAPH)
    def _(d):
        pl.semaphore_signal(
            barrier, inc=1, device_id=(dp, lax.rem(graph + d, N_GRAPH)), device_id_type=MESH
        )

    @pl.loop(1, N_DP)
    def _(d):
        pl.semaphore_signal(
            barrier, inc=1, device_id=(lax.rem(dp + d, N_DP), graph), device_id_type=MESH
        )

    for pair in range(2 * HALF_PAIRS):
        xs[pair // HALF_PAIRS, pair % HALF_PAIRS, 0:NODE_DEV, :] = x_ref[:, (1 + 2 * pair) * C : (3 + 2 * pair) * C]
        xs[pair // HALF_PAIRS, pair % HALF_PAIRS, NODE_DEV:PAD, :] = jnp.zeros((PAD - NODE_DEV, 2 * C), BF16)
    x0all[graph, 0:NODE_DEV, :] = x_ref[:, 0:C]
    x0all[graph, NODE_DEV:PAD, :] = jnp.zeros((PAD - NODE_DEV, C), BF16)

    pl.semaphore_wait(barrier, N_GRAPH - 1 + N_DP - 1)

    sib_copy = remote(xs.at[other], sibx, sib_sems.at[0], sib_sems.at[1], sibling)
    sib_copy.start()

    def x0_copy(d):
        return remote(
            x0all.at[graph], x0all.at[graph], x0_send.at[d], x0_recv.at[d],
            (dp, lax.rem(graph + d, N_GRAPH)),
        )

    @pl.loop(1, N_GRAPH)
    def _(d):
        x0_copy(d).start()

    sib_copy.wait_recv()
    mine = xs[core, :, 0:NODE_DEV, :].astype(F32)
    theirs = sibx[:, 0:NODE_DEV, :].astype(F32)
    first = jnp.where(core == 0, mine, theirs)
    second = jnp.where(core == 0, theirs, mine)
    xall[core, :, rows_of(chip), :] = jnp.concatenate([first, second], axis=1).astype(BF16)

    def block(j, which):
        return xall.at[core, pl.ds(j * CHUNK, CHUNK), rows_of(which), :]

    def gather_copy(j, kind, which, device):
        return lambda: remote(
            block(j, which), block(j, which), ag_send.at[j, kind], ag_recv.at[j, kind], device
        )

    def gather_first(j):
        return [
            gather_copy(j, X_OWN, chip, at(1, 0)),
            gather_copy(j, UP_OWN, chip, at(0, 1)),
            gather_copy(j, DOWN_OWN, chip, at(0, 3)),
            gather_copy(j, FAR_OWN, chip, at(0, 2)),
        ]

    def gather_second(j):
        return [
            gather_copy(j, UP_RELAY, chip_at(1, 0), at(0, 1)),
            gather_copy(j, DOWN_RELAY, chip_at(1, 0), at(0, 3)),
            gather_copy(j, X_RELAY, chip_at(0, 2), at(1, 0)),
        ]

    def to_sibling(j):
        ref = xall.at[core, pl.ds(j * CHUNK, CHUNK)]
        return remote(ref, ref, ag_send.at[j, TO_SIB], ag_recv.at[j, TO_SIB], sibling)

    def got_block(j, kind, which):
        gather_copy(j, kind, which, at(0, 1))().wait_recv()

    @pl.loop(0, CHUNKS)
    def _(j):
        for copy in gather_first(j):
            copy().start()

    def relay(j):
        got_block(j, X_OWN, chip_at(1, 0))
        got_block(j, FAR_OWN, chip_at(0, 2))
        for copy in gather_second(j):
            copy().start()

    def forward(j):
        got_block(j, UP_OWN, chip_at(0, 3))
        got_block(j, DOWN_OWN, chip_at(0, 1))
        got_block(j, UP_RELAY, chip_at(1, 3))
        got_block(j, DOWN_RELAY, chip_at(1, 1))
        got_block(j, X_RELAY, chip_at(1, 2))
        to_sibling(j).start()

    def from_sibling(j):
        ref = xall.at[other, pl.ds(j * CHUNK, CHUNK)]
        remote(ref, ref, ag_send.at[j, TO_SIB], ag_recv.at[j, TO_SIB], sibling).wait_recv()

    src_row = src_ref[...].astype(F32)
    dst_row = (dst_ref[...] - graph * NODE_DEV).astype(F32)
    src_t[...] = (lax.broadcasted_iota(jnp.int32, (NODES, EDGE_DEV), 0).astype(F32) == src_row).astype(F32).astype(BF16)
    dst_t[...] = (lax.broadcasted_iota(jnp.int32, (PAD, EDGE_DEV), 0).astype(F32) == dst_row).astype(F32).astype(BF16)
    src_col = jnp.broadcast_to(src_row, (8, EDGE_DEV)).T[:, 0:1]
    dst_col = jnp.broadcast_to(dst_row, (8, EDGE_DEV)).T[:, 0:1]
    src_hot[...] = (lax.broadcasted_iota(jnp.int32, (EDGE_DEV, NODES), 1).astype(F32) == src_col).astype(F32).astype(BF16)
    dst_hot[...] = (lax.broadcasted_iota(jnp.int32, (EDGE_DEV, PAD), 1).astype(F32) == dst_col).astype(F32).astype(BF16)

    for degree in range(LEVELS):
        pre = mm(rad_ref[...], wr_ref[:, degree * C : (degree + 1) * C])
        sigma = jax.nn.sigmoid(pre)
        gate[degree] = pre * sigma
        slope[degree] = sigma * (1.0 + pre * (1.0 - sigma))
        fold[degree] = jnp.zeros((EDGE_DEV, C), F32)

    zeros = jnp.zeros((PAD - NODE_DEV, C), F32)
    for degree in range(LEVELS):
        begin, end = degree * degree, (degree + 1) * (degree + 1)
        stacked = jnp.concatenate([cot_ref[:, k * C : (k + 1) * C].astype(F32) for k in range(begin, end)], axis=0)
        mixed = mm_nt(stacked.astype(BF16), wd_ref[degree])
        for k in range(begin, end):
            rows = mixed[(k - begin) * NODE_DEV : (k - begin + 1) * NODE_DEV]
            rows = jnp.concatenate([rows, zeros], axis=0).astype(BF16)
            if k == 0:
                g0[...] = rows
            else:
                lane = (k - 1) % 2
                gs[(k - 1) // 2, :, lane * C : (lane + 1) * C] = rows

    query = jnp.concatenate([mm(x_ref[:, 0:C], wq_ref[...]), zeros], axis=0)
    q_high, q_low = two_parts(query)
    qe[...] = mm(dst_hot[...], q_high) + mm(dst_hot[...], q_low)
    gm0[...] = mm(dst_hot[...], g0[...])

    head_rows = lax.broadcasted_iota(jnp.int32, (C, C), 0) // (C // HEADS)
    head_cols = lax.broadcasted_iota(jnp.int32, (C, C), 1) // (C // HEADS)
    same_head = (head_rows == head_cols).astype(F32).astype(BF16)
    scale = 1.0 / math.sqrt(C // HEADS)

    def head_sum(a):
        high, low = two_parts(a)
        return mm(high, same_head) + mm(low, same_head)

    @pl.loop(1, N_GRAPH)
    def _(d):
        x0_copy(d).wait_recv()

    x0[...] = jnp.concatenate([x0all[d, 0:NODE_DEV, :].astype(F32) for d in range(N_GRAPH)], axis=0).astype(BF16)
    relay(0)
    ex0[...] = mm(src_hot[...], x0[...]).astype(BF16)
    key[...] = mm(ex0[...], wk_ref[...])
    att[...] = jax.nn.sigmoid(head_sum(qe[...] * key[...]) * scale)
    for degree in range(LEVELS):
        scaled[degree] = gate[degree] * att[...]
    ex0_float = ex0[...].astype(F32)
    fold[0] = ex0_float * gm0[...]
    relay(1)
    forward(0)
    fwd[0] = mm(dst_t[...], (ex0_float * scaled[0]).astype(BF16))[0:NODE_DEV]

    def edges(half, t):
        pair = half * HALF_PAIRS + t
        k = 1 + 2 * pair
        left, right = degree_of(k), degree_of(k + 1)
        nodes = xall[half, t]
        ups = gs[pair]
        for begin in range(0, EDGE_DEV, ROW_BLOCK):
            rows = slice(begin, begin + ROW_BLOCK)
            ex = mm(src_hot[rows, :], nodes)
            gm = mm(dst_hot[rows, :], ups)
            for lane, degree in ((0, left), (1, right)):
                cols = slice(lane * C, (lane + 1) * C)
                factor = scaled[degree, rows, :]
                msg[rows, cols] = (ex[:, cols] * factor).astype(BF16)
                back[rows, cols] = (gm[:, cols] * factor).astype(BF16)
                fold[degree, rows, :] += ex[:, cols] * gm[:, cols]
        gathered = mm(dst_t[...], msg[...])
        fwd[k] = gathered[0:NODE_DEV, 0:C]
        fwd[k + 1] = gathered[0:NODE_DEV, C : 2 * C]
        part[half, t] = mm(src_t[...], back[...]).astype(BF16)

    def sum_sibling(j):
        return remote(
            part.at[other, pl.ds(j * CHUNK, CHUNK)], from_sib.at[pl.ds(j * CHUNK, CHUNK)],
            rs_send.at[j, SUM_SIB], rs_recv.at[j, SUM_SIB], sibling,
        )

    def part_block(j, which):
        return part.at[core, pl.ds(j * CHUNK, CHUNK), rows_of(which), :]

    def reduce_copy(j, kind, which, landing, slot, device):
        return lambda: remote(
            part_block(j, which), landing.at[slot, pl.ds(j * CHUNK, CHUNK)],
            rs_send.at[j, kind], rs_recv.at[j, kind], device,
        )

    def reduce_first(j):
        return [
            reduce_copy(j, PART_UP, chip_at(1, 1), in_part, 0, at(0, 1)),
            reduce_copy(j, PART_DOWN, chip_at(1, 3), in_part, 1, at(0, 3)),
            reduce_copy(j, PART_X, chip_at(1, 2), in_part, 2, at(1, 0)),
            reduce_copy(j, OWN_UP, chip_at(0, 1), in_total, 0, at(0, 1)),
            reduce_copy(j, OWN_DOWN, chip_at(0, 3), in_total, 1, at(0, 3)),
        ]

    def reduce_second(j):
        return [
            reduce_copy(j, TOTAL_X, chip_at(1, 0), in_total, 2, at(1, 0)),
            reduce_copy(j, TOTAL_FAR, chip_at(0, 2), in_total, 3, at(0, 2)),
        ]

    def last_copy(j):
        return remote(
            last.at[pl.ds(j * CHUNK, CHUNK), pl.ds(pl.multiple_of(other * NODE_DEV, 8), NODE_DEV), :],
            last_in.at[pl.ds(j * CHUNK, CHUNK)],
            rs_send.at[j, LAST_SIB], rs_recv.at[j, LAST_SIB], sibling,
        )

    def reduce_start(j):
        sum_sibling(j).wait_recv()
        for i in range(CHUNK):
            t = j * CHUNK + i
            part[core, t] = (part[core, t].astype(F32) + from_sib[t].astype(F32)).astype(BF16)
        for copy in reduce_first(j):
            copy().start()

    def reduce_next(j):
        for copy in reduce_first(j)[:3]:
            copy().wait_recv()
        for i in range(CHUNK):
            t = j * CHUNK + i
            rows = rows_of(chip_at(1, 0))
            total = part[core, t, rows, :].astype(F32) + in_part[0, t].astype(F32) + in_part[1, t].astype(F32)
            part[core, t, rows, :] = total.astype(BF16)
            rows = rows_of(chip_at(0, 2))
            total = part[core, t, rows, :].astype(F32) + in_part[2, t].astype(F32)
            part[core, t, rows, :] = total.astype(BF16)
        for copy in reduce_second(j):
            copy().start()

    def reduce_end(j):
        for copy in reduce_first(j)[3:] + reduce_second(j):
            copy().wait_recv()
        for i in range(CHUNK):
            t = j * CHUNK + i
            total = part[core, t, rows_of(chip), :].astype(F32)
            for slot in range(4):
                total = total + in_total[slot, t].astype(F32)
            last[t] = total
        last_copy(j).start()

    @pl.loop(0, CHUNKS)
    def _(s):
        @pl.when(s + 2 < CHUNKS)
        def _():
            relay(s + 2)

        @pl.when(s + 1 < CHUNKS)
        def _():
            forward(s + 1)

        from_sibling(s)

        @pl.loop(0, 2 * CHUNK)
        def _(i):
            half = lax.rem(other + i // CHUNK, 2)
            edges(half, s * CHUNK + lax.rem(i, CHUNK))

            @pl.when(i == CHUNK - 1)
            def _():
                sum_sibling(s).start()

        @pl.when(s >= 1)
        def _():
            reduce_start(s - 1)

        @pl.when(s >= 3)
        def _():
            reduce_next(s - 3)

        @pl.when(s >= 5)
        def _():
            reduce_end(s - 5)

    a = att[...]
    g_att = gate[0] * fold[0]
    for degree in range(1, LEVELS):
        g_att = g_att + gate[degree] * fold[degree]
    g_logit = head_sum(g_att) * a * (1.0 - a) * scale
    g_key = (g_logit * qe[...]).astype(BF16)
    q_high, q_low = two_parts(g_logit * key[...])
    back[:, 0:C] = (gm0[...] * scaled[0] + mm_nt(g_key, wk_ref[...])).astype(BF16)
    spread = mm(src_t[...], back[:, 0:C])
    pad_rows = jnp.zeros((PAD - NODE_DEV, C), F32)
    for d in range(N_GRAPH):
        p0[d] = jnp.concatenate([spread[d * NODE_DEV : (d + 1) * NODE_DEV], pad_rows], axis=0).astype(BF16)

    def p0_copy(d):
        to = lax.rem(graph + d, N_GRAPH)
        return remote(p0.at[to], in0.at[d], r0_send.at[d], r0_recv.at[d], (dp, to))

    @pl.loop(1, N_GRAPH)
    def _(d):
        p0_copy(d).start()

    reduce_start(CHUNKS - 1)

    q_node = mm(dst_t[...], q_high) + mm(dst_t[...], q_low)
    q_node = q_node.astype(BF16)
    wpart[0:C] = mm_tn(x_ref[:, 0:C], q_node[0:NODE_DEV]).astype(BF16)
    wpart[C : 2 * C] = mm_tn(ex0[...], g_key).astype(BF16)
    rad_t = rad_ref[...].T
    for degree in range(LEVELS):
        g_pre = (fold[degree] * a * slope[degree]).astype(BF16)
        wpart[(2 + degree) * C : (3 + degree) * C] = mm(rad_t, g_pre).astype(BF16)
    for degree in range(LEVELS):
        begin, end = degree * degree, (degree + 1) * (degree + 1)
        sums = fwd[begin:end].reshape((end - begin) * NODE_DEV, C).astype(BF16)
        stacked = jnp.concatenate([cot_ref[:, k * C : (k + 1) * C].astype(F32) for k in range(begin, end)], axis=0)
        wpart[(9 + degree) * C : (10 + degree) * C] = mm_tn(sums, stacked.astype(BF16)).astype(BF16)

    def w1_copy(d):
        to = lax.rem(graph + d, N_GRAPH)
        piece = wpart.at[pl.ds(pl.multiple_of(to * GRAD_PIECE, GRAD_PIECE), GRAD_PIECE)]
        return remote(piece, win1.at[d], w1_send.at[d], w1_recv.at[d], (dp, to))

    @pl.loop(1, N_GRAPH)
    def _(d):
        w1_copy(d).start()

    for j in range(CHUNKS - 3, CHUNKS):
        reduce_next(j)

    for degree in range(LEVELS):
        begin, end = degree * degree, (degree + 1) * (degree + 1)
        sums = fwd[begin:end].reshape((end - begin) * NODE_DEV, C).astype(BF16)
        mixed = mm(sums, wd_ref[degree])
        for k in range(begin, end):
            rows = mixed[(k - begin) * NODE_DEV : (k - begin + 1) * NODE_DEV]
            upd_ref[:, k * C : (k + 1) * C] = (x_ref[:, k * C : (k + 1) * C].astype(F32) + rows).astype(BF16)

    @pl.loop(1, N_GRAPH)
    def _(d):
        w1_copy(d).wait_recv()

    total = wpart[pl.ds(pl.multiple_of(graph * GRAD_PIECE, GRAD_PIECE), GRAD_PIECE), :].astype(F32)
    for d in range(1, N_GRAPH):
        total = total + win1[d].astype(F32)
    win2[dp] = total.astype(BF16)

    def w2_copy(d):
        return remote(
            win2.at[dp], win2.at[dp], w2_send.at[d], w2_recv.at[d], (lax.rem(dp + d, N_DP), graph)
        )

    @pl.loop(1, N_DP)
    def _(d):
        w2_copy(d).start()

    @pl.loop(1, N_GRAPH)
    def _(d):
        p0_copy(d).wait_recv()

    total = p0[graph, 0:NODE_DEV, :].astype(F32)
    for d in range(1, N_GRAPH):
        total = total + in0[d, 0:NODE_DEV, :].astype(F32)
    total = total + cot_ref[:, 0:C].astype(F32) + mm_nt(q_node, wq_ref[...])[0:NODE_DEV]
    gn_ref[:, 0:C] = total.astype(BF16)

    @pl.loop(1, N_DP)
    def _(d):
        w2_copy(d).wait_recv()

    total = win2[0].astype(F32)
    for d in range(1, N_DP):
        total = total + win2[d].astype(F32)
    my_piece = pl.ds(pl.multiple_of(graph * GRAD_PIECE, GRAD_PIECE), GRAD_PIECE)
    wall[my_piece, :] = total.astype(BF16)

    def w3_copy(d):
        return remote(
            wall.at[my_piece], wall.at[my_piece], w3_send.at[d], w3_recv.at[d],
            (dp, lax.rem(graph + d, N_GRAPH)),
        )

    @pl.loop(1, N_GRAPH)
    def _(d):
        w3_copy(d).start()

    for j in range(CHUNKS - 5, CHUNKS):
        reduce_end(j)

    for j in range(CHUNKS):
        last_copy(j).wait_recv()
    for t in range(HALF_PAIRS):
        own = last[t, pl.ds(pl.multiple_of(core * NODE_DEV, 8), NODE_DEV), :]
        sib = last_in[t]
        for half in range(2):
            k = 1 + 2 * (half * HALF_PAIRS + t)
            spread = jnp.where(core == half, own, sib)
            cols = slice(k * C, (k + 2) * C)
            gn_ref[:, cols] = (cot_ref[:, cols].astype(F32) + spread).astype(BF16)

    @pl.loop(1, N_GRAPH)
    def _(d):
        w3_copy(d).wait_recv()

    gw_ref[...] = wall[...].astype(F32)

    sib_copy.wait_send()

    @pl.loop(1, N_GRAPH)
    def _(d):
        x0_copy(d).wait_send()
        p0_copy(d).wait_send()
        w1_copy(d).wait_send()
        w3_copy(d).wait_send()

    @pl.loop(1, N_DP)
    def _(d):
        w2_copy(d).wait_send()

    @pl.loop(0, CHUNKS)
    def _(j):
        for copy in gather_first(j) + gather_second(j) + reduce_first(j) + reduce_second(j):
            copy().wait_send()
        to_sibling(j).wait_send()
        sum_sibling(j).wait_send()
        last_copy(j).wait_send()


def on_device(node_feat, radial, src_node, dst_node, w_query, w_key, w_radial, w_degree, cotangent):
    vmem = pl.BlockSpec(memory_space=pltpu.VMEM)
    dma = pltpu.SemaphoreType.DMA
    width = node_feat.shape[2]
    scratch = [
        pltpu.VMEM((2, HALF_PAIRS, PAD, 2 * C), BF16),
        pltpu.VMEM((HALF_PAIRS, PAD, 2 * C), BF16),
        pltpu.VMEM((2, HALF_PAIRS, NODES, 2 * C), BF16),
        pltpu.VMEM((N_GRAPH, PAD, C), BF16),
        pltpu.VMEM((NODES, C), BF16),
        pltpu.VMEM((EDGE_DEV, NODES), BF16),
        pltpu.VMEM((NODES, EDGE_DEV), BF16),
        pltpu.VMEM((EDGE_DEV, PAD), BF16),
        pltpu.VMEM((PAD, EDGE_DEV), BF16),
        pltpu.VMEM((2 * HALF_PAIRS, PAD, 2 * C), BF16),
        pltpu.VMEM((PAD, C), BF16),
        pltpu.VMEM((LEVELS, EDGE_DEV, C), F32),
        pltpu.VMEM((LEVELS, EDGE_DEV, C), F32),
        pltpu.VMEM((LEVELS, EDGE_DEV, C), F32),
        pltpu.VMEM((LEVELS, EDGE_DEV, C), F32),
        pltpu.VMEM((LEVELS * LEVELS, NODE_DEV, C), F32),
        pltpu.VMEM((EDGE_DEV, 2 * C), BF16),
        pltpu.VMEM((EDGE_DEV, 2 * C), BF16),
        pltpu.VMEM((2, HALF_PAIRS, NODES, 2 * C), BF16),
        pltpu.VMEM((HALF_PAIRS, NODES, 2 * C), BF16),
        pltpu.VMEM((3, HALF_PAIRS, CHIP_ROWS, 2 * C), BF16),
        pltpu.VMEM((4, HALF_PAIRS, CHIP_ROWS, 2 * C), BF16),
        pltpu.VMEM((HALF_PAIRS, CHIP_ROWS, 2 * C), F32),
        pltpu.VMEM((HALF_PAIRS, NODE_DEV, 2 * C), F32),
        pltpu.VMEM((N_GRAPH, PAD, C), BF16),
        pltpu.VMEM((N_GRAPH, PAD, C), BF16),
        pltpu.VMEM((GRAD_ROWS, C), BF16),
        pltpu.VMEM((N_GRAPH, GRAD_PIECE, C), BF16),
        pltpu.VMEM((N_DP, GRAD_PIECE, C), BF16),
        pltpu.VMEM((GRAD_ROWS, C), BF16),
        pltpu.VMEM((EDGE_DEV, C), F32),
        pltpu.VMEM((EDGE_DEV, C), F32),
        pltpu.VMEM((EDGE_DEV, C), F32),
        pltpu.VMEM((EDGE_DEV, C), BF16),
        pltpu.VMEM((EDGE_DEV, C), F32),
        dma((2,)),
        dma((N_GRAPH,)),
        dma((N_GRAPH,)),
        dma((CHUNKS, 8)),
        dma((CHUNKS, 8)),
        dma((CHUNKS, 9)),
        dma((CHUNKS, 9)),
        dma((N_GRAPH,)),
        dma((N_GRAPH,)),
        dma((N_GRAPH,)),
        dma((N_GRAPH,)),
        dma((N_DP,)),
        dma((N_DP,)),
        dma((N_GRAPH,)),
        dma((N_GRAPH,)),
    ]
    updated, grad_node, grads = pl.pallas_call(
        kernel,
        out_shape=(
            jax.ShapeDtypeStruct((NODE_DEV, width), BF16),
            jax.ShapeDtypeStruct((NODE_DEV, width), BF16),
            jax.ShapeDtypeStruct((GRAD_ROWS, C), F32),
        ),
        in_specs=[vmem] * 9,
        out_specs=(vmem, vmem, vmem),
        scratch_shapes=scratch,
        compiler_params=pltpu.CompilerParams(
            collective_id=0, has_side_effects=True, vmem_limit_bytes=60 << 20
        ),
    )(node_feat[0], radial[0], src_node, dst_node, w_query, w_key, w_radial, w_degree, cotangent[0])
    grad_query = grads[0:C]
    grad_key = grads[C : 2 * C]
    grad_radial = jnp.concatenate([grads[(2 + d) * C : (3 + d) * C] for d in range(LEVELS)], axis=1)
    grad_degree = grads[9 * C :].reshape(LEVELS, C, C)
    return (updated[None], grad_node[None], grad_query, grad_key, grad_radial, grad_degree)


def solution(mesh):
    return jax.shard_map(
        on_device,
        mesh=mesh,
        in_specs=(
            P("dp", "graph", None),
            P("dp", "graph", None),
            P("dp", "graph"),
            P("dp", "graph"),
            P(),
            P(),
            P(),
            P(),
            P("dp", "graph", None),
        ),
        out_specs=(P("dp", "graph", None), P("dp", "graph", None), P(), P(), P(), P()),
        check_vma=False,
    )
```

```python
import functools
import math

import jax
import jax.numpy as jnp
from jax import lax
from jax.experimental import pallas as pl
from jax.experimental.pallas import tpu as pltpu
from jax.sharding import PartitionSpec as P

HEADS = 8
C = 128
LEVELS = 7
NODE_DEV = 24
PAD = 32
EDGE_DEV = 768
NODES = 384
CHIP_ROWS = 48
N_GRAPH = 16
N_DP = 8
HALF_PAIRS = 12
CHUNK = 2
CHUNKS = HALF_PAIRS // CHUNK
ROW_BLOCK = 256
AHEAD = 2
EARLY = 6
EARLY_PIECE = 2 * EARLY * C // N_DP
EARLY_PAD = 256
EARLY_SUB = EARLY_PAD // N_GRAPH
LATE_ROWS = 4 * C
LATE_PIECE = LATE_ROWS // N_GRAPH
MESH = pl.DeviceIdType.MESH
F32 = jnp.float32
BF16 = jnp.bfloat16

X_OWN, UP_OWN, DOWN_OWN, FAR_OWN, UP_RELAY, DOWN_RELAY, X_RELAY, TO_SIB = range(8)
SUM_SIB, PART_UP, PART_DOWN, PART_X, OWN_UP, OWN_DOWN, TOTAL_X, TOTAL_FAR, LAST_SIB = range(9)


def mm(a, b):
    return jnp.dot(a, b, preferred_element_type=F32)


def mm_nt(a, b):
    return lax.dot_general(a, b, (((1,), (1,)), ((), ())), preferred_element_type=F32)


def mm_tn(a, b):
    return lax.dot_general(a, b, (((0,), (0,)), ((), ())), preferred_element_type=F32)


def two_parts(a):
    high = a.astype(BF16)
    return high, (a - high.astype(F32)).astype(BF16)


def degree_of(k):
    total = 0
    for degree in range(1, LEVELS):
        total = total + (k + 64 - degree * degree) // 64
    return total


def columns(k, count=1):
    return pl.ds(pl.multiple_of(k * C, C), count * C)


def kernel(
    x_ref, rad_ref, src_ref, dst_ref, wq_ref, wk_ref, wr_ref, wd_ref, cot_ref,
    upd_ref, gn_ref, gq_ref, gk_ref, gr_ref, gd_ref,
    xs, sibx, xall, x0all, x0, src_hot, src_t, dst_hot, dst_t,
    gs, g0, gate, slope, scaled, fold, fwd, msg, back,
    part, from_sib, in_part, in_total, last, last_in, p0, in0,
    wpart, win1, win2, wall, epart, ein1, esum, ein2, efull, eall,
    qe, key, att, ex0, gm0,
    sib_sems, x0_send, x0_recv, ag_send, ag_recv, rs_send, rs_recv,
    r0_send, r0_recv, w1_send, w1_recv, w2_send, w2_recv, w3_send, w3_recv,
    e1_send, e1_recv, e2_send, e2_recv, e3_send, e3_recv, e4_send, e4_recv,
):
    dp = lax.axis_index("dp")
    graph = lax.axis_index("graph")
    core = lax.rem(graph, 2)
    chip = graph // 2
    x_hi = chip // 4
    y = lax.rem(chip, 4)
    other = 1 - core

    def chip_at(dx, dy):
        return lax.rem(x_hi + dx, 2) * 4 + lax.rem(y + dy, 4)

    def at(dx, dy):
        return (dp, chip_at(dx, dy) * 2 + core)

    sibling = (dp, chip * 2 + other)

    def rows_of(which):
        return pl.ds(pl.multiple_of(which * CHIP_ROWS, 16), CHIP_ROWS)

    def remote(src, dst, send, recv, device):
        return pltpu.make_async_remote_copy(
            src_ref=src, dst_ref=dst, send_sem=send, recv_sem=recv,
            device_id=device, device_id_type=MESH,
        )

    barrier = pltpu.get_barrier_semaphore()

    @pl.loop(1, N_GRAPH)
    def _(d):
        pl.semaphore_signal(
            barrier, inc=1, device_id=(dp, lax.rem(graph + d, N_GRAPH)), device_id_type=MESH
        )

    @pl.loop(1, N_DP)
    def _(d):
        pl.semaphore_signal(
            barrier, inc=1, device_id=(lax.rem(dp + d, N_DP), graph), device_id_type=MESH
        )

    for pair in range(2 * HALF_PAIRS):
        xs[pair % 2, pair // 2, 0:NODE_DEV, :] = x_ref[:, (1 + 2 * pair) * C : (3 + 2 * pair) * C]
        xs[pair % 2, pair // 2, NODE_DEV:PAD, :] = jnp.zeros((PAD - NODE_DEV, 2 * C), BF16)
    x0all[graph, 0:NODE_DEV, :] = x_ref[:, 0:C]
    x0all[graph, NODE_DEV:PAD, :] = jnp.zeros((PAD - NODE_DEV, C), BF16)

    src_row = src_ref[...].astype(F32)
    dst_row = (dst_ref[...] - graph * NODE_DEV).astype(F32)
    src_t[...] = (lax.broadcasted_iota(jnp.int32, (NODES, EDGE_DEV), 0).astype(F32) == src_row).astype(F32).astype(BF16)
    dst_t[...] = (lax.broadcasted_iota(jnp.int32, (PAD, EDGE_DEV), 0).astype(F32) == dst_row).astype(F32).astype(BF16)
    src_col = jnp.broadcast_to(src_row, (8, EDGE_DEV)).T[:, 0:1]
    dst_col = jnp.broadcast_to(dst_row, (8, EDGE_DEV)).T[:, 0:1]
    src_hot[...] = (lax.broadcasted_iota(jnp.int32, (EDGE_DEV, NODES), 1).astype(F32) == src_col).astype(F32).astype(BF16)
    dst_hot[...] = (lax.broadcasted_iota(jnp.int32, (EDGE_DEV, PAD), 1).astype(F32) == dst_col).astype(F32).astype(BF16)

    for degree in range(LEVELS):
        pre = mm(rad_ref[...], wr_ref[:, degree * C : (degree + 1) * C])
        sigma = jax.nn.sigmoid(pre)
        gate[degree] = pre * sigma
        slope[degree] = sigma * (1.0 + pre * (1.0 - sigma))
        fold[degree] = jnp.zeros((EDGE_DEV, C), F32)

    pl.semaphore_wait(barrier, N_GRAPH - 1 + N_DP - 1)

    sib_copy = remote(xs.at[other], sibx, sib_sems.at[0], sib_sems.at[1], sibling)
    sib_copy.start()

    def x0_copy(d):
        return remote(
            x0all.at[graph], x0all.at[graph], x0_send.at[d], x0_recv.at[d],
            (dp, lax.rem(graph + d, N_GRAPH)),
        )

    @pl.loop(1, N_GRAPH)
    def _(d):
        x0_copy(d).start()

    sib_copy.wait_recv()
    mine = xs[core, :, 0:NODE_DEV, :].astype(F32)
    theirs = sibx[:, 0:NODE_DEV, :].astype(F32)
    first = jnp.where(core == 0, mine, theirs)
    second = jnp.where(core == 0, theirs, mine)
    xall[core, :, rows_of(chip), :] = jnp.concatenate([first, second], axis=1).astype(BF16)

    def block(j, which):
        return xall.at[core, pl.ds(j * CHUNK, CHUNK), rows_of(which), :]

    def gather_copy(j, kind, which, device):
        return lambda: remote(
            block(j, which), block(j, which), ag_send.at[j, kind], ag_recv.at[j, kind], device
        )

    def gather_first(j):
        return [
            gather_copy(j, X_OWN, chip, at(1, 0)),
            gather_copy(j, UP_OWN, chip, at(0, 1)),
            gather_copy(j, DOWN_OWN, chip, at(0, 3)),
            gather_copy(j, FAR_OWN, chip, at(0, 2)),
        ]

    def gather_second(j):
        return [
            gather_copy(j, UP_RELAY, chip_at(1, 0), at(0, 1)),
            gather_copy(j, DOWN_RELAY, chip_at(1, 0), at(0, 3)),
            gather_copy(j, X_RELAY, chip_at(0, 2), at(1, 0)),
        ]

    def to_sibling(j):
        ref = xall.at[core, pl.ds(j * CHUNK, CHUNK)]
        return remote(ref, ref, ag_send.at[j, TO_SIB], ag_recv.at[j, TO_SIB], sibling)

    def got_block(j, kind, which):
        gather_copy(j, kind, which, at(0, 1))().wait_recv()

    @pl.loop(0, AHEAD)
    def _(j):
        for copy in gather_first(j):
            copy().start()

    def relay(j):
        got_block(j, X_OWN, chip_at(1, 0))
        got_block(j, FAR_OWN, chip_at(0, 2))
        for copy in gather_second(j):
            copy().start()

        @pl.when(j + AHEAD < CHUNKS)
        def _():
            for copy in gather_first(j + AHEAD):
                copy().start()

    def forward(j):
        got_block(j, UP_OWN, chip_at(0, 3))
        got_block(j, DOWN_OWN, chip_at(0, 1))
        got_block(j, UP_RELAY, chip_at(1, 3))
        got_block(j, DOWN_RELAY, chip_at(1, 1))
        got_block(j, X_RELAY, chip_at(1, 2))
        to_sibling(j).start()

    def from_sibling(j):
        ref = xall.at[other, pl.ds(j * CHUNK, CHUNK)]
        remote(ref, ref, ag_send.at[j, TO_SIB], ag_recv.at[j, TO_SIB], sibling).wait_recv()

    zeros = jnp.zeros((PAD - NODE_DEV, C), F32)
    for degree in range(LEVELS):
        begin, end = degree * degree, (degree + 1) * (degree + 1)
        stacked = jnp.concatenate([cot_ref[:, k * C : (k + 1) * C].astype(F32) for k in range(begin, end)], axis=0)
        mixed = mm_nt(stacked.astype(BF16), wd_ref[degree])
        for k in range(begin, end):
            rows = mixed[(k - begin) * NODE_DEV : (k - begin + 1) * NODE_DEV]
            rows = jnp.concatenate([rows, zeros], axis=0).astype(BF16)
            if k == 0:
                g0[...] = rows
            else:
                lane = (k - 1) % 2
                gs[(k - 1) // 2, :, lane * C : (lane + 1) * C] = rows

    query = jnp.concatenate([mm(x_ref[:, 0:C], wq_ref[...]), zeros], axis=0)
    q_high, q_low = two_parts(query)
    qe[...] = mm(dst_hot[...], q_high) + mm(dst_hot[...], q_low)
    gm0[...] = mm(dst_hot[...], g0[...])

    head_rows = lax.broadcasted_iota(jnp.int32, (C, C), 0) // (C // HEADS)
    head_cols = lax.broadcasted_iota(jnp.int32, (C, C), 1) // (C // HEADS)
    same_head = (head_rows == head_cols).astype(F32).astype(BF16)
    scale = 1.0 / math.sqrt(C // HEADS)

    def head_sum(a):
        high, low = two_parts(a)
        return mm(high, same_head) + mm(low, same_head)

    @pl.loop(1, N_GRAPH)
    def _(d):
        x0_copy(d).wait_recv()

    x0[...] = jnp.concatenate([x0all[d, 0:NODE_DEV, :].astype(F32) for d in range(N_GRAPH)], axis=0).astype(BF16)
    relay(0)
    ex0[...] = mm(src_hot[...], x0[...]).astype(BF16)
    key[...] = mm(ex0[...], wk_ref[...])
    att[...] = jax.nn.sigmoid(head_sum(qe[...] * key[...]) * scale)
    for degree in range(LEVELS):
        scaled[degree] = gate[degree] * att[...]
    ex0_float = ex0[...].astype(F32)
    fold[0] = ex0_float * gm0[...]
    relay(1)
    forward(0)
    fwd[0] = mm(dst_t[...], (ex0_float * scaled[0]).astype(BF16))[0:NODE_DEV]

    def edges(half, t):
        pair = 2 * t + half
        k = 1 + 2 * pair
        left, right = degree_of(k), degree_of(k + 1)
        nodes = xall[half, t]
        ups = gs[pair]
        for begin in range(0, EDGE_DEV, ROW_BLOCK):
            rows = slice(begin, begin + ROW_BLOCK)
            ex = mm(src_hot[rows, :], nodes)
            gm = mm(dst_hot[rows, :], ups)
            for lane, degree in ((0, left), (1, right)):
                cols = slice(lane * C, (lane + 1) * C)
                factor = scaled[degree, rows, :]
                msg[rows, cols] = (ex[:, cols] * factor).astype(BF16)
                back[rows, cols] = (gm[:, cols] * factor).astype(BF16)
                fold[degree, rows, :] += ex[:, cols] * gm[:, cols]
        gathered = mm(dst_t[...], msg[...])
        fwd[k] = gathered[0:NODE_DEV, 0:C]
        fwd[k + 1] = gathered[0:NODE_DEV, C : 2 * C]
        part[half, t] = mm(src_t[...], back[...]).astype(BF16)

    def sum_sibling(j):
        return remote(
            part.at[other, pl.ds(j * CHUNK, CHUNK)], from_sib.at[pl.ds(j * CHUNK, CHUNK)],
            rs_send.at[j, SUM_SIB], rs_recv.at[j, SUM_SIB], sibling,
        )

    def part_block(j, which):
        return part.at[core, pl.ds(j * CHUNK, CHUNK), rows_of(which), :]

    def reduce_copy(j, kind, which, landing, slot, device):
        return lambda: remote(
            part_block(j, which), landing.at[slot, pl.ds(j * CHUNK, CHUNK)],
            rs_send.at[j, kind], rs_recv.at[j, kind], device,
        )

    def reduce_first(j):
        return [
            reduce_copy(j, PART_UP, chip_at(1, 1), in_part, 0, at(0, 1)),
            reduce_copy(j, PART_DOWN, chip_at(1, 3), in_part, 1, at(0, 3)),
            reduce_copy(j, PART_X, chip_at(1, 2), in_part, 2, at(1, 0)),
            reduce_copy(j, OWN_UP, chip_at(0, 1), in_total, 0, at(0, 1)),
            reduce_copy(j, OWN_DOWN, chip_at(0, 3), in_total, 1, at(0, 3)),
        ]

    def reduce_second(j):
        return [
            reduce_copy(j, TOTAL_X, chip_at(1, 0), in_total, 2, at(1, 0)),
            reduce_copy(j, TOTAL_FAR, chip_at(0, 2), in_total, 3, at(0, 2)),
        ]

    def last_copy(j):
        return remote(
            last.at[pl.ds(j * CHUNK, CHUNK), pl.ds(pl.multiple_of(other * NODE_DEV, 8), NODE_DEV), :],
            last_in.at[pl.ds(j * CHUNK, CHUNK)],
            rs_send.at[j, LAST_SIB], rs_recv.at[j, LAST_SIB], sibling,
        )

    def reduce_start(j):
        sum_sibling(j).wait_recv()
        for i in range(CHUNK):
            t = j * CHUNK + i
            part[core, t] = (part[core, t].astype(F32) + from_sib[t].astype(F32)).astype(BF16)
        for copy in reduce_first(j):
            copy().start()

    def reduce_next(j):
        for copy in reduce_first(j)[:3]:
            copy().wait_recv()
        for i in range(CHUNK):
            t = j * CHUNK + i
            rows = rows_of(chip_at(1, 0))
            total = part[core, t, rows, :].astype(F32) + in_part[0, t].astype(F32) + in_part[1, t].astype(F32)
            part[core, t, rows, :] = total.astype(BF16)
            rows = rows_of(chip_at(0, 2))
            total = part[core, t, rows, :].astype(F32) + in_part[2, t].astype(F32)
            part[core, t, rows, :] = total.astype(BF16)
        for copy in reduce_second(j):
            copy().start()

    def reduce_end(j):
        for copy in reduce_first(j)[3:] + reduce_second(j):
            copy().wait_recv()
        for i in range(CHUNK):
            t = j * CHUNK + i
            total = part[core, t, rows_of(chip), :].astype(F32)
            for slot in range(4):
                total = total + in_total[slot, t].astype(F32)
            last[t] = total
        last_copy(j).start()

    def degree_grad(degree):
        begin, end = degree * degree, (degree + 1) * (degree + 1)
        sums = fwd[begin:end].reshape((end - begin) * NODE_DEV, C).astype(BF16)
        stacked = jnp.concatenate([cot_ref[:, k * C : (k + 1) * C].astype(F32) for k in range(begin, end)], axis=0)
        return mm_tn(sums, stacked.astype(BF16)).astype(BF16)

    def radial_grad(degree):
        g_pre = (fold[degree] * att[...] * slope[degree]).astype(BF16)
        return mm_tn(rad_ref[...], g_pre).astype(BF16)

    def dp_peer(d):
        return lax.rem(dp + d, N_DP)

    def graph_peer(d):
        return lax.rem(graph + d, N_GRAPH)

    def early_rows(which):
        return pl.ds(pl.multiple_of(which * EARLY_PIECE, 16), EARLY_PIECE)

    def e1_copy(d):
        to = dp_peer(d)
        return remote(epart.at[early_rows(to)], ein1.at[d], e1_send.at[d], e1_recv.at[d], (to, graph))

    def sub_rows(which):
        return pl.ds(pl.multiple_of(which * EARLY_SUB, EARLY_SUB), EARLY_SUB)

    def e2_copy(d):
        to = graph_peer(d)
        return remote(esum.at[sub_rows(to)], ein2.at[d], e2_send.at[d], e2_recv.at[d], (dp, to))

    def e3_copy(d):
        mine = efull.at[sub_rows(graph)]
        return remote(mine, mine, e3_send.at[d], e3_recv.at[d], (dp, graph_peer(d)))

    def e4_copy(d):
        mine = eall.at[early_rows(dp)]
        return remote(mine, mine, e4_send.at[d], e4_recv.at[d], (dp_peer(d), graph))

    def early_start():
        for degree in range(EARLY):
            epart[degree * C : (degree + 1) * C] = radial_grad(degree)
            epart[(EARLY + degree) * C : (EARLY + degree + 1) * C] = degree_grad(degree)

        @pl.loop(1, N_DP)
        def _(d):
            e1_copy(d).start()

    def early_second():
        @pl.loop(1, N_DP)
        def _(d):
            e1_copy(d).wait_recv()

        total = epart[early_rows(dp), :].astype(F32)
        for d in range(1, N_DP):
            total = total + ein1[d].astype(F32)
        esum[0:EARLY_PIECE] = total.astype(BF16)
        esum[EARLY_PIECE:EARLY_PAD] = jnp.zeros((EARLY_PAD - EARLY_PIECE, C), BF16)

        @pl.loop(1, N_GRAPH)
        def _(d):
            e2_copy(d).start()

    def early_third():
        @pl.loop(1, N_GRAPH)
        def _(d):
            e2_copy(d).wait_recv()

        total = esum[sub_rows(graph), :].astype(F32)
        for d in range(1, N_GRAPH):
            total = total + ein2[d].astype(F32)

        efull[sub_rows(graph), :] = total.astype(BF16)

        @pl.loop(1, N_GRAPH)
        def _(d):
            e3_copy(d).start()

    def early_fourth():
        @pl.loop(1, N_GRAPH)
        def _(d):
            e3_copy(d).wait_recv()

        eall[early_rows(dp), :] = efull[0:EARLY_PIECE]

        @pl.loop(1, N_DP)
        def _(d):
            e4_copy(d).start()

    @pl.loop(0, CHUNKS)
    def _(s):
        @pl.when(s + 2 < CHUNKS)
        def _():
            relay(s + 2)

        @pl.when(s + 1 < CHUNKS)
        def _():
            forward(s + 1)

        @pl.when(s == CHUNKS - 1)
        def _():
            early_start()

        from_sibling(s)

        @pl.loop(0, 2 * CHUNK)
        def _(i):
            half = lax.rem(other + i // CHUNK, 2)
            edges(half, s * CHUNK + lax.rem(i, CHUNK))

            @pl.when(i == CHUNK - 1)
            def _():
                sum_sibling(s).start()

        @pl.when(s >= 1)
        def _():
            reduce_start(s - 1)

        @pl.when(s >= 3)
        def _():
            reduce_next(s - 3)

        @pl.when(s >= 5)
        def _():
            reduce_end(s - 5)

    a = att[...]
    g_att = gate[0] * fold[0]
    for degree in range(1, LEVELS):
        g_att = g_att + gate[degree] * fold[degree]
    g_logit = head_sum(g_att) * a * (1.0 - a) * scale
    g_key = (g_logit * qe[...]).astype(BF16)
    q_high, q_low = two_parts(g_logit * key[...])
    back[:, 0:C] = (gm0[...] * scaled[0] + mm_nt(g_key, wk_ref[...])).astype(BF16)
    spread = mm(src_t[...], back[:, 0:C])
    pad_rows = jnp.zeros((PAD - NODE_DEV, C), F32)
    for d in range(N_GRAPH):
        p0[d] = jnp.concatenate([spread[d * NODE_DEV : (d + 1) * NODE_DEV], pad_rows], axis=0).astype(BF16)

    def p0_copy(d):
        to = lax.rem(graph + d, N_GRAPH)
        return remote(p0.at[to], in0.at[d], r0_send.at[d], r0_recv.at[d], (dp, to))

    @pl.loop(1, N_GRAPH)
    def _(d):
        p0_copy(d).start()

    q_node = (mm(dst_t[...], q_high) + mm(dst_t[...], q_low)).astype(BF16)
    wpart[0:C] = mm_tn(x_ref[:, 0:C], q_node[0:NODE_DEV]).astype(BF16)
    wpart[C : 2 * C] = mm_tn(ex0[...], g_key).astype(BF16)
    wpart[2 * C : 3 * C] = radial_grad(EARLY)
    wpart[3 * C : 4 * C] = degree_grad(EARLY)

    def late_rows(which):
        return pl.ds(pl.multiple_of(which * LATE_PIECE, LATE_PIECE), LATE_PIECE)

    def w1_copy(d):
        to = graph_peer(d)
        return remote(wpart.at[late_rows(to)], win1.at[d], w1_send.at[d], w1_recv.at[d], (dp, to))

    @pl.loop(1, N_GRAPH)
    def _(d):
        w1_copy(d).start()

    reduce_start(CHUNKS - 1)
    early_second()
    for j in range(CHUNKS - 3, CHUNKS - 1):
        reduce_next(j)

    for degree in range(LEVELS):
        begin, end = degree * degree, (degree + 1) * (degree + 1)
        sums = fwd[begin:end].reshape((end - begin) * NODE_DEV, C).astype(BF16)
        mixed = mm(sums, wd_ref[degree])
        for k in range(begin, end):
            rows = mixed[(k - begin) * NODE_DEV : (k - begin + 1) * NODE_DEV]
            upd_ref[:, k * C : (k + 1) * C] = (x_ref[:, k * C : (k + 1) * C].astype(F32) + rows).astype(BF16)

    early_third()

    @pl.loop(1, N_GRAPH)
    def _(d):
        w1_copy(d).wait_recv()

    total = wpart[late_rows(graph), :].astype(F32)
    for d in range(1, N_GRAPH):
        total = total + win1[d].astype(F32)
    win2[dp] = total.astype(BF16)

    def w2_copy(d):
        return remote(win2.at[dp], win2.at[dp], w2_send.at[d], w2_recv.at[d], (dp_peer(d), graph))

    @pl.loop(1, N_DP)
    def _(d):
        w2_copy(d).start()

    reduce_next(CHUNKS - 1)
    early_fourth()

    @pl.loop(1, N_GRAPH)
    def _(d):
        p0_copy(d).wait_recv()

    total = p0[graph, 0:NODE_DEV, :].astype(F32)
    for d in range(1, N_GRAPH):
        total = total + in0[d, 0:NODE_DEV, :].astype(F32)
    total = total + cot_ref[:, 0:C].astype(F32) + mm_nt(q_node, wq_ref[...])[0:NODE_DEV]
    gn_ref[:, 0:C] = total.astype(BF16)

    @pl.loop(1, N_DP)
    def _(d):
        w2_copy(d).wait_recv()

    total = win2[0].astype(F32)
    for d in range(1, N_DP):
        total = total + win2[d].astype(F32)
    wall[late_rows(graph), :] = total.astype(BF16)

    def w3_copy(d):
        mine = wall.at[late_rows(graph)]
        return remote(mine, mine, w3_send.at[d], w3_recv.at[d], (dp, graph_peer(d)))

    @pl.loop(1, N_GRAPH)
    def _(d):
        w3_copy(d).start()

    for j in range(CHUNKS - 5, CHUNKS):
        reduce_end(j)

    for j in range(CHUNKS):
        last_copy(j).wait_recv()
    for t in range(HALF_PAIRS):
        own = last[t, pl.ds(pl.multiple_of(core * NODE_DEV, 8), NODE_DEV), :]
        sib = last_in[t]
        for half in range(2):
            k = 1 + 2 * (2 * t + half)
            spread = jnp.where(core == half, own, sib)
            cols = slice(k * C, (k + 2) * C)
            gn_ref[:, cols] = (cot_ref[:, cols].astype(F32) + spread).astype(BF16)

    @pl.loop(1, N_DP)
    def _(d):
        e4_copy(d).wait_recv()

    for degree in range(EARLY):
        gr_ref[:, degree * C : (degree + 1) * C] = eall[degree * C : (degree + 1) * C].astype(F32)
        gd_ref[degree] = eall[(EARLY + degree) * C : (EARLY + degree + 1) * C].astype(F32)

    @pl.loop(1, N_GRAPH)
    def _(d):
        w3_copy(d).wait_recv()

    gq_ref[...] = wall[0:C].astype(F32)
    gk_ref[...] = wall[C : 2 * C].astype(F32)
    gr_ref[:, EARLY * C :] = wall[2 * C : 3 * C].astype(F32)
    gd_ref[EARLY] = wall[3 * C : 4 * C].astype(F32)

    sib_copy.wait_send()

    @pl.loop(1, N_GRAPH)
    def _(d):
        x0_copy(d).wait_send()
        p0_copy(d).wait_send()
        w1_copy(d).wait_send()
        w3_copy(d).wait_send()
        e2_copy(d).wait_send()
        e3_copy(d).wait_send()

    @pl.loop(1, N_DP)
    def _(d):
        w2_copy(d).wait_send()
        e1_copy(d).wait_send()
        e4_copy(d).wait_send()

    @pl.loop(0, CHUNKS)
    def _(j):
        for copy in gather_first(j) + gather_second(j) + reduce_first(j) + reduce_second(j):
            copy().wait_send()
        to_sibling(j).wait_send()
        sum_sibling(j).wait_send()
        last_copy(j).wait_send()


def on_device(node_feat, radial, src_node, dst_node, w_query, w_key, w_radial, w_degree, cotangent):
    vmem = pl.BlockSpec(memory_space=pltpu.VMEM)
    dma = pltpu.SemaphoreType.DMA
    width = node_feat.shape[2]
    scratch = [
        pltpu.VMEM((2, HALF_PAIRS, PAD, 2 * C), BF16),
        pltpu.VMEM((HALF_PAIRS, PAD, 2 * C), BF16),
        pltpu.VMEM((2, HALF_PAIRS, NODES, 2 * C), BF16),
        pltpu.VMEM((N_GRAPH, PAD, C), BF16),
        pltpu.VMEM((NODES, C), BF16),
        pltpu.VMEM((EDGE_DEV, NODES), BF16),
        pltpu.VMEM((NODES, EDGE_DEV), BF16),
        pltpu.VMEM((EDGE_DEV, PAD), BF16),
        pltpu.VMEM((PAD, EDGE_DEV), BF16),
        pltpu.VMEM((2 * HALF_PAIRS, PAD, 2 * C), BF16),
        pltpu.VMEM((PAD, C), BF16),
        pltpu.VMEM((LEVELS, EDGE_DEV, C), F32),
        pltpu.VMEM((LEVELS, EDGE_DEV, C), F32),
        pltpu.VMEM((LEVELS, EDGE_DEV, C), F32),
        pltpu.VMEM((LEVELS, EDGE_DEV, C), F32),
        pltpu.VMEM((LEVELS * LEVELS, NODE_DEV, C), F32),
        pltpu.VMEM((EDGE_DEV, 2 * C), BF16),
        pltpu.VMEM((EDGE_DEV, 2 * C), BF16),
        pltpu.VMEM((2, HALF_PAIRS, NODES, 2 * C), BF16),
        pltpu.VMEM((HALF_PAIRS, NODES, 2 * C), BF16),
        pltpu.VMEM((3, HALF_PAIRS, CHIP_ROWS, 2 * C), BF16),
        pltpu.VMEM((4, HALF_PAIRS, CHIP_ROWS, 2 * C), BF16),
        pltpu.VMEM((HALF_PAIRS, CHIP_ROWS, 2 * C), F32),
        pltpu.VMEM((HALF_PAIRS, NODE_DEV, 2 * C), F32),
        pltpu.VMEM((N_GRAPH, PAD, C), BF16),
        pltpu.VMEM((N_GRAPH, PAD, C), BF16),
        pltpu.VMEM((LATE_ROWS, C), BF16),
        pltpu.VMEM((N_GRAPH, LATE_PIECE, C), BF16),
        pltpu.VMEM((N_DP, LATE_PIECE, C), BF16),
        pltpu.VMEM((LATE_ROWS, C), BF16),
        pltpu.VMEM((2 * EARLY * C, C), BF16),
        pltpu.VMEM((N_DP, EARLY_PIECE, C), BF16),
        pltpu.VMEM((EARLY_PAD, C), BF16),
        pltpu.VMEM((N_GRAPH, EARLY_SUB, C), BF16),
        pltpu.VMEM((EARLY_PAD, C), BF16),
        pltpu.VMEM((2 * EARLY * C, C), BF16),
        pltpu.VMEM((EDGE_DEV, C), F32),
        pltpu.VMEM((EDGE_DEV, C), F32),
        pltpu.VMEM((EDGE_DEV, C), F32),
        pltpu.VMEM((EDGE_DEV, C), BF16),
        pltpu.VMEM((EDGE_DEV, C), F32),
        dma((2,)),
        dma((N_GRAPH,)),
        dma((N_GRAPH,)),
        dma((CHUNKS, 8)),
        dma((CHUNKS, 8)),
        dma((CHUNKS, 9)),
        dma((CHUNKS, 9)),
        dma((N_GRAPH,)),
        dma((N_GRAPH,)),
        dma((N_GRAPH,)),
        dma((N_GRAPH,)),
        dma((N_DP,)),
        dma((N_DP,)),
        dma((N_GRAPH,)),
        dma((N_GRAPH,)),
        dma((N_DP,)),
        dma((N_DP,)),
        dma((N_GRAPH,)),
        dma((N_GRAPH,)),
        dma((N_GRAPH,)),
        dma((N_GRAPH,)),
        dma((N_DP,)),
        dma((N_DP,)),
    ]
    updated, grad_node, grad_query, grad_key, grad_radial, grad_degree = pl.pallas_call(
        kernel,
        out_shape=(
            jax.ShapeDtypeStruct((NODE_DEV, width), BF16),
            jax.ShapeDtypeStruct((NODE_DEV, width), BF16),
            jax.ShapeDtypeStruct((C, C), F32),
            jax.ShapeDtypeStruct((C, C), F32),
            jax.ShapeDtypeStruct((C, LEVELS * C), F32),
            jax.ShapeDtypeStruct((LEVELS, C, C), F32),
        ),
        in_specs=[vmem] * 9,
        out_specs=(vmem,) * 6,
        scratch_shapes=scratch,
        compiler_params=pltpu.CompilerParams(
            collective_id=0, has_side_effects=True, vmem_limit_bytes=60 << 20
        ),
    )(node_feat[0], radial[0], src_node, dst_node, w_query, w_key, w_radial, w_degree, cotangent[0])
    return (updated[None], grad_node[None], grad_query, grad_key, grad_radial, grad_degree)


def solution(mesh):
    return jax.shard_map(
        on_device,
        mesh=mesh,
        in_specs=(
            P("dp", "graph", None),
            P("dp", "graph", None),
            P("dp", "graph"),
            P("dp", "graph"),
            P(),
            P(),
            P(),
            P(),
            P("dp", "graph", None),
        ),
        out_specs=(P("dp", "graph", None), P("dp", "graph", None), P(), P(), P(), P()),
        check_vma=False,
    )
```

```python
import functools
import math

import jax
import jax.numpy as jnp
from jax import lax
from jax.experimental import pallas as pl
from jax.experimental.pallas import tpu as pltpu
from jax.sharding import PartitionSpec as P

HEADS = 8
C = 128
LEVELS = 7
NODE_DEV = 24
PAD = 32
EDGE_DEV = 768
NODES = 384
CHIP_ROWS = 48
N_GRAPH = 16
N_DP = 8
HALF_PAIRS = 12
CHUNK = 2
CHUNKS = HALF_PAIRS // CHUNK
ROW_BLOCK = 128
AHEAD = 2
NEXT_LAG = 2
END_LAG = 4
EARLY = 5
EARLY_HALF = EARLY * C
EARLY_PIECE = EARLY_HALF // N_DP
EARLY_PAD = 128
N_CHIP = N_GRAPH // 2
EARLY_SUB = EARLY_PAD // N_CHIP
LATE_DEGREES = LEVELS - EARLY
LATE_ROWS = (2 + 2 * LATE_DEGREES) * C
LATE_PIECE = LATE_ROWS // N_GRAPH
MESH = pl.DeviceIdType.MESH
F32 = jnp.float32
BF16 = jnp.bfloat16

FIRST, REST, SIB = range(3)
PARTS, TOTALS, LAST = range(1, 4)


def mm(a, b):
    return jnp.dot(a, b, preferred_element_type=F32)


def mm_nt(a, b):
    return lax.dot_general(a, b, (((1,), (1,)), ((), ())), preferred_element_type=F32)


def mm_tn(a, b):
    return lax.dot_general(a, b, (((0,), (0,)), ((), ())), preferred_element_type=F32)


def two_parts(a):
    high = a.astype(BF16)
    return high, (a - high.astype(F32)).astype(BF16)


def degree_of(k):
    total = 0
    for degree in range(1, LEVELS):
        total = total + (k + 64 - degree * degree) // 64
    return total


def columns(k, count=1):
    return pl.ds(pl.multiple_of(k * C, C), count * C)


def kernel(
    x_ref, rad_ref, src_ref, dst_ref, wq_ref, wk_ref, wr_ref, wd_ref, cot_ref,
    upd_ref, gn_ref, ge_ref, gl_ref,
    xs, sibx, xall, x0all, x0, src_hot, src_t, dst_hot, dst_t,
    gs, g0, gate, slope, scaled, fold, fwd, msg, back,
    part, from_sib, in_part, in_total, last, last_in, p0, in0,
    wpart, win1, win2, wall, epart, esib, e1_in, esum, e2_in, efull, eall,
    qe, key, att, ex0, gm0, rad_t,
    sib_sems, x0_send, x0_recv, ag_send, ag_recv, rs_send, rs_recv,
    r0_send, r0_recv, w1_send, w1_recv, w2_send, w2_recv, w3_send, w3_recv,
    e_send, e_recv,
):
    dp = lax.axis_index("dp")
    graph = lax.axis_index("graph")
    core = lax.rem(graph, 2)
    chip = graph // 2
    x_hi = chip // 4
    y = lax.rem(chip, 4)
    other = 1 - core

    def chip_at(dx, dy):
        return lax.rem(x_hi + dx, 2) * 4 + lax.rem(y + dy, 4)

    def at(dx, dy):
        return (dp, chip_at(dx, dy) * 2 + core)

    sibling = (dp, chip * 2 + other)

    def rows_of(which):
        return pl.ds(pl.multiple_of(which * CHIP_ROWS, 16), CHIP_ROWS)

    def remote(src, dst, send, recv, device):
        return pltpu.make_async_remote_copy(
            src_ref=src, dst_ref=dst, send_sem=send, recv_sem=recv,
            device_id=device, device_id_type=MESH,
        )

    barrier = pltpu.get_barrier_semaphore()

    @pl.loop(1, N_GRAPH)
    def _(d):
        pl.semaphore_signal(
            barrier, inc=1, device_id=(dp, lax.rem(graph + d, N_GRAPH)), device_id_type=MESH
        )

    @pl.loop(1, N_DP)
    def _(d):
        pl.semaphore_signal(
            barrier, inc=1, device_id=(lax.rem(dp + d, N_DP), graph), device_id_type=MESH
        )

    for pair in range(2 * HALF_PAIRS):
        xs[pair % 2, pair // 2, 0:NODE_DEV, :] = x_ref[:, (1 + 2 * pair) * C : (3 + 2 * pair) * C]
        xs[pair % 2, pair // 2, NODE_DEV:PAD, :] = jnp.zeros((PAD - NODE_DEV, 2 * C), BF16)
    x0all[graph, 0:NODE_DEV, :] = x_ref[:, 0:C]
    x0all[graph, NODE_DEV:PAD, :] = jnp.zeros((PAD - NODE_DEV, C), BF16)

    pl.semaphore_wait(barrier, N_GRAPH - 1 + N_DP - 1)

    sib_copy = remote(xs.at[other], sibx, sib_sems.at[0], sib_sems.at[1], sibling)
    sib_copy.start()

    def x0_copy(d):
        return remote(
            x0all.at[graph], x0all.at[graph], x0_send.at[0], x0_recv.at[0],
            (dp, lax.rem(graph + d, N_GRAPH)),
        )

    @pl.loop(1, N_GRAPH)
    def _(d):
        x0_copy(d).start()

    sib_copy.wait_recv()
    mine = xs[core, :, 0:NODE_DEV, :].astype(F32)
    theirs = sibx[:, 0:NODE_DEV, :].astype(F32)
    first = jnp.where(core == 0, mine, theirs)
    second = jnp.where(core == 0, theirs, mine)
    xall[core, :, rows_of(chip), :] = jnp.concatenate([first, second], axis=1).astype(BF16)

    def block(j, which):
        return xall.at[core, pl.ds(j * CHUNK, CHUNK), rows_of(which), :]

    def gather_copy(j, group, which, device):
        return lambda: remote(block(j, which), block(j, which), ag_send.at[0], ag_recv.at[j, group], device)

    def gather_first(j):
        return [
            gather_copy(j, FIRST, chip, at(1, 0)),
            gather_copy(j, REST, chip, at(0, 1)),
            gather_copy(j, REST, chip, at(0, 3)),
            gather_copy(j, FIRST, chip, at(0, 2)),
        ]

    def gather_second(j):
        return [
            gather_copy(j, REST, chip_at(1, 0), at(0, 1)),
            gather_copy(j, REST, chip_at(1, 0), at(0, 3)),
            gather_copy(j, REST, chip_at(0, 2), at(1, 0)),
        ]

    def to_sibling(j):
        ref = xall.at[core, pl.ds(j * CHUNK, CHUNK)]
        return remote(ref, ref, ag_send.at[1], ag_recv.at[j, SIB], sibling)

    def got_blocks(j, group, count):
        ref = xall.at[core, pl.ds(j * CHUNK, CHUNK), pl.ds(0, count * CHIP_ROWS), :]
        remote(ref, ref, ag_send.at[0], ag_recv.at[j, group], sibling).wait_recv()

    @pl.loop(0, AHEAD)
    def _(j):
        for copy in gather_first(j):
            copy().start()

    def relay(j):
        got_blocks(j, FIRST, 2)
        for copy in gather_second(j):
            copy().start()

        @pl.when(j + AHEAD < CHUNKS)
        def _():
            for copy in gather_first(j + AHEAD):
                copy().start()

    def forward(j):
        got_blocks(j, REST, 5)
        to_sibling(j).start()

    def from_sibling(j):
        ref = xall.at[other, pl.ds(j * CHUNK, CHUNK)]
        remote(ref, ref, ag_send.at[1], ag_recv.at[j, SIB], sibling).wait_recv()

    src_row = src_ref[...].astype(F32)
    dst_row = (dst_ref[...] - graph * NODE_DEV).astype(F32)
    src_t[...] = (lax.broadcasted_iota(jnp.int32, (NODES, EDGE_DEV), 0).astype(F32) == src_row).astype(F32).astype(BF16)
    dst_t[...] = (lax.broadcasted_iota(jnp.int32, (PAD, EDGE_DEV), 0).astype(F32) == dst_row).astype(F32).astype(BF16)
    src_col = jnp.broadcast_to(src_row, (8, EDGE_DEV)).T[:, 0:1]
    dst_col = jnp.broadcast_to(dst_row, (8, EDGE_DEV)).T[:, 0:1]
    src_hot[...] = (lax.broadcasted_iota(jnp.int32, (EDGE_DEV, NODES), 1).astype(F32) == src_col).astype(F32).astype(BF16)
    dst_hot[...] = (lax.broadcasted_iota(jnp.int32, (EDGE_DEV, PAD), 1).astype(F32) == dst_col).astype(F32).astype(BF16)

    rad_t[...] = rad_ref[...].T
    for degree in range(LEVELS):
        pre = mm(rad_ref[...], wr_ref[:, degree * C : (degree + 1) * C])
        sigma = jax.nn.sigmoid(pre)
        gate[degree] = pre * sigma
        slope[degree] = sigma * (1.0 + pre * (1.0 - sigma))
        fold[degree] = jnp.zeros((EDGE_DEV, C), F32)

    relay(0)
    zeros = jnp.zeros((PAD - NODE_DEV, C), F32)
    for degree in range(LEVELS):
        begin, end = degree * degree, (degree + 1) * (degree + 1)
        stacked = jnp.concatenate([cot_ref[:, k * C : (k + 1) * C].astype(F32) for k in range(begin, end)], axis=0)
        mixed = mm_nt(stacked.astype(BF16), wd_ref[degree])
        for k in range(begin, end):
            rows = mixed[(k - begin) * NODE_DEV : (k - begin + 1) * NODE_DEV]
            rows = jnp.concatenate([rows, zeros], axis=0).astype(BF16)
            if k == 0:
                g0[...] = rows
            else:
                lane = (k - 1) % 2
                gs[(k - 1) // 2, :, lane * C : (lane + 1) * C] = rows

    query = jnp.concatenate([mm(x_ref[:, 0:C], wq_ref[...]), zeros], axis=0)
    q_high, q_low = two_parts(query)
    qe[...] = mm(dst_hot[...], q_high) + mm(dst_hot[...], q_low)
    gm0[...] = mm(dst_hot[...], g0[...])

    head_rows = lax.broadcasted_iota(jnp.int32, (C, C), 0) // (C // HEADS)
    head_cols = lax.broadcasted_iota(jnp.int32, (C, C), 1) // (C // HEADS)
    same_head = (head_rows == head_cols).astype(F32).astype(BF16)
    scale = 1.0 / math.sqrt(C // HEADS)

    def head_sum(a):
        high, low = two_parts(a)
        return mm(high, same_head) + mm(low, same_head)

    remote(x0all.at[pl.ds(1, N_GRAPH - 1)], x0all.at[pl.ds(1, N_GRAPH - 1)], x0_send.at[0], x0_recv.at[0], sibling).wait_recv()

    x0[...] = jnp.concatenate([x0all[d, 0:NODE_DEV, :].astype(F32) for d in range(N_GRAPH)], axis=0).astype(BF16)
    relay(1)
    ex0[...] = mm(src_hot[...], x0[...]).astype(BF16)
    key[...] = mm(ex0[...], wk_ref[...])
    att[...] = jax.nn.sigmoid(head_sum(qe[...] * key[...]) * scale)
    for degree in range(LEVELS):
        scaled[degree] = gate[degree] * att[...]
    ex0_float = ex0[...].astype(F32)
    fold[0] = ex0_float * gm0[...]
    forward(0)
    fwd[0] = mm(dst_t[...], (ex0_float * scaled[0]).astype(BF16))[0:NODE_DEV]

    def edges(half, t):
        pair = 2 * t + half
        k = 1 + 2 * pair
        left, right = degree_of(k), degree_of(k + 1)
        nodes = xall[half, t]
        ups = gs[pair]
        for begin in range(0, EDGE_DEV, ROW_BLOCK):
            rows = slice(begin, begin + ROW_BLOCK)
            ex = mm(src_hot[rows, :], nodes)
            gm = mm(dst_hot[rows, :], ups)
            for lane, degree in ((0, left), (1, right)):
                cols = slice(lane * C, (lane + 1) * C)
                factor = scaled[degree, rows, :]
                msg[rows, cols] = (ex[:, cols] * factor).astype(BF16)
                back[rows, cols] = (gm[:, cols] * factor).astype(BF16)
                fold[degree, rows, :] += ex[:, cols] * gm[:, cols]
        gathered = mm(dst_t[...], msg[...])
        fwd[k] = gathered[0:NODE_DEV, 0:C]
        fwd[k + 1] = gathered[0:NODE_DEV, C : 2 * C]
        part[half, t] = mm(src_t[...], back[...]).astype(BF16)

    def sum_sibling(j):
        return remote(
            part.at[other, pl.ds(j * CHUNK, CHUNK)], from_sib.at[pl.ds(j * CHUNK, CHUNK)],
            rs_send.at[0], rs_recv.at[j, 0], sibling,
        )

    def part_block(j, which):
        return part.at[core, pl.ds(j * CHUNK, CHUNK), rows_of(which), :]

    def reduce_copy(j, group, which, landing, slot, device):
        return lambda: remote(
            part_block(j, which), landing.at[slot, pl.ds(j * CHUNK, CHUNK)],
            rs_send.at[1], rs_recv.at[j, group], device,
        )

    def reduce_first(j):
        return [
            reduce_copy(j, PARTS, chip_at(1, 1), in_part, 0, at(0, 1)),
            reduce_copy(j, PARTS, chip_at(1, 3), in_part, 1, at(0, 3)),
            reduce_copy(j, PARTS, chip_at(1, 2), in_part, 2, at(1, 0)),
            reduce_copy(j, TOTALS, chip_at(0, 1), in_total, 0, at(0, 1)),
            reduce_copy(j, TOTALS, chip_at(0, 3), in_total, 1, at(0, 3)),
        ]

    def reduce_second(j):
        return [
            reduce_copy(j, TOTALS, chip_at(1, 0), in_total, 2, at(1, 0)),
            reduce_copy(j, TOTALS, chip_at(0, 2), in_total, 3, at(0, 2)),
        ]

    def last_copy(j):
        return remote(
            last.at[pl.ds(j * CHUNK, CHUNK), pl.ds(pl.multiple_of(other * NODE_DEV, 8), NODE_DEV), :],
            last_in.at[pl.ds(j * CHUNK, CHUNK)],
            rs_send.at[2], rs_recv.at[j, LAST], sibling,
        )

    def reduce_start(j):
        sum_sibling(j).wait_recv()
        for i in range(CHUNK):
            t = j * CHUNK + i
            part[core, t] = (part[core, t].astype(F32) + from_sib[t].astype(F32)).astype(BF16)
        for copy in reduce_first(j):
            copy().start()

    def reduce_next(j):
        ref = in_part.at[:, pl.ds(j * CHUNK, CHUNK)]
        remote(ref, ref, rs_send.at[1], rs_recv.at[j, PARTS], sibling).wait_recv()
        for i in range(CHUNK):
            t = j * CHUNK + i
            rows = rows_of(chip_at(1, 0))
            total = part[core, t, rows, :].astype(F32) + in_part[0, t].astype(F32) + in_part[1, t].astype(F32)
            part[core, t, rows, :] = total.astype(BF16)
            rows = rows_of(chip_at(0, 2))
            total = part[core, t, rows, :].astype(F32) + in_part[2, t].astype(F32)
            part[core, t, rows, :] = total.astype(BF16)
        for copy in reduce_second(j):
            copy().start()

    def reduce_end(j):
        ref = in_total.at[:, pl.ds(j * CHUNK, CHUNK)]
        remote(ref, ref, rs_send.at[1], rs_recv.at[j, TOTALS], sibling).wait_recv()
        for i in range(CHUNK):
            t = j * CHUNK + i
            total = part[core, t, rows_of(chip), :].astype(F32)
            for slot in range(4):
                total = total + in_total[slot, t].astype(F32)
            last[t] = total
        last_copy(j).start()

    def degree_grad(degree):
        begin, end = degree * degree, (degree + 1) * (degree + 1)
        sums = fwd[begin:end].reshape((end - begin) * NODE_DEV, C).astype(BF16)
        stacked = jnp.concatenate([cot_ref[:, k * C : (k + 1) * C].astype(F32) for k in range(begin, end)], axis=0)
        return mm_tn(sums, stacked.astype(BF16)).astype(BF16)

    def radial_grad(degree):
        g_pre = (fold[degree] * att[...] * slope[degree]).astype(BF16)
        return mm(rad_t[...], g_pre).astype(BF16)

    def dp_peer(d):
        return lax.rem(dp + d, N_DP)

    def graph_peer(d):
        return lax.rem(graph + d, N_GRAPH)

    def early_rows(half, which=0, count=1):
        return pl.ds(pl.multiple_of(half * EARLY_HALF + which * EARLY_PIECE, 16), count * EARLY_PIECE)

    def sub_rows(which):
        return pl.ds(pl.multiple_of(which * EARLY_SUB, 16), EARLY_SUB)

    def chip_peer(d):
        return lax.rem(chip + d, N_CHIP)

    def e0_copy():
        return remote(epart.at[early_rows(other, 0, N_DP)], esib, e_send.at[0], e_recv.at[0], sibling)

    def e1_copy(d):
        to = dp_peer(d)
        return remote(epart.at[early_rows(core, to)], e1_in.at[d], e_send.at[1], e_recv.at[1], (to, graph))

    def e2_copy(d):
        to = chip_peer(d)
        return remote(esum.at[sub_rows(to)], e2_in.at[d], e_send.at[2], e_recv.at[2], (dp, to * 2 + core))

    def e3_copy(d):
        mine = efull.at[sub_rows(chip)]
        return remote(mine, mine, e_send.at[3], e_recv.at[3], (dp, chip_peer(d) * 2 + core))

    def e4_copy(d):
        mine = eall.at[early_rows(core, dp)]
        return remote(mine, mine, e_send.at[4], e_recv.at[4], (dp_peer(d), graph))

    def e5_copy():
        mine = eall.at[early_rows(core, 0, N_DP)]
        return remote(mine, mine, e_send.at[5], e_recv.at[5], sibling)

    def early_first():
        for degree in range(EARLY):
            epart[2 * degree * C : (2 * degree + 1) * C] = radial_grad(degree)
            epart[(2 * degree + 1) * C : (2 * degree + 2) * C] = degree_grad(degree)
        e0_copy().start()

    def early_second():
        e0_copy().wait_recv()
        rows = early_rows(core, 0, N_DP)
        epart[rows, :] = (epart[rows, :].astype(F32) + esib[...].astype(F32)).astype(BF16)

        @pl.loop(1, N_DP)
        def _(d):
            e1_copy(d).start()

    def early_third():
        ref = e1_in.at[pl.ds(1, N_DP - 1)]
        remote(ref, ref, e_send.at[1], e_recv.at[1], sibling).wait_recv()
        total = epart[early_rows(core, dp), :].astype(F32)
        for d in range(1, N_DP):
            total = total + e1_in[d].astype(F32)
        esum[0:EARLY_PIECE] = total.astype(BF16)
        esum[EARLY_PIECE:EARLY_PAD] = jnp.zeros((EARLY_PAD - EARLY_PIECE, C), BF16)

        @pl.loop(1, N_CHIP)
        def _(d):
            e2_copy(d).start()

    def early_fourth():
        ref = e2_in.at[pl.ds(1, N_CHIP - 1)]
        remote(ref, ref, e_send.at[2], e_recv.at[2], sibling).wait_recv()
        total = esum[sub_rows(chip), :].astype(F32)
        for d in range(1, N_CHIP):
            total = total + e2_in[d].astype(F32)
        efull[sub_rows(chip), :] = total.astype(BF16)

        @pl.loop(1, N_CHIP)
        def _(d):
            e3_copy(d).start()

    def early_fifth():
        ref = e2_in.at[pl.ds(1, N_CHIP - 1)]
        remote(ref, ref, e_send.at[3], e_recv.at[3], sibling).wait_recv()
        eall[early_rows(core, dp), :] = efull[0:EARLY_PIECE]

        @pl.loop(1, N_DP)
        def _(d):
            e4_copy(d).start()

    def early_sixth():
        ref = e1_in.at[pl.ds(1, N_DP - 1)]
        remote(ref, ref, e_send.at[4], e_recv.at[4], sibling).wait_recv()
        e5_copy().start()

    @pl.loop(0, CHUNKS)
    def _(s):
        @pl.when(s + 2 < CHUNKS)
        def _():
            relay(s + 2)

        @pl.when(s + 1 < CHUNKS)
        def _():
            forward(s + 1)

        @pl.when(s == CHUNKS - 3)
        def _():
            early_first()

        from_sibling(s)

        @pl.loop(0, 2 * CHUNK)
        def _(i):
            half = lax.rem(other + i // CHUNK, 2)
            edges(half, s * CHUNK + lax.rem(i, CHUNK))

            @pl.when(i == CHUNK - 1)
            def _():
                sum_sibling(s).start()

        @pl.when(s >= 1)
        def _():
            reduce_start(s - 1)

        @pl.when(s >= NEXT_LAG)
        def _():
            reduce_next(s - NEXT_LAG)

        @pl.when(s >= END_LAG)
        def _():
            reduce_end(s - END_LAG)

        @pl.when(s == CHUNKS - 3)
        def _():
            early_second()

    reduce_start(CHUNKS - 1)

    early_third()

    a = att[...]
    g_att = gate[0] * fold[0]
    for degree in range(1, LEVELS):
        g_att = g_att + gate[degree] * fold[degree]
    g_logit = head_sum(g_att) * a * (1.0 - a) * scale
    g_key = (g_logit * qe[...]).astype(BF16)
    q_high, q_low = two_parts(g_logit * key[...])
    q_node = (mm(dst_t[...], q_high) + mm(dst_t[...], q_low)).astype(BF16)
    wpart[0:C] = mm_tn(x_ref[:, 0:C], q_node[0:NODE_DEV]).astype(BF16)
    wpart[C : 2 * C] = mm_tn(ex0[...], g_key).astype(BF16)
    for i in range(LATE_DEGREES):
        wpart[(2 + 2 * i) * C : (3 + 2 * i) * C] = radial_grad(EARLY + i)
        wpart[(3 + 2 * i) * C : (4 + 2 * i) * C] = degree_grad(EARLY + i)

    def late_rows(which):
        return pl.ds(pl.multiple_of(which * LATE_PIECE, 16), LATE_PIECE)

    def w1_copy(d):
        to = graph_peer(d)
        return remote(wpart.at[late_rows(to)], win1.at[d], w1_send.at[0], w1_recv.at[0], (dp, to))

    @pl.loop(1, N_GRAPH)
    def _(d):
        w1_copy(d).start()

    back[:, 0:C] = (gm0[...] * scaled[0] + mm_nt(g_key, wk_ref[...])).astype(BF16)
    spread = mm(src_t[...], back[:, 0:C])
    pad_rows = jnp.zeros((PAD - NODE_DEV, C), F32)
    for d in range(N_GRAPH):
        p0[d] = jnp.concatenate([spread[d * NODE_DEV : (d + 1) * NODE_DEV], pad_rows], axis=0).astype(BF16)

    def p0_copy(d):
        to = lax.rem(graph + d, N_GRAPH)
        return remote(p0.at[to], in0.at[d], r0_send.at[0], r0_recv.at[0], (dp, to))

    @pl.loop(1, N_GRAPH)
    def _(d):
        p0_copy(d).start()

    early_fourth()
    for j in range(CHUNKS - NEXT_LAG, CHUNKS):
        reduce_next(j)

    for degree in range(LEVELS):
        begin, end = degree * degree, (degree + 1) * (degree + 1)
        sums = fwd[begin:end].reshape((end - begin) * NODE_DEV, C).astype(BF16)
        mixed = mm(sums, wd_ref[degree])
        for k in range(begin, end):
            rows = mixed[(k - begin) * NODE_DEV : (k - begin + 1) * NODE_DEV]
            upd_ref[:, k * C : (k + 1) * C] = (x_ref[:, k * C : (k + 1) * C].astype(F32) + rows).astype(BF16)

    remote(win1.at[pl.ds(1, N_GRAPH - 1)], win1.at[pl.ds(1, N_GRAPH - 1)], w1_send.at[0], w1_recv.at[0], sibling).wait_recv()

    total = wpart[late_rows(graph), :].astype(F32)
    for d in range(1, N_GRAPH):
        total = total + win1[d].astype(F32)
    win2[dp] = total.astype(BF16)

    def w2_copy(d):
        return remote(win2.at[dp], win2.at[dp], w2_send.at[0], w2_recv.at[0], (dp_peer(d), graph))

    @pl.loop(1, N_DP)
    def _(d):
        w2_copy(d).start()

    early_fifth()
    for j in range(CHUNKS - END_LAG, CHUNKS - 1):
        reduce_end(j)

    remote(win2.at[pl.ds(1, N_DP - 1)], win2.at[pl.ds(1, N_DP - 1)], w2_send.at[0], w2_recv.at[0], sibling).wait_recv()

    total = win2[0].astype(F32)
    for d in range(1, N_DP):
        total = total + win2[d].astype(F32)
    wall[late_rows(graph), :] = total.astype(BF16)

    def w3_copy(d):
        mine = wall.at[late_rows(graph)]
        return remote(mine, mine, w3_send.at[0], w3_recv.at[0], (dp, graph_peer(d)))

    @pl.loop(1, N_GRAPH)
    def _(d):
        w3_copy(d).start()

    early_sixth()
    reduce_end(CHUNKS - 1)

    remote(in0.at[pl.ds(1, N_GRAPH - 1)], in0.at[pl.ds(1, N_GRAPH - 1)], r0_send.at[0], r0_recv.at[0], sibling).wait_recv()

    total = p0[graph, 0:NODE_DEV, :].astype(F32)
    for d in range(1, N_GRAPH):
        total = total + in0[d, 0:NODE_DEV, :].astype(F32)
    total = total + cot_ref[:, 0:C].astype(F32) + mm_nt(q_node, wq_ref[...])[0:NODE_DEV]
    gn_ref[:, 0:C] = total.astype(BF16)

    for j in range(CHUNKS):
        last_copy(j).wait_recv()
    for t in range(HALF_PAIRS):
        own = last[t, pl.ds(pl.multiple_of(core * NODE_DEV, 8), NODE_DEV), :]
        sib = last_in[t]
        for half in range(2):
            k = 1 + 2 * (2 * t + half)
            spread = jnp.where(core == half, own, sib)
            cols = slice(k * C, (k + 2) * C)
            gn_ref[:, cols] = (cot_ref[:, cols].astype(F32) + spread).astype(BF16)

    e5_copy().wait_recv()
    ge_ref[...] = eall[...]

    remote(wall.at[pl.ds(0, (N_GRAPH - 1) * LATE_PIECE)], wall.at[pl.ds(0, (N_GRAPH - 1) * LATE_PIECE)], w3_send.at[0], w3_recv.at[0], sibling).wait_recv()

    gl_ref[...] = wall[...]

    sib_copy.wait_send()
    remote(x0all.at[pl.ds(1, N_GRAPH - 1)], x0all.at[pl.ds(1, N_GRAPH - 1)], x0_send.at[0], x0_recv.at[0], sibling).wait_send()
    remote(in0.at[pl.ds(1, N_GRAPH - 1)], in0.at[pl.ds(1, N_GRAPH - 1)], r0_send.at[0], r0_recv.at[0], sibling).wait_send()
    remote(win1.at[pl.ds(1, N_GRAPH - 1)], win1.at[pl.ds(1, N_GRAPH - 1)], w1_send.at[0], w1_recv.at[0], sibling).wait_send()
    remote(win2.at[pl.ds(1, N_DP - 1)], win2.at[pl.ds(1, N_DP - 1)], w2_send.at[0], w2_recv.at[0], sibling).wait_send()
    remote(wall.at[pl.ds(0, (N_GRAPH - 1) * LATE_PIECE)], wall.at[pl.ds(0, (N_GRAPH - 1) * LATE_PIECE)], w3_send.at[0], w3_recv.at[0], sibling).wait_send()
    remote(xall.at[0, :, pl.ds(0, 7 * CHIP_ROWS), :], xall.at[0, :, pl.ds(0, 7 * CHIP_ROWS), :], ag_send.at[0], e_recv.at[0], sibling).wait_send()
    remote(xall.at[0], xall.at[0], ag_send.at[1], e_recv.at[0], sibling).wait_send()
    remote(from_sib, from_sib, rs_send.at[0], e_recv.at[0], sibling).wait_send()
    remote(xall.at[0, :, pl.ds(0, 7 * CHIP_ROWS), :], xall.at[0, :, pl.ds(0, 7 * CHIP_ROWS), :], rs_send.at[1], e_recv.at[0], sibling).wait_send()
    remote(last_in, last_in, rs_send.at[2], e_recv.at[0], sibling).wait_send()
    remote(e1_in.at[pl.ds(1, N_DP - 1)], e1_in.at[pl.ds(1, N_DP - 1)], e_send.at[1], e_recv.at[0], sibling).wait_send()
    remote(e2_in.at[pl.ds(1, N_CHIP - 1)], e2_in.at[pl.ds(1, N_CHIP - 1)], e_send.at[2], e_recv.at[0], sibling).wait_send()
    remote(e2_in.at[pl.ds(1, N_CHIP - 1)], e2_in.at[pl.ds(1, N_CHIP - 1)], e_send.at[3], e_recv.at[0], sibling).wait_send()
    remote(e1_in.at[pl.ds(1, N_DP - 1)], e1_in.at[pl.ds(1, N_DP - 1)], e_send.at[4], e_recv.at[0], sibling).wait_send()
    remote(esib, esib, e_send.at[0], e_recv.at[0], sibling).wait_send()
    remote(esib, esib, e_send.at[5], e_recv.at[0], sibling).wait_send()


def write_kernel(u_ref, n_ref, ge_ref, gl_ref, upd_ref, gn_ref, gq_ref, gk_ref, gr_ref, gd_ref):
    upd_ref[...] = u_ref[...]
    gn_ref[...] = n_ref[...]
    for degree in range(EARLY):
        gr_ref[:, degree * C : (degree + 1) * C] = ge_ref[2 * degree * C : (2 * degree + 1) * C].astype(F32)
        gd_ref[degree] = ge_ref[(2 * degree + 1) * C : (2 * degree + 2) * C].astype(F32)
    gq_ref[...] = gl_ref[0:C].astype(F32)
    gk_ref[...] = gl_ref[C : 2 * C].astype(F32)
    for i in range(LATE_DEGREES):
        degree = EARLY + i
        gr_ref[:, degree * C : (degree + 1) * C] = gl_ref[(2 + 2 * i) * C : (3 + 2 * i) * C].astype(F32)
        gd_ref[degree] = gl_ref[(3 + 2 * i) * C : (4 + 2 * i) * C].astype(F32)


def on_device(node_feat, radial, src_node, dst_node, w_query, w_key, w_radial, w_degree, cotangent):
    vmem = pl.BlockSpec(memory_space=pltpu.VMEM)
    dma = pltpu.SemaphoreType.DMA
    width = node_feat.shape[2]
    scratch = [
        pltpu.VMEM((2, HALF_PAIRS, PAD, 2 * C), BF16),
        pltpu.VMEM((HALF_PAIRS, PAD, 2 * C), BF16),
        pltpu.VMEM((2, HALF_PAIRS, NODES, 2 * C), BF16),
        pltpu.VMEM((N_GRAPH, PAD, C), BF16),
        pltpu.VMEM((NODES, C), BF16),
        pltpu.VMEM((EDGE_DEV, NODES), BF16),
        pltpu.VMEM((NODES, EDGE_DEV), BF16),
        pltpu.VMEM((EDGE_DEV, PAD), BF16),
        pltpu.VMEM((PAD, EDGE_DEV), BF16),
        pltpu.VMEM((2 * HALF_PAIRS, PAD, 2 * C), BF16),
        pltpu.VMEM((PAD, C), BF16),
        pltpu.VMEM((LEVELS, EDGE_DEV, C), F32),
        pltpu.VMEM((LEVELS, EDGE_DEV, C), F32),
        pltpu.VMEM((LEVELS, EDGE_DEV, C), F32),
        pltpu.VMEM((LEVELS, EDGE_DEV, C), F32),
        pltpu.VMEM((LEVELS * LEVELS, NODE_DEV, C), F32),
        pltpu.VMEM((EDGE_DEV, 2 * C), BF16),
        pltpu.VMEM((EDGE_DEV, 2 * C), BF16),
        pltpu.VMEM((2, HALF_PAIRS, NODES, 2 * C), BF16),
        pltpu.VMEM((HALF_PAIRS, NODES, 2 * C), BF16),
        pltpu.VMEM((3, HALF_PAIRS, CHIP_ROWS, 2 * C), BF16),
        pltpu.VMEM((4, HALF_PAIRS, CHIP_ROWS, 2 * C), BF16),
        pltpu.VMEM((HALF_PAIRS, CHIP_ROWS, 2 * C), F32),
        pltpu.VMEM((HALF_PAIRS, NODE_DEV, 2 * C), F32),
        pltpu.VMEM((N_GRAPH, PAD, C), BF16),
        pltpu.VMEM((N_GRAPH, PAD, C), BF16),
        pltpu.VMEM((LATE_ROWS, C), BF16),
        pltpu.VMEM((N_GRAPH, LATE_PIECE, C), BF16),
        pltpu.VMEM((N_DP, LATE_PIECE, C), BF16),
        pltpu.VMEM((LATE_ROWS, C), BF16),
        pltpu.VMEM((2 * EARLY_HALF, C), BF16),
        pltpu.VMEM((EARLY_HALF, C), BF16),
        pltpu.VMEM((N_DP, EARLY_PIECE, C), BF16),
        pltpu.VMEM((EARLY_PAD, C), BF16),
        pltpu.VMEM((N_CHIP, EARLY_SUB, C), BF16),
        pltpu.VMEM((EARLY_PAD, C), BF16),
        pltpu.VMEM((2 * EARLY_HALF, C), BF16),
        pltpu.VMEM((EDGE_DEV, C), F32),
        pltpu.VMEM((EDGE_DEV, C), F32),
        pltpu.VMEM((EDGE_DEV, C), F32),
        pltpu.VMEM((EDGE_DEV, C), BF16),
        pltpu.VMEM((EDGE_DEV, C), F32),
        pltpu.VMEM((C, EDGE_DEV), BF16),
        dma((2,)),
        dma((1,)),
        dma((1,)),
        dma((2,)),
        dma((CHUNKS, 3)),
        dma((3,)),
        dma((CHUNKS, 4)),
        dma((1,)),
        dma((1,)),
        dma((1,)),
        dma((1,)),
        dma((1,)),
        dma((1,)),
        dma((1,)),
        dma((1,)),
        dma((6,)),
        dma((6,)),
    ]
    updated, grad_node, early, late = pl.pallas_call(
        kernel,
        out_shape=(
            jax.ShapeDtypeStruct((NODE_DEV, width), BF16),
            jax.ShapeDtypeStruct((NODE_DEV, width), BF16),
            jax.ShapeDtypeStruct((2 * EARLY * C, C), BF16),
            jax.ShapeDtypeStruct((LATE_ROWS, C), BF16),
        ),
        in_specs=[vmem] * 9,
        out_specs=(vmem,) * 4,
        scratch_shapes=scratch,
        compiler_params=pltpu.CompilerParams(
            collective_id=0, has_side_effects=True, vmem_limit_bytes=60 << 20
        ),
    )(node_feat[0], radial[0], src_node, dst_node, w_query, w_key, w_radial, w_degree, cotangent[0])
    updated, grad_node, grad_query, grad_key, grad_radial, grad_degree = pl.pallas_call(
        write_kernel,
        out_shape=(
            jax.ShapeDtypeStruct((NODE_DEV, width), BF16),
            jax.ShapeDtypeStruct((NODE_DEV, width), BF16),
            jax.ShapeDtypeStruct((C, C), F32),
            jax.ShapeDtypeStruct((C, C), F32),
            jax.ShapeDtypeStruct((C, LEVELS * C), F32),
            jax.ShapeDtypeStruct((LEVELS, C, C), F32),
        ),
        in_specs=[vmem] * 4,
        out_specs=(vmem,) * 6,
        compiler_params=pltpu.CompilerParams(vmem_limit_bytes=32 << 20),
    )(updated, grad_node, early, late)
    return (updated[None], grad_node[None], grad_query, grad_key, grad_radial, grad_degree)


def solution(mesh):
    return jax.shard_map(
        on_device,
        mesh=mesh,
        in_specs=(
            P("dp", "graph", None),
            P("dp", "graph", None),
            P("dp", "graph"),
            P("dp", "graph"),
            P(),
            P(),
            P(),
            P(),
            P("dp", "graph", None),
        ),
        out_specs=(P("dp", "graph", None), P("dp", "graph", None), P(), P(), P(), P()),
        check_vma=False,
    )
```

```python
import functools
import math

import jax
import jax.numpy as jnp
from jax import lax
from jax.experimental import pallas as pl
from jax.experimental.pallas import tpu as pltpu
from jax.sharding import PartitionSpec as P

HEADS = 8
C = 128
LEVELS = 7
NODE_DEV = 24
PAD = 32
EDGE_DEV = 768
NODES = 384
CHIP_ROWS = 48
N_GRAPH = 16
N_DP = 8
HALF_PAIRS = 12
CHUNK = 2
CHUNKS = HALF_PAIRS // CHUNK
ROW_BLOCK = 128
AHEAD = 2
LEAD = 2
NEXT_LAG = 2
END_LAG = 4
EARLY = 5
EARLY_HALF = EARLY * C
EARLY_PIECE = EARLY_HALF // N_DP
EARLY_PAD = 128
N_CHIP = N_GRAPH // 2
EARLY_SUB = EARLY_PAD // N_CHIP
LATE_DEGREES = LEVELS - EARLY
LATE_ROWS = (2 + 2 * LATE_DEGREES) * C
LATE_PIECE = LATE_ROWS // N_GRAPH
MESH = pl.DeviceIdType.MESH
F32 = jnp.float32
BF16 = jnp.bfloat16

FIRST, REST, SIB = range(3)
PARTS, TOTALS, LAST = range(1, 4)


def mm(a, b):
    return jnp.dot(a, b, preferred_element_type=F32)


def mm_nt(a, b):
    return lax.dot_general(a, b, (((1,), (1,)), ((), ())), preferred_element_type=F32)


def mm_tn(a, b):
    return lax.dot_general(a, b, (((0,), (0,)), ((), ())), preferred_element_type=F32)


def two_parts(a):
    high = a.astype(BF16)
    return high, (a - high.astype(F32)).astype(BF16)


def degree_of(k):
    total = 0
    for degree in range(1, LEVELS):
        total = total + (k + 64 - degree * degree) // 64
    return total


def columns(k, count=1):
    return pl.ds(pl.multiple_of(k * C, C), count * C)


def kernel(
    x_ref, rad_ref, src_ref, dst_ref, wq_ref, wk_ref, wr_ref, wd_ref, cot_ref,
    upd_ref, gn_ref, ge_ref, gl_ref,
    xs, sibx, xall, x0all, x0, src_hot, src_t, dst_hot, dst_t,
    gs, g0, gate, slope, scaled, fold, fwd, msg, back,
    part, from_sib, in_part, in_total, last, last_in, p0, in0,
    wpart, win1, win2, wall, epart, esib, e1_in, esum, e2_in, efull, eall,
    qe, key, att, ex0, gm0, rad_t,
    sib_sems, x0_send, x0_recv, ag_send, ag_recv, rs_send, rs_recv,
    r0_send, r0_recv, w1_send, w1_recv, w2_send, w2_recv, w3_send, w3_recv,
    e_send, e_recv,
):
    dp = lax.axis_index("dp")
    graph = lax.axis_index("graph")
    core = lax.rem(graph, 2)
    chip = graph // 2
    x_hi = chip // 4
    y = lax.rem(chip, 4)
    other = 1 - core

    def chip_at(dx, dy):
        return lax.rem(x_hi + dx, 2) * 4 + lax.rem(y + dy, 4)

    def at(dx, dy):
        return (dp, chip_at(dx, dy) * 2 + core)

    sibling = (dp, chip * 2 + other)

    def rows_of(which):
        return pl.ds(pl.multiple_of(which * CHIP_ROWS, 16), CHIP_ROWS)

    def remote(src, dst, send, recv, device):
        return pltpu.make_async_remote_copy(
            src_ref=src, dst_ref=dst, send_sem=send, recv_sem=recv,
            device_id=device, device_id_type=MESH,
        )

    barrier = pltpu.get_barrier_semaphore()

    @pl.loop(1, N_GRAPH)
    def _(d):
        pl.semaphore_signal(
            barrier, inc=1, device_id=(dp, lax.rem(graph + d, N_GRAPH)), device_id_type=MESH
        )

    @pl.loop(1, N_DP)
    def _(d):
        pl.semaphore_signal(
            barrier, inc=1, device_id=(lax.rem(dp + d, N_DP), graph), device_id_type=MESH
        )

    for pair in range(2 * HALF_PAIRS):
        xs[pair % 2, pair // 2, 0:NODE_DEV, :] = x_ref[:, (1 + 2 * pair) * C : (3 + 2 * pair) * C]
        xs[pair % 2, pair // 2, NODE_DEV:PAD, :] = jnp.zeros((PAD - NODE_DEV, 2 * C), BF16)
    x0all[graph, 0:NODE_DEV, :] = x_ref[:, 0:C]
    x0all[graph, NODE_DEV:PAD, :] = jnp.zeros((PAD - NODE_DEV, C), BF16)

    pl.semaphore_wait(barrier, N_GRAPH - 1 + N_DP - 1)

    sib_copy = remote(xs.at[other], sibx, sib_sems.at[0], sib_sems.at[1], sibling)
    sib_copy.start()

    def x0_copy(d):
        return remote(
            x0all.at[graph], x0all.at[graph], x0_send.at[0], x0_recv.at[0],
            (dp, lax.rem(graph + d, N_GRAPH)),
        )

    @pl.loop(1, N_GRAPH)
    def _(d):
        x0_copy(d).start()

    sib_copy.wait_recv()
    mine = xs[core, :, 0:NODE_DEV, :].astype(F32)
    theirs = sibx[:, 0:NODE_DEV, :].astype(F32)
    first = jnp.where(core == 0, mine, theirs)
    second = jnp.where(core == 0, theirs, mine)
    xall[core, :, rows_of(chip), :] = jnp.concatenate([first, second], axis=1).astype(BF16)

    def block(j, which):
        return xall.at[core, pl.ds(j * CHUNK, CHUNK), rows_of(which), :]

    def gather_copy(j, group, which, device):
        return lambda: remote(block(j, which), block(j, which), ag_send.at[0], ag_recv.at[j, group], device)

    def gather_first(j):
        return [
            gather_copy(j, FIRST, chip, at(1, 0)),
            gather_copy(j, REST, chip, at(0, 1)),
            gather_copy(j, REST, chip, at(0, 3)),
            gather_copy(j, FIRST, chip, at(0, 2)),
        ]

    def gather_second(j):
        return [
            gather_copy(j, REST, chip_at(1, 0), at(0, 1)),
            gather_copy(j, REST, chip_at(1, 0), at(0, 3)),
            gather_copy(j, REST, chip_at(0, 2), at(1, 0)),
        ]

    def to_sibling(j):
        ref = xall.at[core, pl.ds(j * CHUNK, CHUNK)]
        return remote(ref, ref, ag_send.at[1], ag_recv.at[j, SIB], sibling)

    def got_blocks(j, group, count):
        ref = xall.at[core, pl.ds(j * CHUNK, CHUNK), pl.ds(0, count * CHIP_ROWS), :]
        remote(ref, ref, ag_send.at[0], ag_recv.at[j, group], sibling).wait_recv()

    @pl.loop(0, AHEAD)
    def _(j):
        for copy in gather_first(j):
            copy().start()

    def relay(j):
        got_blocks(j, FIRST, 2)
        for copy in gather_second(j):
            copy().start()

        @pl.when(j + AHEAD < CHUNKS)
        def _():
            for copy in gather_first(j + AHEAD):
                copy().start()

    def forward(j):
        got_blocks(j, REST, 5)
        to_sibling(j).start()

    def from_sibling(j):
        ref = xall.at[other, pl.ds(j * CHUNK, CHUNK)]
        remote(ref, ref, ag_send.at[1], ag_recv.at[j, SIB], sibling).wait_recv()

    src_row = src_ref[...].astype(F32)
    dst_row = (dst_ref[...] - graph * NODE_DEV).astype(F32)
    src_t[...] = (lax.broadcasted_iota(jnp.int32, (NODES, EDGE_DEV), 0).astype(F32) == src_row).astype(F32).astype(BF16)
    dst_t[...] = (lax.broadcasted_iota(jnp.int32, (PAD, EDGE_DEV), 0).astype(F32) == dst_row).astype(F32).astype(BF16)
    src_col = jnp.broadcast_to(src_row, (8, EDGE_DEV)).T[:, 0:1]
    dst_col = jnp.broadcast_to(dst_row, (8, EDGE_DEV)).T[:, 0:1]
    src_hot[...] = (lax.broadcasted_iota(jnp.int32, (EDGE_DEV, NODES), 1).astype(F32) == src_col).astype(F32).astype(BF16)
    dst_hot[...] = (lax.broadcasted_iota(jnp.int32, (EDGE_DEV, PAD), 1).astype(F32) == dst_col).astype(F32).astype(BF16)

    rad_t[...] = rad_ref[...].T
    for degree in range(LEVELS):
        pre = mm(rad_ref[...], wr_ref[:, degree * C : (degree + 1) * C])
        sigma = jax.nn.sigmoid(pre)
        gate[degree] = pre * sigma
        slope[degree] = sigma * (1.0 + pre * (1.0 - sigma))
        fold[degree] = jnp.zeros((EDGE_DEV, C), F32)

    relay(0)
    zeros = jnp.zeros((PAD - NODE_DEV, C), F32)
    for degree in range(LEVELS):
        begin, end = degree * degree, (degree + 1) * (degree + 1)
        stacked = jnp.concatenate([cot_ref[:, k * C : (k + 1) * C].astype(F32) for k in range(begin, end)], axis=0)
        mixed = mm_nt(stacked.astype(BF16), wd_ref[degree])
        for k in range(begin, end):
            rows = mixed[(k - begin) * NODE_DEV : (k - begin + 1) * NODE_DEV]
            rows = jnp.concatenate([rows, zeros], axis=0).astype(BF16)
            if k == 0:
                g0[...] = rows
            else:
                lane = (k - 1) % 2
                gs[(k - 1) // 2, :, lane * C : (lane + 1) * C] = rows

    query = jnp.concatenate([mm(x_ref[:, 0:C], wq_ref[...]), zeros], axis=0)
    q_high, q_low = two_parts(query)
    qe[...] = mm(dst_hot[...], q_high) + mm(dst_hot[...], q_low)
    gm0[...] = mm(dst_hot[...], g0[...])

    head_rows = lax.broadcasted_iota(jnp.int32, (C, C), 0) // (C // HEADS)
    head_cols = lax.broadcasted_iota(jnp.int32, (C, C), 1) // (C // HEADS)
    same_head = (head_rows == head_cols).astype(F32).astype(BF16)
    scale = 1.0 / math.sqrt(C // HEADS)

    def head_sum(a):
        high, low = two_parts(a)
        return mm(high, same_head) + mm(low, same_head)

    remote(x0all.at[pl.ds(1, N_GRAPH - 1)], x0all.at[pl.ds(1, N_GRAPH - 1)], x0_send.at[0], x0_recv.at[0], sibling).wait_recv()

    x0[...] = jnp.concatenate([x0all[d, 0:NODE_DEV, :].astype(F32) for d in range(N_GRAPH)], axis=0).astype(BF16)
    relay(1)
    ex0[...] = mm(src_hot[...], x0[...]).astype(BF16)
    key[...] = mm(ex0[...], wk_ref[...])
    att[...] = jax.nn.sigmoid(head_sum(qe[...] * key[...]) * scale)
    for degree in range(LEVELS):
        scaled[degree] = gate[degree] * att[...]
    ex0_float = ex0[...].astype(F32)
    fold[0] = ex0_float * gm0[...]
    forward(0)
    fwd[0] = mm(dst_t[...], (ex0_float * scaled[0]).astype(BF16))[0:NODE_DEV]

    def edges(half, t):
        pair = 2 * t + half
        k = 1 + 2 * pair
        left, right = degree_of(k), degree_of(k + 1)
        nodes = xall[half, t]
        ups = gs[pair]
        for begin in range(0, EDGE_DEV, ROW_BLOCK):
            rows = slice(begin, begin + ROW_BLOCK)
            ex = mm(src_hot[rows, :], nodes)
            gm = mm(dst_hot[rows, :], ups)
            for lane, degree in ((0, left), (1, right)):
                cols = slice(lane * C, (lane + 1) * C)
                factor = scaled[degree, rows, :]
                msg[rows, cols] = (ex[:, cols] * factor).astype(BF16)
                back[rows, cols] = (gm[:, cols] * factor).astype(BF16)
                fold[degree, rows, :] += ex[:, cols] * gm[:, cols]
        gathered = mm(dst_t[...], msg[...])
        fwd[k] = gathered[0:NODE_DEV, 0:C]
        fwd[k + 1] = gathered[0:NODE_DEV, C : 2 * C]
        part[half, t] = mm(src_t[...], back[...]).astype(BF16)

    def sum_sibling(j):
        return remote(
            part.at[other, pl.ds(j * CHUNK, CHUNK)], from_sib.at[pl.ds(j * CHUNK, CHUNK)],
            rs_send.at[0], rs_recv.at[j, 0], sibling,
        )

    def part_block(j, which):
        return part.at[core, pl.ds(j * CHUNK, CHUNK), rows_of(which), :]

    def reduce_copy(j, group, which, landing, slot, device):
        return lambda: remote(
            part_block(j, which), landing.at[slot, pl.ds(j * CHUNK, CHUNK)],
            rs_send.at[1], rs_recv.at[j, group], device,
        )

    def reduce_first(j):
        return [
            reduce_copy(j, PARTS, chip_at(1, 1), in_part, 0, at(0, 1)),
            reduce_copy(j, PARTS, chip_at(1, 3), in_part, 1, at(0, 3)),
            reduce_copy(j, PARTS, chip_at(1, 2), in_part, 2, at(1, 0)),
            reduce_copy(j, TOTALS, chip_at(0, 1), in_total, 0, at(0, 1)),
            reduce_copy(j, TOTALS, chip_at(0, 3), in_total, 1, at(0, 3)),
        ]

    def reduce_second(j):
        return [
            reduce_copy(j, TOTALS, chip_at(1, 0), in_total, 2, at(1, 0)),
            reduce_copy(j, TOTALS, chip_at(0, 2), in_total, 3, at(0, 2)),
        ]

    def last_copy(j):
        return remote(
            last.at[pl.ds(j * CHUNK, CHUNK), pl.ds(pl.multiple_of(other * NODE_DEV, 8), NODE_DEV), :],
            last_in.at[pl.ds(j * CHUNK, CHUNK)],
            rs_send.at[2], rs_recv.at[j, LAST], sibling,
        )

    def reduce_start(j):
        sum_sibling(j).wait_recv()
        for i in range(CHUNK):
            t = j * CHUNK + i
            part[core, t] = (part[core, t].astype(F32) + from_sib[t].astype(F32)).astype(BF16)
        for copy in reduce_first(j):
            copy().start()

    def reduce_next(j):
        ref = in_part.at[:, pl.ds(j * CHUNK, CHUNK)]
        remote(ref, ref, rs_send.at[1], rs_recv.at[j, PARTS], sibling).wait_recv()
        for i in range(CHUNK):
            t = j * CHUNK + i
            rows = rows_of(chip_at(1, 0))
            total = part[core, t, rows, :].astype(F32) + in_part[0, t].astype(F32) + in_part[1, t].astype(F32)
            part[core, t, rows, :] = total.astype(BF16)
            rows = rows_of(chip_at(0, 2))
            total = part[core, t, rows, :].astype(F32) + in_part[2, t].astype(F32)
            part[core, t, rows, :] = total.astype(BF16)
        for copy in reduce_second(j):
            copy().start()

    def reduce_end(j):
        ref = in_total.at[:, pl.ds(j * CHUNK, CHUNK)]
        remote(ref, ref, rs_send.at[1], rs_recv.at[j, TOTALS], sibling).wait_recv()
        for i in range(CHUNK):
            t = j * CHUNK + i
            total = part[core, t, rows_of(chip), :].astype(F32)
            for slot in range(4):
                total = total + in_total[slot, t].astype(F32)
            last[t] = total
        last_copy(j).start()

    def degree_grad(degree):
        begin, end = degree * degree, (degree + 1) * (degree + 1)
        sums = fwd[begin:end].reshape((end - begin) * NODE_DEV, C).astype(BF16)
        stacked = jnp.concatenate([cot_ref[:, k * C : (k + 1) * C].astype(F32) for k in range(begin, end)], axis=0)
        return mm_tn(sums, stacked.astype(BF16)).astype(BF16)

    def radial_grad(degree):
        g_pre = (fold[degree] * att[...] * slope[degree]).astype(BF16)
        return mm(rad_t[...], g_pre).astype(BF16)

    def dp_peer(d):
        return lax.rem(dp + d, N_DP)

    def graph_peer(d):
        return lax.rem(graph + d, N_GRAPH)

    def early_rows(half, which=0, count=1):
        return pl.ds(pl.multiple_of(half * EARLY_HALF + which * EARLY_PIECE, 16), count * EARLY_PIECE)

    def sub_rows(which):
        return pl.ds(pl.multiple_of(which * EARLY_SUB, 16), EARLY_SUB)

    def chip_peer(d):
        return lax.rem(chip + d, N_CHIP)

    def e0_copy():
        return remote(epart.at[early_rows(other, 0, N_DP)], esib, e_send.at[0], e_recv.at[0], sibling)

    def e1_copy(d):
        to = dp_peer(d)
        return remote(epart.at[early_rows(core, to)], e1_in.at[d], e_send.at[1], e_recv.at[1], (to, graph))

    def e2_copy(d):
        to = chip_peer(d)
        return remote(esum.at[sub_rows(to)], e2_in.at[d], e_send.at[2], e_recv.at[2], (dp, to * 2 + core))

    def e3_copy(d):
        mine = efull.at[sub_rows(chip)]
        return remote(mine, mine, e_send.at[3], e_recv.at[3], (dp, chip_peer(d) * 2 + core))

    def e4_copy(d):
        mine = eall.at[early_rows(core, dp)]
        return remote(mine, mine, e_send.at[4], e_recv.at[4], (dp_peer(d), graph))

    def e5_copy():
        mine = eall.at[early_rows(core, 0, N_DP)]
        return remote(mine, mine, e_send.at[5], e_recv.at[5], sibling)

    def early_first():
        for degree in range(EARLY):
            epart[2 * degree * C : (2 * degree + 1) * C] = radial_grad(degree)
            epart[(2 * degree + 1) * C : (2 * degree + 2) * C] = degree_grad(degree)
        e0_copy().start()

    def early_second():
        e0_copy().wait_recv()
        rows = early_rows(core, 0, N_DP)
        epart[rows, :] = (epart[rows, :].astype(F32) + esib[...].astype(F32)).astype(BF16)

        @pl.loop(1, N_DP)
        def _(d):
            e1_copy(d).start()

    def early_third():
        ref = e1_in.at[pl.ds(1, N_DP - 1)]
        remote(ref, ref, e_send.at[1], e_recv.at[1], sibling).wait_recv()
        total = epart[early_rows(core, dp), :].astype(F32)
        for d in range(1, N_DP):
            total = total + e1_in[d].astype(F32)
        esum[0:EARLY_PIECE] = total.astype(BF16)
        esum[EARLY_PIECE:EARLY_PAD] = jnp.zeros((EARLY_PAD - EARLY_PIECE, C), BF16)

        @pl.loop(1, N_CHIP)
        def _(d):
            e2_copy(d).start()

    def early_fourth():
        ref = e2_in.at[pl.ds(1, N_CHIP - 1)]
        remote(ref, ref, e_send.at[2], e_recv.at[2], sibling).wait_recv()
        total = esum[sub_rows(chip), :].astype(F32)
        for d in range(1, N_CHIP):
            total = total + e2_in[d].astype(F32)
        efull[sub_rows(chip), :] = total.astype(BF16)

        @pl.loop(1, N_CHIP)
        def _(d):
            e3_copy(d).start()

    def early_fifth():
        ref = e2_in.at[pl.ds(1, N_CHIP - 1)]
        remote(ref, ref, e_send.at[3], e_recv.at[3], sibling).wait_recv()
        eall[early_rows(core, dp), :] = efull[0:EARLY_PIECE]

        @pl.loop(1, N_DP)
        def _(d):
            e4_copy(d).start()

    def early_sixth():
        ref = e1_in.at[pl.ds(1, N_DP - 1)]
        remote(ref, ref, e_send.at[4], e_recv.at[4], sibling).wait_recv()
        e5_copy().start()

    @pl.loop(0, CHUNKS)
    def _(s):
        @pl.when(s + LEAD < CHUNKS)
        def _():
            relay(s + LEAD)

        @pl.when(s == CHUNKS - 3)
        def _():
            early_first()

        @pl.loop(0, 2 * CHUNK)
        def _(i):
            @pl.when(i == CHUNK)
            def _():
                @pl.when(s + 1 < CHUNKS)
                def _():
                    forward(s + 1)

                from_sibling(s)

            edges(lax.rem(core + i // CHUNK, 2), s * CHUNK + lax.rem(i, CHUNK))

        sum_sibling(s).start()

        @pl.when(s >= 1)
        def _():
            reduce_start(s - 1)

        @pl.when(s >= NEXT_LAG)
        def _():
            reduce_next(s - NEXT_LAG)

        @pl.when(s >= END_LAG)
        def _():
            reduce_end(s - END_LAG)

        @pl.when(s == CHUNKS - 3)
        def _():
            early_second()

    reduce_start(CHUNKS - 1)

    early_third()

    a = att[...]
    g_att = gate[0] * fold[0]
    for degree in range(1, LEVELS):
        g_att = g_att + gate[degree] * fold[degree]
    g_logit = head_sum(g_att) * a * (1.0 - a) * scale
    g_key = (g_logit * qe[...]).astype(BF16)
    q_high, q_low = two_parts(g_logit * key[...])
    q_node = (mm(dst_t[...], q_high) + mm(dst_t[...], q_low)).astype(BF16)
    wpart[0:C] = mm_tn(x_ref[:, 0:C], q_node[0:NODE_DEV]).astype(BF16)
    wpart[C : 2 * C] = mm_tn(ex0[...], g_key).astype(BF16)
    for i in range(LATE_DEGREES):
        wpart[(2 + 2 * i) * C : (3 + 2 * i) * C] = radial_grad(EARLY + i)
        wpart[(3 + 2 * i) * C : (4 + 2 * i) * C] = degree_grad(EARLY + i)

    def late_rows(which):
        return pl.ds(pl.multiple_of(which * LATE_PIECE, 16), LATE_PIECE)

    def w1_copy(d):
        to = graph_peer(d)
        return remote(wpart.at[late_rows(to)], win1.at[d], w1_send.at[0], w1_recv.at[0], (dp, to))

    @pl.loop(1, N_GRAPH)
    def _(d):
        w1_copy(d).start()

    back[:, 0:C] = (gm0[...] * scaled[0] + mm_nt(g_key, wk_ref[...])).astype(BF16)
    spread = mm(src_t[...], back[:, 0:C])
    pad_rows = jnp.zeros((PAD - NODE_DEV, C), F32)
    for d in range(N_GRAPH):
        p0[d] = jnp.concatenate([spread[d * NODE_DEV : (d + 1) * NODE_DEV], pad_rows], axis=0).astype(BF16)

    def p0_copy(d):
        to = lax.rem(graph + d, N_GRAPH)
        return remote(p0.at[to], in0.at[d], r0_send.at[0], r0_recv.at[0], (dp, to))

    @pl.loop(1, N_GRAPH)
    def _(d):
        p0_copy(d).start()

    early_fourth()
    for j in range(CHUNKS - NEXT_LAG, CHUNKS):
        reduce_next(j)

    for degree in range(LEVELS):
        begin, end = degree * degree, (degree + 1) * (degree + 1)
        sums = fwd[begin:end].reshape((end - begin) * NODE_DEV, C).astype(BF16)
        mixed = mm(sums, wd_ref[degree])
        for k in range(begin, end):
            rows = mixed[(k - begin) * NODE_DEV : (k - begin + 1) * NODE_DEV]
            upd_ref[:, k * C : (k + 1) * C] = (x_ref[:, k * C : (k + 1) * C].astype(F32) + rows).astype(BF16)

    remote(win1.at[pl.ds(1, N_GRAPH - 1)], win1.at[pl.ds(1, N_GRAPH - 1)], w1_send.at[0], w1_recv.at[0], sibling).wait_recv()

    total = wpart[late_rows(graph), :].astype(F32)
    for d in range(1, N_GRAPH):
        total = total + win1[d].astype(F32)
    win2[dp] = total.astype(BF16)

    def w2_copy(d):
        return remote(win2.at[dp], win2.at[dp], w2_send.at[0], w2_recv.at[0], (dp_peer(d), graph))

    @pl.loop(1, N_DP)
    def _(d):
        w2_copy(d).start()

    early_fifth()
    for j in range(CHUNKS - END_LAG, CHUNKS - 1):
        reduce_end(j)

    remote(win2.at[pl.ds(1, N_DP - 1)], win2.at[pl.ds(1, N_DP - 1)], w2_send.at[0], w2_recv.at[0], sibling).wait_recv()

    total = win2[0].astype(F32)
    for d in range(1, N_DP):
        total = total + win2[d].astype(F32)
    wall[late_rows(graph), :] = total.astype(BF16)

    def w3_copy(d):
        mine = wall.at[late_rows(graph)]
        return remote(mine, mine, w3_send.at[0], w3_recv.at[0], (dp, graph_peer(d)))

    @pl.loop(1, N_GRAPH)
    def _(d):
        w3_copy(d).start()

    early_sixth()
    reduce_end(CHUNKS - 1)

    remote(in0.at[pl.ds(1, N_GRAPH - 1)], in0.at[pl.ds(1, N_GRAPH - 1)], r0_send.at[0], r0_recv.at[0], sibling).wait_recv()

    total = p0[graph, 0:NODE_DEV, :].astype(F32)
    for d in range(1, N_GRAPH):
        total = total + in0[d, 0:NODE_DEV, :].astype(F32)
    total = total + cot_ref[:, 0:C].astype(F32) + mm_nt(q_node, wq_ref[...])[0:NODE_DEV]
    gn_ref[:, 0:C] = total.astype(BF16)

    for j in range(CHUNKS):
        last_copy(j).wait_recv()
    for t in range(HALF_PAIRS):
        own = last[t, pl.ds(pl.multiple_of(core * NODE_DEV, 8), NODE_DEV), :]
        sib = last_in[t]
        for half in range(2):
            k = 1 + 2 * (2 * t + half)
            spread = jnp.where(core == half, own, sib)
            cols = slice(k * C, (k + 2) * C)
            gn_ref[:, cols] = (cot_ref[:, cols].astype(F32) + spread).astype(BF16)

    e5_copy().wait_recv()
    ge_ref[...] = eall[...]

    remote(wall.at[pl.ds(0, (N_GRAPH - 1) * LATE_PIECE)], wall.at[pl.ds(0, (N_GRAPH - 1) * LATE_PIECE)], w3_send.at[0], w3_recv.at[0], sibling).wait_recv()

    gl_ref[...] = wall[...]

    sib_copy.wait_send()
    remote(x0all.at[pl.ds(1, N_GRAPH - 1)], x0all.at[pl.ds(1, N_GRAPH - 1)], x0_send.at[0], x0_recv.at[0], sibling).wait_send()
    remote(in0.at[pl.ds(1, N_GRAPH - 1)], in0.at[pl.ds(1, N_GRAPH - 1)], r0_send.at[0], r0_recv.at[0], sibling).wait_send()
    remote(win1.at[pl.ds(1, N_GRAPH - 1)], win1.at[pl.ds(1, N_GRAPH - 1)], w1_send.at[0], w1_recv.at[0], sibling).wait_send()
    remote(win2.at[pl.ds(1, N_DP - 1)], win2.at[pl.ds(1, N_DP - 1)], w2_send.at[0], w2_recv.at[0], sibling).wait_send()
    remote(wall.at[pl.ds(0, (N_GRAPH - 1) * LATE_PIECE)], wall.at[pl.ds(0, (N_GRAPH - 1) * LATE_PIECE)], w3_send.at[0], w3_recv.at[0], sibling).wait_send()
    remote(xall.at[0, :, pl.ds(0, 7 * CHIP_ROWS), :], xall.at[0, :, pl.ds(0, 7 * CHIP_ROWS), :], ag_send.at[0], e_recv.at[0], sibling).wait_send()
    remote(xall.at[0], xall.at[0], ag_send.at[1], e_recv.at[0], sibling).wait_send()
    remote(from_sib, from_sib, rs_send.at[0], e_recv.at[0], sibling).wait_send()
    remote(xall.at[0, :, pl.ds(0, 7 * CHIP_ROWS), :], xall.at[0, :, pl.ds(0, 7 * CHIP_ROWS), :], rs_send.at[1], e_recv.at[0], sibling).wait_send()
    remote(last_in, last_in, rs_send.at[2], e_recv.at[0], sibling).wait_send()
    remote(e1_in.at[pl.ds(1, N_DP - 1)], e1_in.at[pl.ds(1, N_DP - 1)], e_send.at[1], e_recv.at[0], sibling).wait_send()
    remote(e2_in.at[pl.ds(1, N_CHIP - 1)], e2_in.at[pl.ds(1, N_CHIP - 1)], e_send.at[2], e_recv.at[0], sibling).wait_send()
    remote(e2_in.at[pl.ds(1, N_CHIP - 1)], e2_in.at[pl.ds(1, N_CHIP - 1)], e_send.at[3], e_recv.at[0], sibling).wait_send()
    remote(e1_in.at[pl.ds(1, N_DP - 1)], e1_in.at[pl.ds(1, N_DP - 1)], e_send.at[4], e_recv.at[0], sibling).wait_send()
    remote(esib, esib, e_send.at[0], e_recv.at[0], sibling).wait_send()
    remote(esib, esib, e_send.at[5], e_recv.at[0], sibling).wait_send()


def write_kernel(u_ref, n_ref, ge_ref, gl_ref, upd_ref, gn_ref, gq_ref, gk_ref, gr_ref, gd_ref):
    upd_ref[...] = u_ref[...]
    gn_ref[...] = n_ref[...]
    for degree in range(EARLY):
        gr_ref[:, degree * C : (degree + 1) * C] = ge_ref[2 * degree * C : (2 * degree + 1) * C].astype(F32)
        gd_ref[degree] = ge_ref[(2 * degree + 1) * C : (2 * degree + 2) * C].astype(F32)
    gq_ref[...] = gl_ref[0:C].astype(F32)
    gk_ref[...] = gl_ref[C : 2 * C].astype(F32)
    for i in range(LATE_DEGREES):
        degree = EARLY + i
        gr_ref[:, degree * C : (degree + 1) * C] = gl_ref[(2 + 2 * i) * C : (3 + 2 * i) * C].astype(F32)
        gd_ref[degree] = gl_ref[(3 + 2 * i) * C : (4 + 2 * i) * C].astype(F32)


def on_device(node_feat, radial, src_node, dst_node, w_query, w_key, w_radial, w_degree, cotangent):
    vmem = pl.BlockSpec(memory_space=pltpu.VMEM)
    dma = pltpu.SemaphoreType.DMA
    width = node_feat.shape[2]
    scratch = [
        pltpu.VMEM((2, HALF_PAIRS, PAD, 2 * C), BF16),
        pltpu.VMEM((HALF_PAIRS, PAD, 2 * C), BF16),
        pltpu.VMEM((2, HALF_PAIRS, NODES, 2 * C), BF16),
        pltpu.VMEM((N_GRAPH, PAD, C), BF16),
        pltpu.VMEM((NODES, C), BF16),
        pltpu.VMEM((EDGE_DEV, NODES), BF16),
        pltpu.VMEM((NODES, EDGE_DEV), BF16),
        pltpu.VMEM((EDGE_DEV, PAD), BF16),
        pltpu.VMEM((PAD, EDGE_DEV), BF16),
        pltpu.VMEM((2 * HALF_PAIRS, PAD, 2 * C), BF16),
        pltpu.VMEM((PAD, C), BF16),
        pltpu.VMEM((LEVELS, EDGE_DEV, C), F32),
        pltpu.VMEM((LEVELS, EDGE_DEV, C), F32),
        pltpu.VMEM((LEVELS, EDGE_DEV, C), F32),
        pltpu.VMEM((LEVELS, EDGE_DEV, C), F32),
        pltpu.VMEM((LEVELS * LEVELS, NODE_DEV, C), F32),
        pltpu.VMEM((EDGE_DEV, 2 * C), BF16),
        pltpu.VMEM((EDGE_DEV, 2 * C), BF16),
        pltpu.VMEM((2, HALF_PAIRS, NODES, 2 * C), BF16),
        pltpu.VMEM((HALF_PAIRS, NODES, 2 * C), BF16),
        pltpu.VMEM((3, HALF_PAIRS, CHIP_ROWS, 2 * C), BF16),
        pltpu.VMEM((4, HALF_PAIRS, CHIP_ROWS, 2 * C), BF16),
        pltpu.VMEM((HALF_PAIRS, CHIP_ROWS, 2 * C), F32),
        pltpu.VMEM((HALF_PAIRS, NODE_DEV, 2 * C), F32),
        pltpu.VMEM((N_GRAPH, PAD, C), BF16),
        pltpu.VMEM((N_GRAPH, PAD, C), BF16),
        pltpu.VMEM((LATE_ROWS, C), BF16),
        pltpu.VMEM((N_GRAPH, LATE_PIECE, C), BF16),
        pltpu.VMEM((N_DP, LATE_PIECE, C), BF16),
        pltpu.VMEM((LATE_ROWS, C), BF16),
        pltpu.VMEM((2 * EARLY_HALF, C), BF16),
        pltpu.VMEM((EARLY_HALF, C), BF16),
        pltpu.VMEM((N_DP, EARLY_PIECE, C), BF16),
        pltpu.VMEM((EARLY_PAD, C), BF16),
        pltpu.VMEM((N_CHIP, EARLY_SUB, C), BF16),
        pltpu.VMEM((EARLY_PAD, C), BF16),
        pltpu.VMEM((2 * EARLY_HALF, C), BF16),
        pltpu.VMEM((EDGE_DEV, C), F32),
        pltpu.VMEM((EDGE_DEV, C), F32),
        pltpu.VMEM((EDGE_DEV, C), F32),
        pltpu.VMEM((EDGE_DEV, C), BF16),
        pltpu.VMEM((EDGE_DEV, C), F32),
        pltpu.VMEM((C, EDGE_DEV), BF16),
        dma((2,)),
        dma((1,)),
        dma((1,)),
        dma((2,)),
        dma((CHUNKS, 3)),
        dma((3,)),
        dma((CHUNKS, 4)),
        dma((1,)),
        dma((1,)),
        dma((1,)),
        dma((1,)),
        dma((1,)),
        dma((1,)),
        dma((1,)),
        dma((1,)),
        dma((6,)),
        dma((6,)),
    ]
    updated, grad_node, early, late = pl.pallas_call(
        kernel,
        out_shape=(
            jax.ShapeDtypeStruct((NODE_DEV, width), BF16),
            jax.ShapeDtypeStruct((NODE_DEV, width), BF16),
            jax.ShapeDtypeStruct((2 * EARLY * C, C), BF16),
            jax.ShapeDtypeStruct((LATE_ROWS, C), BF16),
        ),
        in_specs=[vmem] * 9,
        out_specs=(vmem,) * 4,
        scratch_shapes=scratch,
        compiler_params=pltpu.CompilerParams(
            collective_id=0, has_side_effects=True, vmem_limit_bytes=60 << 20
        ),
    )(node_feat[0], radial[0], src_node, dst_node, w_query, w_key, w_radial, w_degree, cotangent[0])
    updated, grad_node, grad_query, grad_key, grad_radial, grad_degree = pl.pallas_call(
        write_kernel,
        out_shape=(
            jax.ShapeDtypeStruct((NODE_DEV, width), BF16),
            jax.ShapeDtypeStruct((NODE_DEV, width), BF16),
            jax.ShapeDtypeStruct((C, C), F32),
            jax.ShapeDtypeStruct((C, C), F32),
            jax.ShapeDtypeStruct((C, LEVELS * C), F32),
            jax.ShapeDtypeStruct((LEVELS, C, C), F32),
        ),
        in_specs=[vmem] * 4,
        out_specs=(vmem,) * 6,
        compiler_params=pltpu.CompilerParams(vmem_limit_bytes=32 << 20),
    )(updated, grad_node, early, late)
    return (updated[None], grad_node[None], grad_query, grad_key, grad_radial, grad_degree)


def solution(mesh):
    return jax.shard_map(
        on_device,
        mesh=mesh,
        in_specs=(
            P("dp", "graph", None),
            P("dp", "graph", None),
            P("dp", "graph"),
            P("dp", "graph"),
            P(),
            P(),
            P(),
            P(),
            P("dp", "graph", None),
        ),
        out_specs=(P("dp", "graph", None), P("dp", "graph", None), P(), P(), P(), P()),
        check_vma=False,
    )
```

```python
import functools
import math

import jax
import jax.numpy as jnp
from jax import lax
from jax.experimental import pallas as pl
from jax.experimental.pallas import tpu as pltpu
from jax.sharding import PartitionSpec as P

HEADS = 8
C = 128
LEVELS = 7
NODE_DEV = 24
PAD = 32
EDGE_DEV = 768
NODES = 384
CHIP_ROWS = 48
N_GRAPH = 16
N_DP = 8
HALF_PAIRS = 12
CHUNK = 2
CHUNKS = HALF_PAIRS // CHUNK
ROW_BLOCK = 128
AHEAD = 2
LEAD = 2
NEXT_LAG = 2
END_LAG = 4
EARLY = 5
EARLY_HALF = EARLY * C
EARLY_PIECE = EARLY_HALF // N_DP
EARLY_PAD = 128
N_CHIP = N_GRAPH // 2
EARLY_SUB = EARLY_PAD // N_CHIP
LATE_DEGREES = LEVELS - EARLY
LATE_ROWS = (2 + 2 * LATE_DEGREES) * C
LATE_PIECE = LATE_ROWS // N_GRAPH
MESH = pl.DeviceIdType.MESH
F32 = jnp.float32
BF16 = jnp.bfloat16

FIRST, REST, SIB = range(3)
PARTS, TOTALS, LAST = range(1, 4)


def mm(a, b):
    return jnp.dot(a, b, preferred_element_type=F32)


def mm_nt(a, b):
    return lax.dot_general(a, b, (((1,), (1,)), ((), ())), preferred_element_type=F32)


def mm_tn(a, b):
    return lax.dot_general(a, b, (((0,), (0,)), ((), ())), preferred_element_type=F32)


def two_parts(a):
    high = a.astype(BF16)
    return high, (a - high.astype(F32)).astype(BF16)


def degree_of(k):
    total = 0
    for degree in range(1, LEVELS):
        total = total + (k + 64 - degree * degree) // 64
    return total


def columns(k, count=1):
    return pl.ds(pl.multiple_of(k * C, C), count * C)


def kernel(
    x_ref, rad_ref, src_ref, dst_ref, wq_ref, wk_ref, wr_ref, wd_ref, cot_ref,
    upd_ref, gn_ref, ge_ref, gl_ref,
    xs, sibx, xall, x0all, x0, src_hot, src_t, dst_hot, dst_t,
    gs, g0, gate, slope, scaled, fold, fwd, msg, back,
    part, from_sib, in_part, in_total, last, last_in, p0, in0,
    wpart, win1, win2, wall, epart, esib, e1_in, esum, e2_in, efull, eall,
    qe, key, att, ex0, gm0, rad_t,
    sib_sems, x0_send, x0_recv, ag_send, ag_recv, rs_send, rs_recv,
    r0_send, r0_recv, w1_send, w1_recv, w2_send, w2_recv, w3_send, w3_recv,
    e_send, e_recv,
):
    dp = lax.axis_index("dp")
    graph = lax.axis_index("graph")
    core = lax.rem(graph, 2)
    chip = graph // 2
    x_hi = chip // 4
    y = lax.rem(chip, 4)
    other = 1 - core

    def chip_at(dx, dy):
        return lax.rem(x_hi + dx, 2) * 4 + lax.rem(y + dy, 4)

    def at(dx, dy):
        return (dp, chip_at(dx, dy) * 2 + core)

    sibling = (dp, chip * 2 + other)

    def rows_of(which):
        return pl.ds(pl.multiple_of(which * CHIP_ROWS, 16), CHIP_ROWS)

    def remote(src, dst, send, recv, device):
        return pltpu.make_async_remote_copy(
            src_ref=src, dst_ref=dst, send_sem=send, recv_sem=recv,
            device_id=device, device_id_type=MESH,
        )

    barrier = pltpu.get_barrier_semaphore()

    @pl.loop(1, N_GRAPH)
    def _(d):
        pl.semaphore_signal(
            barrier, inc=1, device_id=(dp, lax.rem(graph + d, N_GRAPH)), device_id_type=MESH
        )

    @pl.loop(1, N_DP)
    def _(d):
        pl.semaphore_signal(
            barrier, inc=1, device_id=(lax.rem(dp + d, N_DP), graph), device_id_type=MESH
        )

    for pair in range(2 * HALF_PAIRS):
        xs[pair % 2, pair // 2, 0:NODE_DEV, :] = x_ref[:, (1 + 2 * pair) * C : (3 + 2 * pair) * C]
        xs[pair % 2, pair // 2, NODE_DEV:PAD, :] = jnp.zeros((PAD - NODE_DEV, 2 * C), BF16)
    x0all[graph, 0:NODE_DEV, :] = x_ref[:, 0:C]
    x0all[graph, NODE_DEV:PAD, :] = jnp.zeros((PAD - NODE_DEV, C), BF16)

    pl.semaphore_wait(barrier, N_GRAPH - 1 + N_DP - 1)

    sib_copy = remote(xs.at[other], sibx, sib_sems.at[0], sib_sems.at[1], sibling)
    sib_copy.start()

    def x0_copy(d):
        return remote(
            x0all.at[graph], x0all.at[graph], x0_send.at[0], x0_recv.at[0],
            (dp, lax.rem(graph + d, N_GRAPH)),
        )

    @pl.loop(1, N_GRAPH)
    def _(d):
        x0_copy(d).start()

    sib_copy.wait_recv()
    mine = xs[core, :, 0:NODE_DEV, :].astype(F32)
    theirs = sibx[:, 0:NODE_DEV, :].astype(F32)
    first = jnp.where(core == 0, mine, theirs)
    second = jnp.where(core == 0, theirs, mine)
    xall[core, :, rows_of(chip), :] = jnp.concatenate([first, second], axis=1).astype(BF16)

    def block(j, which):
        return xall.at[core, pl.ds(j * CHUNK, CHUNK), rows_of(which), :]

    def gather_copy(j, group, which, device):
        return lambda: remote(block(j, which), block(j, which), ag_send.at[0], ag_recv.at[j, group], device)

    def gather_first(j):
        return [
            gather_copy(j, FIRST, chip, at(1, 0)),
            gather_copy(j, REST, chip, at(0, 1)),
            gather_copy(j, REST, chip, at(0, 3)),
            gather_copy(j, FIRST, chip, at(0, 2)),
        ]

    def gather_second(j):
        return [
            gather_copy(j, REST, chip_at(1, 0), at(0, 1)),
            gather_copy(j, REST, chip_at(1, 0), at(0, 3)),
            gather_copy(j, REST, chip_at(0, 2), at(1, 0)),
        ]

    def to_sibling(j):
        ref = xall.at[core, pl.ds(j * CHUNK, CHUNK)]
        return remote(ref, ref, ag_send.at[1], ag_recv.at[j, SIB], sibling)

    def got_blocks(j, group, count):
        ref = xall.at[core, pl.ds(j * CHUNK, CHUNK), pl.ds(0, count * CHIP_ROWS), :]
        remote(ref, ref, ag_send.at[0], ag_recv.at[j, group], sibling).wait_recv()

    @pl.loop(0, AHEAD)
    def _(j):
        for copy in gather_first(j):
            copy().start()

    def relay(j):
        got_blocks(j, FIRST, 2)
        for copy in gather_second(j):
            copy().start()

        @pl.when(j + AHEAD < CHUNKS)
        def _():
            for copy in gather_first(j + AHEAD):
                copy().start()

    def forward(j):
        got_blocks(j, REST, 5)
        to_sibling(j).start()

    def from_sibling(j):
        ref = xall.at[other, pl.ds(j * CHUNK, CHUNK)]
        remote(ref, ref, ag_send.at[1], ag_recv.at[j, SIB], sibling).wait_recv()

    src_row = src_ref[...].astype(F32)
    dst_row = (dst_ref[...] - graph * NODE_DEV).astype(F32)
    src_t[...] = (lax.broadcasted_iota(jnp.int32, (NODES, EDGE_DEV), 0).astype(F32) == src_row).astype(F32).astype(BF16)
    dst_t[...] = (lax.broadcasted_iota(jnp.int32, (PAD, EDGE_DEV), 0).astype(F32) == dst_row).astype(F32).astype(BF16)
    src_col = jnp.broadcast_to(src_row, (8, EDGE_DEV)).T[:, 0:1]
    dst_col = jnp.broadcast_to(dst_row, (8, EDGE_DEV)).T[:, 0:1]
    src_hot[...] = (lax.broadcasted_iota(jnp.int32, (EDGE_DEV, NODES), 1).astype(F32) == src_col).astype(F32).astype(BF16)
    dst_hot[...] = (lax.broadcasted_iota(jnp.int32, (EDGE_DEV, PAD), 1).astype(F32) == dst_col).astype(F32).astype(BF16)

    rad_t[...] = rad_ref[...].T
    for degree in range(LEVELS):
        pre = mm(rad_ref[...], wr_ref[:, degree * C : (degree + 1) * C])
        sigma = jax.nn.sigmoid(pre)
        gate[degree] = pre * sigma
        slope[degree] = sigma * (1.0 + pre * (1.0 - sigma))
        fold[degree] = jnp.zeros((EDGE_DEV, C), F32)

    relay(0)
    zeros = jnp.zeros((PAD - NODE_DEV, C), F32)
    for degree in range(LEVELS):
        begin, end = degree * degree, (degree + 1) * (degree + 1)
        stacked = jnp.concatenate([cot_ref[:, k * C : (k + 1) * C].astype(F32) for k in range(begin, end)], axis=0)
        mixed = mm_nt(stacked.astype(BF16), wd_ref[degree])
        for k in range(begin, end):
            rows = mixed[(k - begin) * NODE_DEV : (k - begin + 1) * NODE_DEV]
            rows = jnp.concatenate([rows, zeros], axis=0).astype(BF16)
            if k == 0:
                g0[...] = rows
            else:
                lane = (k - 1) % 2
                gs[(k - 1) // 2, :, lane * C : (lane + 1) * C] = rows

    query = jnp.concatenate([mm(x_ref[:, 0:C], wq_ref[...]), zeros], axis=0)
    q_high, q_low = two_parts(query)
    qe[...] = mm(dst_hot[...], q_high) + mm(dst_hot[...], q_low)
    gm0[...] = mm(dst_hot[...], g0[...])

    head_rows = lax.broadcasted_iota(jnp.int32, (C, C), 0) // (C // HEADS)
    head_cols = lax.broadcasted_iota(jnp.int32, (C, C), 1) // (C // HEADS)
    same_head = (head_rows == head_cols).astype(F32).astype(BF16)
    scale = 1.0 / math.sqrt(C // HEADS)

    def head_sum(a):
        high, low = two_parts(a)
        return mm(high, same_head) + mm(low, same_head)

    remote(x0all.at[pl.ds(1, N_GRAPH - 1)], x0all.at[pl.ds(1, N_GRAPH - 1)], x0_send.at[0], x0_recv.at[0], sibling).wait_recv()

    x0[...] = jnp.concatenate([x0all[d, 0:NODE_DEV, :].astype(F32) for d in range(N_GRAPH)], axis=0).astype(BF16)
    relay(1)
    ex0[...] = mm(src_hot[...], x0[...]).astype(BF16)
    key[...] = mm(ex0[...], wk_ref[...])
    att[...] = jax.nn.sigmoid(head_sum(qe[...] * key[...]) * scale)
    for degree in range(LEVELS):
        scaled[degree] = gate[degree] * att[...]
    ex0_float = ex0[...].astype(F32)
    fold[0] = ex0_float * gm0[...]
    forward(0)
    fwd[0] = mm(dst_t[...], (ex0_float * scaled[0]).astype(BF16))[0:NODE_DEV]

    def edges(half, t):
        pair = 2 * t + half
        k = 1 + 2 * pair
        left, right = degree_of(k), degree_of(k + 1)
        nodes = xall[half, t]
        ups = gs[pair]
        for begin in range(0, EDGE_DEV, ROW_BLOCK):
            rows = slice(begin, begin + ROW_BLOCK)
            ex = mm(src_hot[rows, :], nodes)
            gm = mm(dst_hot[rows, :], ups)
            for lane, degree in ((0, left), (1, right)):
                cols = slice(lane * C, (lane + 1) * C)
                factor = scaled[degree, rows, :]
                msg[rows, cols] = (ex[:, cols] * factor).astype(BF16)
                back[rows, cols] = (gm[:, cols] * factor).astype(BF16)
                fold[degree, rows, :] += ex[:, cols] * gm[:, cols]
        gathered = mm(dst_t[...], msg[...])
        fwd[k] = gathered[0:NODE_DEV, 0:C]
        fwd[k + 1] = gathered[0:NODE_DEV, C : 2 * C]
        part[half, t] = mm(src_t[...], back[...]).astype(BF16)

    def sum_sibling(j):
        return remote(
            part.at[other, pl.ds(j * CHUNK, CHUNK)], from_sib.at[pl.ds(j * CHUNK, CHUNK)],
            rs_send.at[0], rs_recv.at[j, 0], sibling,
        )

    def part_block(j, which):
        return part.at[core, pl.ds(j * CHUNK, CHUNK), rows_of(which), :]

    def reduce_copy(j, group, which, landing, slot, device):
        return lambda: remote(
            part_block(j, which), landing.at[slot, pl.ds(j * CHUNK, CHUNK)],
            rs_send.at[1], rs_recv.at[j, group], device,
        )

    def reduce_first(j):
        return [
            reduce_copy(j, PARTS, chip_at(1, 1), in_part, 0, at(0, 1)),
            reduce_copy(j, PARTS, chip_at(1, 3), in_part, 1, at(0, 3)),
            reduce_copy(j, PARTS, chip_at(1, 2), in_part, 2, at(1, 0)),
            reduce_copy(j, TOTALS, chip_at(0, 1), in_total, 0, at(0, 1)),
            reduce_copy(j, TOTALS, chip_at(0, 3), in_total, 1, at(0, 3)),
        ]

    def reduce_second(j):
        return [
            reduce_copy(j, TOTALS, chip_at(1, 0), in_total, 2, at(1, 0)),
            reduce_copy(j, TOTALS, chip_at(0, 2), in_total, 3, at(0, 2)),
        ]

    def last_copy(j):
        return remote(
            last.at[pl.ds(j * CHUNK, CHUNK), pl.ds(pl.multiple_of(other * NODE_DEV, 8), NODE_DEV), :],
            last_in.at[pl.ds(j * CHUNK, CHUNK)],
            rs_send.at[2], rs_recv.at[j, LAST], sibling,
        )

    def reduce_start(j):
        sum_sibling(j).wait_recv()
        for i in range(CHUNK):
            t = j * CHUNK + i
            part[core, t] = (part[core, t].astype(F32) + from_sib[t].astype(F32)).astype(BF16)
        for copy in reduce_first(j):
            copy().start()

    def reduce_next(j):
        ref = in_part.at[:, pl.ds(j * CHUNK, CHUNK)]
        remote(ref, ref, rs_send.at[1], rs_recv.at[j, PARTS], sibling).wait_recv()
        for i in range(CHUNK):
            t = j * CHUNK + i
            rows = rows_of(chip_at(1, 0))
            total = part[core, t, rows, :].astype(F32) + in_part[0, t].astype(F32) + in_part[1, t].astype(F32)
            part[core, t, rows, :] = total.astype(BF16)
            rows = rows_of(chip_at(0, 2))
            total = part[core, t, rows, :].astype(F32) + in_part[2, t].astype(F32)
            part[core, t, rows, :] = total.astype(BF16)
        for copy in reduce_second(j):
            copy().start()

    def reduce_end(j):
        ref = in_total.at[:, pl.ds(j * CHUNK, CHUNK)]
        remote(ref, ref, rs_send.at[1], rs_recv.at[j, TOTALS], sibling).wait_recv()
        for i in range(CHUNK):
            t = j * CHUNK + i
            total = part[core, t, rows_of(chip), :].astype(F32)
            for slot in range(4):
                total = total + in_total[slot, t].astype(F32)
            last[t] = total
        last_copy(j).start()

    def degree_grad(degree):
        begin, end = degree * degree, (degree + 1) * (degree + 1)
        sums = fwd[begin:end].reshape((end - begin) * NODE_DEV, C).astype(BF16)
        stacked = jnp.concatenate([cot_ref[:, k * C : (k + 1) * C].astype(F32) for k in range(begin, end)], axis=0)
        return mm_tn(sums, stacked.astype(BF16)).astype(BF16)

    def radial_grad(degree):
        g_pre = (fold[degree] * att[...] * slope[degree]).astype(BF16)
        return mm(rad_t[...], g_pre).astype(BF16)

    def dp_peer(d):
        return lax.rem(dp + d, N_DP)

    def graph_peer(d):
        return lax.rem(graph + d, N_GRAPH)

    def early_rows(half, which=0, count=1):
        return pl.ds(pl.multiple_of(half * EARLY_HALF + which * EARLY_PIECE, 16), count * EARLY_PIECE)

    def sub_rows(which):
        return pl.ds(pl.multiple_of(which * EARLY_SUB, 16), EARLY_SUB)

    def chip_peer(d):
        return lax.rem(chip + d, N_CHIP)

    def e0_copy():
        return remote(epart.at[early_rows(other, 0, N_DP)], esib, e_send.at[0], e_recv.at[0], sibling)

    def e1_copy(d):
        to = dp_peer(d)
        return remote(epart.at[early_rows(core, to)], e1_in.at[d], e_send.at[1], e_recv.at[1], (to, graph))

    def e2_copy(d):
        to = chip_peer(d)
        return remote(esum.at[sub_rows(to)], e2_in.at[d], e_send.at[2], e_recv.at[2], (dp, to * 2 + core))

    def e3_copy(d):
        mine = efull.at[sub_rows(chip)]
        return remote(mine, mine, e_send.at[3], e_recv.at[3], (dp, chip_peer(d) * 2 + core))

    def e4_copy(d):
        mine = eall.at[early_rows(core, dp)]
        return remote(mine, mine, e_send.at[4], e_recv.at[4], (dp_peer(d), graph))

    def e5_copy():
        mine = eall.at[early_rows(core, 0, N_DP)]
        return remote(mine, mine, e_send.at[5], e_recv.at[5], sibling)

    def early_first():
        for degree in range(EARLY):
            epart[2 * degree * C : (2 * degree + 1) * C] = radial_grad(degree)
            epart[(2 * degree + 1) * C : (2 * degree + 2) * C] = degree_grad(degree)
        e0_copy().start()

    def early_second():
        e0_copy().wait_recv()
        rows = early_rows(core, 0, N_DP)
        epart[rows, :] = (epart[rows, :].astype(F32) + esib[...].astype(F32)).astype(BF16)

        @pl.loop(1, N_DP)
        def _(d):
            e1_copy(d).start()

    def early_third():
        ref = e1_in.at[pl.ds(1, N_DP - 1)]
        remote(ref, ref, e_send.at[1], e_recv.at[1], sibling).wait_recv()
        total = epart[early_rows(core, dp), :].astype(F32)
        for d in range(1, N_DP):
            total = total + e1_in[d].astype(F32)
        esum[0:EARLY_PIECE] = total.astype(BF16)
        esum[EARLY_PIECE:EARLY_PAD] = jnp.zeros((EARLY_PAD - EARLY_PIECE, C), BF16)

        @pl.loop(1, N_CHIP)
        def _(d):
            e2_copy(d).start()

    def early_fourth():
        ref = e2_in.at[pl.ds(1, N_CHIP - 1)]
        remote(ref, ref, e_send.at[2], e_recv.at[2], sibling).wait_recv()
        total = esum[sub_rows(chip), :].astype(F32)
        for d in range(1, N_CHIP):
            total = total + e2_in[d].astype(F32)
        efull[sub_rows(chip), :] = total.astype(BF16)

        @pl.loop(1, N_CHIP)
        def _(d):
            e3_copy(d).start()

    def early_fifth():
        ref = e2_in.at[pl.ds(1, N_CHIP - 1)]
        remote(ref, ref, e_send.at[3], e_recv.at[3], sibling).wait_recv()
        eall[early_rows(core, dp), :] = efull[0:EARLY_PIECE]

        @pl.loop(1, N_DP)
        def _(d):
            e4_copy(d).start()

    def early_sixth():
        ref = e1_in.at[pl.ds(1, N_DP - 1)]
        remote(ref, ref, e_send.at[4], e_recv.at[4], sibling).wait_recv()
        e5_copy().start()

    @pl.loop(0, CHUNKS)
    def _(s):
        @pl.when(s + LEAD < CHUNKS)
        def _():
            relay(s + LEAD)

        @pl.when(s == CHUNKS - 3)
        def _():
            early_first()

        @pl.loop(0, 2 * CHUNK)
        def _(i):
            @pl.when(i == CHUNK)
            def _():
                @pl.when(s + 1 < CHUNKS)
                def _():
                    forward(s + 1)

                from_sibling(s)

            edges(lax.rem(core + i // CHUNK, 2), s * CHUNK + lax.rem(i, CHUNK))

        sum_sibling(s).start()

        @pl.when(s >= 1)
        def _():
            reduce_start(s - 1)

        @pl.when(s >= NEXT_LAG)
        def _():
            reduce_next(s - NEXT_LAG)

        @pl.when(s >= END_LAG)
        def _():
            reduce_end(s - END_LAG)

        @pl.when(s == CHUNKS - 3)
        def _():
            early_second()

    early_third()

    a = att[...]
    g_att = gate[0] * fold[0]
    for degree in range(1, LEVELS):
        g_att = g_att + gate[degree] * fold[degree]
    g_logit = head_sum(g_att) * a * (1.0 - a) * scale
    g_key = (g_logit * qe[...]).astype(BF16)
    q_high, q_low = two_parts(g_logit * key[...])
    q_node = (mm(dst_t[...], q_high) + mm(dst_t[...], q_low)).astype(BF16)
    wpart[0:C] = mm_tn(x_ref[:, 0:C], q_node[0:NODE_DEV]).astype(BF16)
    wpart[C : 2 * C] = mm_tn(ex0[...], g_key).astype(BF16)
    for i in range(LATE_DEGREES):
        wpart[(2 + 2 * i) * C : (3 + 2 * i) * C] = radial_grad(EARLY + i)
        wpart[(3 + 2 * i) * C : (4 + 2 * i) * C] = degree_grad(EARLY + i)

    def late_rows(which):
        return pl.ds(pl.multiple_of(which * LATE_PIECE, 16), LATE_PIECE)

    def w1_copy(d):
        to = graph_peer(d)
        return remote(wpart.at[late_rows(to)], win1.at[d], w1_send.at[0], w1_recv.at[0], (dp, to))

    @pl.loop(1, N_GRAPH)
    def _(d):
        w1_copy(d).start()

    reduce_start(CHUNKS - 1)

    back[:, 0:C] = (gm0[...] * scaled[0] + mm_nt(g_key, wk_ref[...])).astype(BF16)
    spread = mm(src_t[...], back[:, 0:C])
    pad_rows = jnp.zeros((PAD - NODE_DEV, C), F32)
    for d in range(N_GRAPH):
        p0[d] = jnp.concatenate([spread[d * NODE_DEV : (d + 1) * NODE_DEV], pad_rows], axis=0).astype(BF16)

    def p0_copy(d):
        to = lax.rem(graph + d, N_GRAPH)
        return remote(p0.at[to], in0.at[d], r0_send.at[0], r0_recv.at[0], (dp, to))

    @pl.loop(1, N_GRAPH)
    def _(d):
        p0_copy(d).start()

    early_fourth()
    for j in range(CHUNKS - NEXT_LAG, CHUNKS):
        reduce_next(j)

    for degree in range(LEVELS):
        begin, end = degree * degree, (degree + 1) * (degree + 1)
        sums = fwd[begin:end].reshape((end - begin) * NODE_DEV, C).astype(BF16)
        mixed = mm(sums, wd_ref[degree])
        for k in range(begin, end):
            rows = mixed[(k - begin) * NODE_DEV : (k - begin + 1) * NODE_DEV]
            upd_ref[:, k * C : (k + 1) * C] = (x_ref[:, k * C : (k + 1) * C].astype(F32) + rows).astype(BF16)

    remote(win1.at[pl.ds(1, N_GRAPH - 1)], win1.at[pl.ds(1, N_GRAPH - 1)], w1_send.at[0], w1_recv.at[0], sibling).wait_recv()

    total = wpart[late_rows(graph), :].astype(F32)
    for d in range(1, N_GRAPH):
        total = total + win1[d].astype(F32)
    win2[dp] = total.astype(BF16)

    def w2_copy(d):
        return remote(win2.at[dp], win2.at[dp], w2_send.at[0], w2_recv.at[0], (dp_peer(d), graph))

    @pl.loop(1, N_DP)
    def _(d):
        w2_copy(d).start()

    early_fifth()
    for j in range(CHUNKS - END_LAG, CHUNKS - 1):
        reduce_end(j)

    remote(win2.at[pl.ds(1, N_DP - 1)], win2.at[pl.ds(1, N_DP - 1)], w2_send.at[0], w2_recv.at[0], sibling).wait_recv()

    total = win2[0].astype(F32)
    for d in range(1, N_DP):
        total = total + win2[d].astype(F32)
    wall[late_rows(graph), :] = total.astype(BF16)

    def w3_copy(d):
        mine = wall.at[late_rows(graph)]
        return remote(mine, mine, w3_send.at[0], w3_recv.at[0], (dp, graph_peer(d)))

    @pl.loop(1, N_GRAPH)
    def _(d):
        w3_copy(d).start()

    early_sixth()
    reduce_end(CHUNKS - 1)

    remote(in0.at[pl.ds(1, N_GRAPH - 1)], in0.at[pl.ds(1, N_GRAPH - 1)], r0_send.at[0], r0_recv.at[0], sibling).wait_recv()

    total = p0[graph, 0:NODE_DEV, :].astype(F32)
    for d in range(1, N_GRAPH):
        total = total + in0[d, 0:NODE_DEV, :].astype(F32)
    total = total + cot_ref[:, 0:C].astype(F32) + mm_nt(q_node, wq_ref[...])[0:NODE_DEV]
    gn_ref[:, 0:C] = total.astype(BF16)

    for j in range(CHUNKS):
        last_copy(j).wait_recv()
    for t in range(HALF_PAIRS):
        own = last[t, pl.ds(pl.multiple_of(core * NODE_DEV, 8), NODE_DEV), :]
        sib = last_in[t]
        for half in range(2):
            k = 1 + 2 * (2 * t + half)
            spread = jnp.where(core == half, own, sib)
            cols = slice(k * C, (k + 2) * C)
            gn_ref[:, cols] = (cot_ref[:, cols].astype(F32) + spread).astype(BF16)

    e5_copy().wait_recv()
    ge_ref[...] = eall[...]

    remote(wall.at[pl.ds(0, (N_GRAPH - 1) * LATE_PIECE)], wall.at[pl.ds(0, (N_GRAPH - 1) * LATE_PIECE)], w3_send.at[0], w3_recv.at[0], sibling).wait_recv()

    gl_ref[...] = wall[...]

    sib_copy.wait_send()
    remote(x0all.at[pl.ds(1, N_GRAPH - 1)], x0all.at[pl.ds(1, N_GRAPH - 1)], x0_send.at[0], x0_recv.at[0], sibling).wait_send()
    remote(in0.at[pl.ds(1, N_GRAPH - 1)], in0.at[pl.ds(1, N_GRAPH - 1)], r0_send.at[0], r0_recv.at[0], sibling).wait_send()
    remote(win1.at[pl.ds(1, N_GRAPH - 1)], win1.at[pl.ds(1, N_GRAPH - 1)], w1_send.at[0], w1_recv.at[0], sibling).wait_send()
    remote(win2.at[pl.ds(1, N_DP - 1)], win2.at[pl.ds(1, N_DP - 1)], w2_send.at[0], w2_recv.at[0], sibling).wait_send()
    remote(wall.at[pl.ds(0, (N_GRAPH - 1) * LATE_PIECE)], wall.at[pl.ds(0, (N_GRAPH - 1) * LATE_PIECE)], w3_send.at[0], w3_recv.at[0], sibling).wait_send()
    remote(xall.at[0, :, pl.ds(0, 7 * CHIP_ROWS), :], xall.at[0, :, pl.ds(0, 7 * CHIP_ROWS), :], ag_send.at[0], e_recv.at[0], sibling).wait_send()
    remote(xall.at[0], xall.at[0], ag_send.at[1], e_recv.at[0], sibling).wait_send()
    remote(from_sib, from_sib, rs_send.at[0], e_recv.at[0], sibling).wait_send()
    remote(xall.at[0, :, pl.ds(0, 7 * CHIP_ROWS), :], xall.at[0, :, pl.ds(0, 7 * CHIP_ROWS), :], rs_send.at[1], e_recv.at[0], sibling).wait_send()
    remote(last_in, last_in, rs_send.at[2], e_recv.at[0], sibling).wait_send()
    remote(e1_in.at[pl.ds(1, N_DP - 1)], e1_in.at[pl.ds(1, N_DP - 1)], e_send.at[1], e_recv.at[0], sibling).wait_send()
    remote(e2_in.at[pl.ds(1, N_CHIP - 1)], e2_in.at[pl.ds(1, N_CHIP - 1)], e_send.at[2], e_recv.at[0], sibling).wait_send()
    remote(e2_in.at[pl.ds(1, N_CHIP - 1)], e2_in.at[pl.ds(1, N_CHIP - 1)], e_send.at[3], e_recv.at[0], sibling).wait_send()
    remote(e1_in.at[pl.ds(1, N_DP - 1)], e1_in.at[pl.ds(1, N_DP - 1)], e_send.at[4], e_recv.at[0], sibling).wait_send()
    remote(esib, esib, e_send.at[0], e_recv.at[0], sibling).wait_send()
    remote(esib, esib, e_send.at[5], e_recv.at[0], sibling).wait_send()


def write_kernel(u_ref, n_ref, ge_ref, gl_ref, upd_ref, gn_ref, gq_ref, gk_ref, gr_ref, gd_ref):
    upd_ref[...] = u_ref[...]
    gn_ref[...] = n_ref[...]
    for degree in range(EARLY):
        gr_ref[:, degree * C : (degree + 1) * C] = ge_ref[2 * degree * C : (2 * degree + 1) * C].astype(F32)
        gd_ref[degree] = ge_ref[(2 * degree + 1) * C : (2 * degree + 2) * C].astype(F32)
    gq_ref[...] = gl_ref[0:C].astype(F32)
    gk_ref[...] = gl_ref[C : 2 * C].astype(F32)
    for i in range(LATE_DEGREES):
        degree = EARLY + i
        gr_ref[:, degree * C : (degree + 1) * C] = gl_ref[(2 + 2 * i) * C : (3 + 2 * i) * C].astype(F32)
        gd_ref[degree] = gl_ref[(3 + 2 * i) * C : (4 + 2 * i) * C].astype(F32)


def on_device(node_feat, radial, src_node, dst_node, w_query, w_key, w_radial, w_degree, cotangent):
    vmem = pl.BlockSpec(memory_space=pltpu.VMEM)
    dma = pltpu.SemaphoreType.DMA
    width = node_feat.shape[2]
    scratch = [
        pltpu.VMEM((2, HALF_PAIRS, PAD, 2 * C), BF16),
        pltpu.VMEM((HALF_PAIRS, PAD, 2 * C), BF16),
        pltpu.VMEM((2, HALF_PAIRS, NODES, 2 * C), BF16),
        pltpu.VMEM((N_GRAPH, PAD, C), BF16),
        pltpu.VMEM((NODES, C), BF16),
        pltpu.VMEM((EDGE_DEV, NODES), BF16),
        pltpu.VMEM((NODES, EDGE_DEV), BF16),
        pltpu.VMEM((EDGE_DEV, PAD), BF16),
        pltpu.VMEM((PAD, EDGE_DEV), BF16),
        pltpu.VMEM((2 * HALF_PAIRS, PAD, 2 * C), BF16),
        pltpu.VMEM((PAD, C), BF16),
        pltpu.VMEM((LEVELS, EDGE_DEV, C), F32),
        pltpu.VMEM((LEVELS, EDGE_DEV, C), F32),
        pltpu.VMEM((LEVELS, EDGE_DEV, C), F32),
        pltpu.VMEM((LEVELS, EDGE_DEV, C), F32),
        pltpu.VMEM((LEVELS * LEVELS, NODE_DEV, C), F32),
        pltpu.VMEM((EDGE_DEV, 2 * C), BF16),
        pltpu.VMEM((EDGE_DEV, 2 * C), BF16),
        pltpu.VMEM((2, HALF_PAIRS, NODES, 2 * C), BF16),
        pltpu.VMEM((HALF_PAIRS, NODES, 2 * C), BF16),
        pltpu.VMEM((3, HALF_PAIRS, CHIP_ROWS, 2 * C), BF16),
        pltpu.VMEM((4, HALF_PAIRS, CHIP_ROWS, 2 * C), BF16),
        pltpu.VMEM((HALF_PAIRS, CHIP_ROWS, 2 * C), F32),
        pltpu.VMEM((HALF_PAIRS, NODE_DEV, 2 * C), F32),
        pltpu.VMEM((N_GRAPH, PAD, C), BF16),
        pltpu.VMEM((N_GRAPH, PAD, C), BF16),
        pltpu.VMEM((LATE_ROWS, C), BF16),
        pltpu.VMEM((N_GRAPH, LATE_PIECE, C), BF16),
        pltpu.VMEM((N_DP, LATE_PIECE, C), BF16),
        pltpu.VMEM((LATE_ROWS, C), BF16),
        pltpu.VMEM((2 * EARLY_HALF, C), BF16),
        pltpu.VMEM((EARLY_HALF, C), BF16),
        pltpu.VMEM((N_DP, EARLY_PIECE, C), BF16),
        pltpu.VMEM((EARLY_PAD, C), BF16),
        pltpu.VMEM((N_CHIP, EARLY_SUB, C), BF16),
        pltpu.VMEM((EARLY_PAD, C), BF16),
        pltpu.VMEM((2 * EARLY_HALF, C), BF16),
        pltpu.VMEM((EDGE_DEV, C), F32),
        pltpu.VMEM((EDGE_DEV, C), F32),
        pltpu.VMEM((EDGE_DEV, C), F32),
        pltpu.VMEM((EDGE_DEV, C), BF16),
        pltpu.VMEM((EDGE_DEV, C), F32),
        pltpu.VMEM((C, EDGE_DEV), BF16),
        dma((2,)),
        dma((1,)),
        dma((1,)),
        dma((2,)),
        dma((CHUNKS, 3)),
        dma((3,)),
        dma((CHUNKS, 4)),
        dma((1,)),
        dma((1,)),
        dma((1,)),
        dma((1,)),
        dma((1,)),
        dma((1,)),
        dma((1,)),
        dma((1,)),
        dma((6,)),
        dma((6,)),
    ]
    updated, grad_node, early, late = pl.pallas_call(
        kernel,
        out_shape=(
            jax.ShapeDtypeStruct((NODE_DEV, width), BF16),
            jax.ShapeDtypeStruct((NODE_DEV, width), BF16),
            jax.ShapeDtypeStruct((2 * EARLY * C, C), BF16),
            jax.ShapeDtypeStruct((LATE_ROWS, C), BF16),
        ),
        in_specs=[vmem] * 9,
        out_specs=(vmem,) * 4,
        scratch_shapes=scratch,
        compiler_params=pltpu.CompilerParams(
            collective_id=0, has_side_effects=True, vmem_limit_bytes=60 << 20
        ),
    )(node_feat[0], radial[0], src_node, dst_node, w_query, w_key, w_radial, w_degree, cotangent[0])
    updated, grad_node, grad_query, grad_key, grad_radial, grad_degree = pl.pallas_call(
        write_kernel,
        out_shape=(
            jax.ShapeDtypeStruct((NODE_DEV, width), BF16),
            jax.ShapeDtypeStruct((NODE_DEV, width), BF16),
            jax.ShapeDtypeStruct((C, C), F32),
            jax.ShapeDtypeStruct((C, C), F32),
            jax.ShapeDtypeStruct((C, LEVELS * C), F32),
            jax.ShapeDtypeStruct((LEVELS, C, C), F32),
        ),
        in_specs=[vmem] * 4,
        out_specs=(vmem,) * 6,
        compiler_params=pltpu.CompilerParams(vmem_limit_bytes=60 << 20),
    )(updated, grad_node, early, late)
    return (updated[None], grad_node[None], grad_query, grad_key, grad_radial, grad_degree)


def solution(mesh):
    return jax.shard_map(
        on_device,
        mesh=mesh,
        in_specs=(
            P("dp", "graph", None),
            P("dp", "graph", None),
            P("dp", "graph"),
            P("dp", "graph"),
            P(),
            P(),
            P(),
            P(),
            P("dp", "graph", None),
        ),
        out_specs=(P("dp", "graph", None), P("dp", "graph", None), P(), P(), P(), P()),
        check_vma=False,
    )
```

```python
import functools
import math

import jax
import jax.numpy as jnp
from jax import lax
from jax.experimental import pallas as pl
from jax.experimental.pallas import tpu as pltpu
from jax.sharding import PartitionSpec as P

HEADS = 8
C = 128
LEVELS = 7
NODE_DEV = 24
PAD = 32
EDGE_DEV = 768
NODES = 384
CHIP_ROWS = 48
N_GRAPH = 16
N_DP = 8
HALF_PAIRS = 12
CHUNK = 2
CHUNKS = HALF_PAIRS // CHUNK
ROW_BLOCK = 128
AHEAD = 2
LEAD = 2
NEXT_LAG = 2
END_LAG = 4
EARLY = 5
EARLY_HALF = EARLY * C
EARLY_PIECE = EARLY_HALF // N_DP
EARLY_PAD = 128
N_CHIP = N_GRAPH // 2
EARLY_SUB = EARLY_PAD // N_CHIP
LATE_DEGREES = LEVELS - EARLY
LATE_ROWS = (2 + 2 * LATE_DEGREES) * C
LATE_PIECE = LATE_ROWS // N_GRAPH
MESH = pl.DeviceIdType.MESH
F32 = jnp.float32
BF16 = jnp.bfloat16

FIRST, REST, SIB = range(3)
PARTS, TOTALS, LAST = range(1, 4)


def mm(a, b):
    return jnp.dot(a, b, preferred_element_type=F32)


def mm_nt(a, b):
    return lax.dot_general(a, b, (((1,), (1,)), ((), ())), preferred_element_type=F32)


def mm_tn(a, b):
    return lax.dot_general(a, b, (((0,), (0,)), ((), ())), preferred_element_type=F32)


def two_parts(a):
    high = a.astype(BF16)
    return high, (a - high.astype(F32)).astype(BF16)


def degree_of(k):
    total = 0
    for degree in range(1, LEVELS):
        total = total + (k + 64 - degree * degree) // 64
    return total


def columns(k, count=1):
    return pl.ds(pl.multiple_of(k * C, C), count * C)


def kernel(
    x_ref, rad_ref, src_ref, dst_ref, wq_ref, wk_ref, wr_ref, wd_ref, cot_ref,
    upd_ref, gn_ref, ge_ref, gl_ref,
    xs, sibx, xall, x0all, x0, src_hot, src_t, dst_hot, dst_t,
    gs, g0, gate, slope, scaled, fold, fwd, msg, back,
    part, from_sib, in_part, in_total, last, last_in, p0, in0,
    wpart, win1, win2, wall, epart, esib, e1_in, esum, e2_in, efull, eall,
    qe, key, att, ex0, gm0, rad_t,
    sib_sems, x0_send, x0_recv, ag_send, ag_recv, rs_send, rs_recv,
    r0_send, r0_recv, w1_send, w1_recv, w2_send, w2_recv, w3_send, w3_recv,
    e_send, e_recv,
):
    dp = lax.axis_index("dp")
    graph = lax.axis_index("graph")
    core = lax.rem(graph, 2)
    chip = graph // 2
    x_hi = chip // 4
    y = lax.rem(chip, 4)
    other = 1 - core

    def chip_at(dx, dy):
        return lax.rem(x_hi + dx, 2) * 4 + lax.rem(y + dy, 4)

    def at(dx, dy):
        return (dp, chip_at(dx, dy) * 2 + core)

    sibling = (dp, chip * 2 + other)

    def rows_of(which):
        return pl.ds(pl.multiple_of(which * CHIP_ROWS, 16), CHIP_ROWS)

    def remote(src, dst, send, recv, device):
        return pltpu.make_async_remote_copy(
            src_ref=src, dst_ref=dst, send_sem=send, recv_sem=recv,
            device_id=device, device_id_type=MESH,
        )

    barrier = pltpu.get_barrier_semaphore()

    @pl.loop(1, N_GRAPH)
    def _(d):
        pl.semaphore_signal(
            barrier, inc=1, device_id=(dp, lax.rem(graph + d, N_GRAPH)), device_id_type=MESH
        )

    @pl.loop(1, N_DP)
    def _(d):
        pl.semaphore_signal(
            barrier, inc=1, device_id=(lax.rem(dp + d, N_DP), graph), device_id_type=MESH
        )

    for pair in range(2 * HALF_PAIRS):
        xs[pair % 2, pair // 2, 0:NODE_DEV, :] = x_ref[:, (1 + 2 * pair) * C : (3 + 2 * pair) * C]
        xs[pair % 2, pair // 2, NODE_DEV:PAD, :] = jnp.zeros((PAD - NODE_DEV, 2 * C), BF16)
    x0all[graph, 0:NODE_DEV, :] = x_ref[:, 0:C]
    x0all[graph, NODE_DEV:PAD, :] = jnp.zeros((PAD - NODE_DEV, C), BF16)

    src_row = src_ref[...].astype(F32)
    dst_row = (dst_ref[...] - graph * NODE_DEV).astype(F32)
    src_t[...] = (lax.broadcasted_iota(jnp.int32, (NODES, EDGE_DEV), 0).astype(F32) == src_row).astype(F32).astype(BF16)
    dst_t[...] = (lax.broadcasted_iota(jnp.int32, (PAD, EDGE_DEV), 0).astype(F32) == dst_row).astype(F32).astype(BF16)
    src_col = jnp.broadcast_to(src_row, (8, EDGE_DEV)).T[:, 0:1]
    dst_col = jnp.broadcast_to(dst_row, (8, EDGE_DEV)).T[:, 0:1]
    src_hot[...] = (lax.broadcasted_iota(jnp.int32, (EDGE_DEV, NODES), 1).astype(F32) == src_col).astype(F32).astype(BF16)
    dst_hot[...] = (lax.broadcasted_iota(jnp.int32, (EDGE_DEV, PAD), 1).astype(F32) == dst_col).astype(F32).astype(BF16)

    pl.semaphore_wait(barrier, N_GRAPH - 1 + N_DP - 1)

    sib_copy = remote(xs.at[other], sibx, sib_sems.at[0], sib_sems.at[1], sibling)
    sib_copy.start()

    def x0_copy(d):
        return remote(
            x0all.at[graph], x0all.at[graph], x0_send.at[0], x0_recv.at[0],
            (dp, lax.rem(graph + d, N_GRAPH)),
        )

    @pl.loop(1, N_GRAPH)
    def _(d):
        x0_copy(d).start()

    sib_copy.wait_recv()
    mine = xs[core, :, 0:NODE_DEV, :].astype(F32)
    theirs = sibx[:, 0:NODE_DEV, :].astype(F32)
    first = jnp.where(core == 0, mine, theirs)
    second = jnp.where(core == 0, theirs, mine)
    xall[core, :, rows_of(chip), :] = jnp.concatenate([first, second], axis=1).astype(BF16)

    def block(j, which):
        return xall.at[core, pl.ds(j * CHUNK, CHUNK), rows_of(which), :]

    def gather_copy(j, group, which, device):
        return lambda: remote(block(j, which), block(j, which), ag_send.at[0], ag_recv.at[j, group], device)

    def gather_first(j):
        return [
            gather_copy(j, FIRST, chip, at(1, 0)),
            gather_copy(j, REST, chip, at(0, 1)),
            gather_copy(j, REST, chip, at(0, 3)),
            gather_copy(j, FIRST, chip, at(0, 2)),
        ]

    def gather_second(j):
        return [
            gather_copy(j, REST, chip_at(1, 0), at(0, 1)),
            gather_copy(j, REST, chip_at(1, 0), at(0, 3)),
            gather_copy(j, REST, chip_at(0, 2), at(1, 0)),
        ]

    def to_sibling(j):
        ref = xall.at[core, pl.ds(j * CHUNK, CHUNK)]
        return remote(ref, ref, ag_send.at[1], ag_recv.at[j, SIB], sibling)

    def got_blocks(j, group, count):
        ref = xall.at[core, pl.ds(j * CHUNK, CHUNK), pl.ds(0, count * CHIP_ROWS), :]
        remote(ref, ref, ag_send.at[0], ag_recv.at[j, group], sibling).wait_recv()

    @pl.loop(0, AHEAD)
    def _(j):
        for copy in gather_first(j):
            copy().start()

    def relay(j):
        got_blocks(j, FIRST, 2)
        for copy in gather_second(j):
            copy().start()

        @pl.when(j + AHEAD < CHUNKS)
        def _():
            for copy in gather_first(j + AHEAD):
                copy().start()

    def forward(j):
        got_blocks(j, REST, 5)
        to_sibling(j).start()

    def from_sibling(j):
        ref = xall.at[other, pl.ds(j * CHUNK, CHUNK)]
        remote(ref, ref, ag_send.at[1], ag_recv.at[j, SIB], sibling).wait_recv()

    rad_t[...] = rad_ref[...].T
    for degree in range(LEVELS):
        pre = mm(rad_ref[...], wr_ref[:, degree * C : (degree + 1) * C])
        sigma = jax.nn.sigmoid(pre)
        gate[degree] = pre * sigma
        slope[degree] = sigma * (1.0 + pre * (1.0 - sigma))
        fold[degree] = jnp.zeros((EDGE_DEV, C), F32)

    relay(0)
    zeros = jnp.zeros((PAD - NODE_DEV, C), F32)
    for degree in range(LEVELS):
        begin, end = degree * degree, (degree + 1) * (degree + 1)
        stacked = jnp.concatenate([cot_ref[:, k * C : (k + 1) * C].astype(F32) for k in range(begin, end)], axis=0)
        mixed = mm_nt(stacked.astype(BF16), wd_ref[degree])
        for k in range(begin, end):
            rows = mixed[(k - begin) * NODE_DEV : (k - begin + 1) * NODE_DEV]
            rows = jnp.concatenate([rows, zeros], axis=0).astype(BF16)
            if k == 0:
                g0[...] = rows
            else:
                lane = (k - 1) % 2
                gs[(k - 1) // 2, :, lane * C : (lane + 1) * C] = rows

    query = jnp.concatenate([mm(x_ref[:, 0:C], wq_ref[...]), zeros], axis=0)
    q_high, q_low = two_parts(query)
    qe[...] = mm(dst_hot[...], q_high) + mm(dst_hot[...], q_low)
    gm0[...] = mm(dst_hot[...], g0[...])

    head_rows = lax.broadcasted_iota(jnp.int32, (C, C), 0) // (C // HEADS)
    head_cols = lax.broadcasted_iota(jnp.int32, (C, C), 1) // (C // HEADS)
    same_head = (head_rows == head_cols).astype(F32).astype(BF16)
    scale = 1.0 / math.sqrt(C // HEADS)

    def head_sum(a):
        high, low = two_parts(a)
        return mm(high, same_head) + mm(low, same_head)

    remote(x0all.at[pl.ds(1, N_GRAPH - 1)], x0all.at[pl.ds(1, N_GRAPH - 1)], x0_send.at[0], x0_recv.at[0], sibling).wait_recv()

    x0[...] = jnp.concatenate([x0all[d, 0:NODE_DEV, :].astype(F32) for d in range(N_GRAPH)], axis=0).astype(BF16)
    relay(1)
    ex0[...] = mm(src_hot[...], x0[...]).astype(BF16)
    key[...] = mm(ex0[...], wk_ref[...])
    att[...] = jax.nn.sigmoid(head_sum(qe[...] * key[...]) * scale)
    for degree in range(LEVELS):
        scaled[degree] = gate[degree] * att[...]
    ex0_float = ex0[...].astype(F32)
    fold[0] = ex0_float * gm0[...]
    forward(0)
    fwd[0] = mm(dst_t[...], (ex0_float * scaled[0]).astype(BF16))[0:NODE_DEV]

    def edges(half, t):
        pair = 2 * t + half
        k = 1 + 2 * pair
        left, right = degree_of(k), degree_of(k + 1)
        nodes = xall[half, t]
        ups = gs[pair]
        for begin in range(0, EDGE_DEV, ROW_BLOCK):
            rows = slice(begin, begin + ROW_BLOCK)
            ex = mm(src_hot[rows, :], nodes)
            gm = mm(dst_hot[rows, :], ups)
            for lane, degree in ((0, left), (1, right)):
                cols = slice(lane * C, (lane + 1) * C)
                factor = scaled[degree, rows, :]
                msg[rows, cols] = (ex[:, cols] * factor).astype(BF16)
                back[rows, cols] = (gm[:, cols] * factor).astype(BF16)
                fold[degree, rows, :] += ex[:, cols] * gm[:, cols]
        gathered = mm(dst_t[...], msg[...])
        fwd[k] = gathered[0:NODE_DEV, 0:C]
        fwd[k + 1] = gathered[0:NODE_DEV, C : 2 * C]
        part[half, t] = mm(src_t[...], back[...]).astype(BF16)

    def sum_sibling(j):
        return remote(
            part.at[other, pl.ds(j * CHUNK, CHUNK)], from_sib.at[pl.ds(j * CHUNK, CHUNK)],
            rs_send.at[0], rs_recv.at[j, 0], sibling,
        )

    def part_block(j, which):
        return part.at[core, pl.ds(j * CHUNK, CHUNK), rows_of(which), :]

    def reduce_copy(j, group, which, landing, slot, device):
        return lambda: remote(
            part_block(j, which), landing.at[slot, pl.ds(j * CHUNK, CHUNK)],
            rs_send.at[1], rs_recv.at[j, group], device,
        )

    def reduce_first(j):
        return [
            reduce_copy(j, PARTS, chip_at(1, 1), in_part, 0, at(0, 1)),
            reduce_copy(j, PARTS, chip_at(1, 3), in_part, 1, at(0, 3)),
            reduce_copy(j, PARTS, chip_at(1, 2), in_part, 2, at(1, 0)),
            reduce_copy(j, TOTALS, chip_at(0, 1), in_total, 0, at(0, 1)),
            reduce_copy(j, TOTALS, chip_at(0, 3), in_total, 1, at(0, 3)),
        ]

    def reduce_second(j):
        return [
            reduce_copy(j, TOTALS, chip_at(1, 0), in_total, 2, at(1, 0)),
            reduce_copy(j, TOTALS, chip_at(0, 2), in_total, 3, at(0, 2)),
        ]

    def last_copy(j):
        return remote(
            last.at[pl.ds(j * CHUNK, CHUNK), pl.ds(pl.multiple_of(other * NODE_DEV, 8), NODE_DEV), :],
            last_in.at[pl.ds(j * CHUNK, CHUNK)],
            rs_send.at[2], rs_recv.at[j, LAST], sibling,
        )

    def reduce_start(j):
        sum_sibling(j).wait_recv()
        for i in range(CHUNK):
            t = j * CHUNK + i
            part[core, t] = (part[core, t].astype(F32) + from_sib[t].astype(F32)).astype(BF16)
        for copy in reduce_first(j):
            copy().start()

    def reduce_next(j):
        ref = in_part.at[:, pl.ds(j * CHUNK, CHUNK)]
        remote(ref, ref, rs_send.at[1], rs_recv.at[j, PARTS], sibling).wait_recv()
        for i in range(CHUNK):
            t = j * CHUNK + i
            rows = rows_of(chip_at(1, 0))
            total = part[core, t, rows, :].astype(F32) + in_part[0, t].astype(F32) + in_part[1, t].astype(F32)
            part[core, t, rows, :] = total.astype(BF16)
            rows = rows_of(chip_at(0, 2))
            total = part[core, t, rows, :].astype(F32) + in_part[2, t].astype(F32)
            part[core, t, rows, :] = total.astype(BF16)
        for copy in reduce_second(j):
            copy().start()

    def reduce_end(j):
        ref = in_total.at[:, pl.ds(j * CHUNK, CHUNK)]
        remote(ref, ref, rs_send.at[1], rs_recv.at[j, TOTALS], sibling).wait_recv()
        for i in range(CHUNK):
            t = j * CHUNK + i
            total = part[core, t, rows_of(chip), :].astype(F32)
            for slot in range(4):
                total = total + in_total[slot, t].astype(F32)
            last[t] = total
        last_copy(j).start()

    def degree_grad(degree):
        begin, end = degree * degree, (degree + 1) * (degree + 1)
        sums = fwd[begin:end].reshape((end - begin) * NODE_DEV, C).astype(BF16)
        stacked = jnp.concatenate([cot_ref[:, k * C : (k + 1) * C].astype(F32) for k in range(begin, end)], axis=0)
        return mm_tn(sums, stacked.astype(BF16)).astype(BF16)

    def radial_grad(degree):
        g_pre = (fold[degree] * att[...] * slope[degree]).astype(BF16)
        return mm(rad_t[...], g_pre).astype(BF16)

    def dp_peer(d):
        return lax.rem(dp + d, N_DP)

    def graph_peer(d):
        return lax.rem(graph + d, N_GRAPH)

    def early_rows(half, which=0, count=1):
        return pl.ds(pl.multiple_of(half * EARLY_HALF + which * EARLY_PIECE, 16), count * EARLY_PIECE)

    def sub_rows(which):
        return pl.ds(pl.multiple_of(which * EARLY_SUB, 16), EARLY_SUB)

    def chip_peer(d):
        return lax.rem(chip + d, N_CHIP)

    def e0_copy():
        return remote(epart.at[early_rows(other, 0, N_DP)], esib, e_send.at[0], e_recv.at[0], sibling)

    def e1_copy(d):
        to = dp_peer(d)
        return remote(epart.at[early_rows(core, to)], e1_in.at[d], e_send.at[1], e_recv.at[1], (to, graph))

    def e2_copy(d):
        to = chip_peer(d)
        return remote(esum.at[sub_rows(to)], e2_in.at[d], e_send.at[2], e_recv.at[2], (dp, to * 2 + core))

    def e3_copy(d):
        mine = efull.at[sub_rows(chip)]
        return remote(mine, mine, e_send.at[3], e_recv.at[3], (dp, chip_peer(d) * 2 + core))

    def e4_copy(d):
        mine = eall.at[early_rows(core, dp)]
        return remote(mine, mine, e_send.at[4], e_recv.at[4], (dp_peer(d), graph))

    def e5_copy():
        mine = eall.at[early_rows(core, 0, N_DP)]
        return remote(mine, mine, e_send.at[5], e_recv.at[5], sibling)

    def early_first():
        for degree in range(EARLY):
            epart[2 * degree * C : (2 * degree + 1) * C] = radial_grad(degree)
            epart[(2 * degree + 1) * C : (2 * degree + 2) * C] = degree_grad(degree)
        e0_copy().start()

    def early_second():
        e0_copy().wait_recv()
        rows = early_rows(core, 0, N_DP)
        epart[rows, :] = (epart[rows, :].astype(F32) + esib[...].astype(F32)).astype(BF16)

        @pl.loop(1, N_DP)
        def _(d):
            e1_copy(d).start()

    def early_third():
        ref = e1_in.at[pl.ds(1, N_DP - 1)]
        remote(ref, ref, e_send.at[1], e_recv.at[1], sibling).wait_recv()
        total = epart[early_rows(core, dp), :].astype(F32)
        for d in range(1, N_DP):
            total = total + e1_in[d].astype(F32)
        esum[0:EARLY_PIECE] = total.astype(BF16)
        esum[EARLY_PIECE:EARLY_PAD] = jnp.zeros((EARLY_PAD - EARLY_PIECE, C), BF16)

        @pl.loop(1, N_CHIP)
        def _(d):
            e2_copy(d).start()

    def early_fourth():
        ref = e2_in.at[pl.ds(1, N_CHIP - 1)]
        remote(ref, ref, e_send.at[2], e_recv.at[2], sibling).wait_recv()
        total = esum[sub_rows(chip), :].astype(F32)
        for d in range(1, N_CHIP):
            total = total + e2_in[d].astype(F32)
        efull[sub_rows(chip), :] = total.astype(BF16)

        @pl.loop(1, N_CHIP)
        def _(d):
            e3_copy(d).start()

    def early_fifth():
        ref = e2_in.at[pl.ds(1, N_CHIP - 1)]
        remote(ref, ref, e_send.at[3], e_recv.at[3], sibling).wait_recv()
        eall[early_rows(core, dp), :] = efull[0:EARLY_PIECE]

        @pl.loop(1, N_DP)
        def _(d):
            e4_copy(d).start()

    def early_sixth():
        ref = e1_in.at[pl.ds(1, N_DP - 1)]
        remote(ref, ref, e_send.at[4], e_recv.at[4], sibling).wait_recv()
        e5_copy().start()

    @pl.loop(0, CHUNKS)
    def _(s):
        @pl.when(s + LEAD < CHUNKS)
        def _():
            relay(s + LEAD)

        @pl.when(s == CHUNKS - 3)
        def _():
            early_first()

        @pl.loop(0, 2 * CHUNK)
        def _(i):
            @pl.when(i == CHUNK)
            def _():
                @pl.when(s + 1 < CHUNKS)
                def _():
                    forward(s + 1)

                from_sibling(s)

            edges(lax.rem(core + i // CHUNK, 2), s * CHUNK + lax.rem(i, CHUNK))

        sum_sibling(s).start()

        @pl.when(s >= 1)
        def _():
            reduce_start(s - 1)

        @pl.when(s >= NEXT_LAG)
        def _():
            reduce_next(s - NEXT_LAG)

        @pl.when(s >= END_LAG)
        def _():
            reduce_end(s - END_LAG)

        @pl.when(s == CHUNKS - 3)
        def _():
            early_second()

    early_third()

    a = att[...]
    g_att = gate[0] * fold[0]
    for degree in range(1, LEVELS):
        g_att = g_att + gate[degree] * fold[degree]
    g_logit = head_sum(g_att) * a * (1.0 - a) * scale
    g_key = (g_logit * qe[...]).astype(BF16)
    q_high, q_low = two_parts(g_logit * key[...])
    q_node = (mm(dst_t[...], q_high) + mm(dst_t[...], q_low)).astype(BF16)
    wpart[0:C] = mm_tn(x_ref[:, 0:C], q_node[0:NODE_DEV]).astype(BF16)
    wpart[C : 2 * C] = mm_tn(ex0[...], g_key).astype(BF16)
    for i in range(LATE_DEGREES):
        wpart[(2 + 2 * i) * C : (3 + 2 * i) * C] = radial_grad(EARLY + i)
        wpart[(3 + 2 * i) * C : (4 + 2 * i) * C] = degree_grad(EARLY + i)

    def late_rows(which):
        return pl.ds(pl.multiple_of(which * LATE_PIECE, 16), LATE_PIECE)

    def w1_copy(d):
        to = graph_peer(d)
        return remote(wpart.at[late_rows(to)], win1.at[d], w1_send.at[0], w1_recv.at[0], (dp, to))

    @pl.loop(1, N_GRAPH)
    def _(d):
        w1_copy(d).start()

    reduce_start(CHUNKS - 1)

    back[:, 0:C] = (gm0[...] * scaled[0] + mm_nt(g_key, wk_ref[...])).astype(BF16)
    spread = mm(src_t[...], back[:, 0:C])
    pad_rows = jnp.zeros((PAD - NODE_DEV, C), F32)
    for d in range(N_GRAPH):
        p0[d] = jnp.concatenate([spread[d * NODE_DEV : (d + 1) * NODE_DEV], pad_rows], axis=0).astype(BF16)

    def p0_copy(d):
        to = lax.rem(graph + d, N_GRAPH)
        return remote(p0.at[to], in0.at[d], r0_send.at[0], r0_recv.at[0], (dp, to))

    @pl.loop(1, N_GRAPH)
    def _(d):
        p0_copy(d).start()

    early_fourth()
    for j in range(CHUNKS - NEXT_LAG, CHUNKS):
        reduce_next(j)

    remote(win1.at[pl.ds(1, N_GRAPH - 1)], win1.at[pl.ds(1, N_GRAPH - 1)], w1_send.at[0], w1_recv.at[0], sibling).wait_recv()

    total = wpart[late_rows(graph), :].astype(F32)
    for d in range(1, N_GRAPH):
        total = total + win1[d].astype(F32)
    win2[dp] = total.astype(BF16)

    def w2_copy(d):
        return remote(win2.at[dp], win2.at[dp], w2_send.at[0], w2_recv.at[0], (dp_peer(d), graph))

    @pl.loop(1, N_DP)
    def _(d):
        w2_copy(d).start()

    for degree in range(LEVELS):
        begin, end = degree * degree, (degree + 1) * (degree + 1)
        sums = fwd[begin:end].reshape((end - begin) * NODE_DEV, C).astype(BF16)
        mixed = mm(sums, wd_ref[degree])
        for k in range(begin, end):
            rows = mixed[(k - begin) * NODE_DEV : (k - begin + 1) * NODE_DEV]
            upd_ref[:, k * C : (k + 1) * C] = (x_ref[:, k * C : (k + 1) * C].astype(F32) + rows).astype(BF16)

    early_fifth()
    for j in range(CHUNKS - END_LAG, CHUNKS - 1):
        reduce_end(j)

    remote(win2.at[pl.ds(1, N_DP - 1)], win2.at[pl.ds(1, N_DP - 1)], w2_send.at[0], w2_recv.at[0], sibling).wait_recv()

    total = win2[0].astype(F32)
    for d in range(1, N_DP):
        total = total + win2[d].astype(F32)
    wall[late_rows(graph), :] = total.astype(BF16)

    def w3_copy(d):
        mine = wall.at[late_rows(graph)]
        return remote(mine, mine, w3_send.at[0], w3_recv.at[0], (dp, graph_peer(d)))

    @pl.loop(1, N_GRAPH)
    def _(d):
        w3_copy(d).start()

    early_sixth()
    reduce_end(CHUNKS - 1)

    remote(in0.at[pl.ds(1, N_GRAPH - 1)], in0.at[pl.ds(1, N_GRAPH - 1)], r0_send.at[0], r0_recv.at[0], sibling).wait_recv()

    total = p0[graph, 0:NODE_DEV, :].astype(F32)
    for d in range(1, N_GRAPH):
        total = total + in0[d, 0:NODE_DEV, :].astype(F32)
    total = total + cot_ref[:, 0:C].astype(F32) + mm_nt(q_node, wq_ref[...])[0:NODE_DEV]
    gn_ref[:, 0:C] = total.astype(BF16)

    for j in range(CHUNKS):
        last_copy(j).wait_recv()
    for t in range(HALF_PAIRS):
        own = last[t, pl.ds(pl.multiple_of(core * NODE_DEV, 8), NODE_DEV), :]
        sib = last_in[t]
        for half in range(2):
            k = 1 + 2 * (2 * t + half)
            spread = jnp.where(core == half, own, sib)
            cols = slice(k * C, (k + 2) * C)
            gn_ref[:, cols] = (cot_ref[:, cols].astype(F32) + spread).astype(BF16)

    e5_copy().wait_recv()
    ge_ref[...] = eall[...]

    remote(wall.at[pl.ds(0, (N_GRAPH - 1) * LATE_PIECE)], wall.at[pl.ds(0, (N_GRAPH - 1) * LATE_PIECE)], w3_send.at[0], w3_recv.at[0], sibling).wait_recv()

    gl_ref[...] = wall[...]

    sib_copy.wait_send()
    remote(x0all.at[pl.ds(1, N_GRAPH - 1)], x0all.at[pl.ds(1, N_GRAPH - 1)], x0_send.at[0], x0_recv.at[0], sibling).wait_send()
    remote(in0.at[pl.ds(1, N_GRAPH - 1)], in0.at[pl.ds(1, N_GRAPH - 1)], r0_send.at[0], r0_recv.at[0], sibling).wait_send()
    remote(win1.at[pl.ds(1, N_GRAPH - 1)], win1.at[pl.ds(1, N_GRAPH - 1)], w1_send.at[0], w1_recv.at[0], sibling).wait_send()
    remote(win2.at[pl.ds(1, N_DP - 1)], win2.at[pl.ds(1, N_DP - 1)], w2_send.at[0], w2_recv.at[0], sibling).wait_send()
    remote(wall.at[pl.ds(0, (N_GRAPH - 1) * LATE_PIECE)], wall.at[pl.ds(0, (N_GRAPH - 1) * LATE_PIECE)], w3_send.at[0], w3_recv.at[0], sibling).wait_send()
    remote(xall.at[0, :, pl.ds(0, 7 * CHIP_ROWS), :], xall.at[0, :, pl.ds(0, 7 * CHIP_ROWS), :], ag_send.at[0], e_recv.at[0], sibling).wait_send()
    remote(xall.at[0], xall.at[0], ag_send.at[1], e_recv.at[0], sibling).wait_send()
    remote(from_sib, from_sib, rs_send.at[0], e_recv.at[0], sibling).wait_send()
    remote(xall.at[0, :, pl.ds(0, 7 * CHIP_ROWS), :], xall.at[0, :, pl.ds(0, 7 * CHIP_ROWS), :], rs_send.at[1], e_recv.at[0], sibling).wait_send()
    remote(last_in, last_in, rs_send.at[2], e_recv.at[0], sibling).wait_send()
    remote(e1_in.at[pl.ds(1, N_DP - 1)], e1_in.at[pl.ds(1, N_DP - 1)], e_send.at[1], e_recv.at[0], sibling).wait_send()
    remote(e2_in.at[pl.ds(1, N_CHIP - 1)], e2_in.at[pl.ds(1, N_CHIP - 1)], e_send.at[2], e_recv.at[0], sibling).wait_send()
    remote(e2_in.at[pl.ds(1, N_CHIP - 1)], e2_in.at[pl.ds(1, N_CHIP - 1)], e_send.at[3], e_recv.at[0], sibling).wait_send()
    remote(e1_in.at[pl.ds(1, N_DP - 1)], e1_in.at[pl.ds(1, N_DP - 1)], e_send.at[4], e_recv.at[0], sibling).wait_send()
    remote(esib, esib, e_send.at[0], e_recv.at[0], sibling).wait_send()
    remote(esib, esib, e_send.at[5], e_recv.at[0], sibling).wait_send()


def write_kernel(u_ref, n_ref, ge_ref, gl_ref, upd_ref, gn_ref, gq_ref, gk_ref, gr_ref, gd_ref):
    upd_ref[...] = u_ref[...]
    gn_ref[...] = n_ref[...]
    for degree in range(EARLY):
        gr_ref[:, degree * C : (degree + 1) * C] = ge_ref[2 * degree * C : (2 * degree + 1) * C].astype(F32)
        gd_ref[degree] = ge_ref[(2 * degree + 1) * C : (2 * degree + 2) * C].astype(F32)
    gq_ref[...] = gl_ref[0:C].astype(F32)
    gk_ref[...] = gl_ref[C : 2 * C].astype(F32)
    for i in range(LATE_DEGREES):
        degree = EARLY + i
        gr_ref[:, degree * C : (degree + 1) * C] = gl_ref[(2 + 2 * i) * C : (3 + 2 * i) * C].astype(F32)
        gd_ref[degree] = gl_ref[(3 + 2 * i) * C : (4 + 2 * i) * C].astype(F32)


def on_device(node_feat, radial, src_node, dst_node, w_query, w_key, w_radial, w_degree, cotangent):
    vmem = pl.BlockSpec(memory_space=pltpu.VMEM)
    dma = pltpu.SemaphoreType.DMA
    width = node_feat.shape[2]
    scratch = [
        pltpu.VMEM((2, HALF_PAIRS, PAD, 2 * C), BF16),
        pltpu.VMEM((HALF_PAIRS, PAD, 2 * C), BF16),
        pltpu.VMEM((2, HALF_PAIRS, NODES, 2 * C), BF16),
        pltpu.VMEM((N_GRAPH, PAD, C), BF16),
        pltpu.VMEM((NODES, C), BF16),
        pltpu.VMEM((EDGE_DEV, NODES), BF16),
        pltpu.VMEM((NODES, EDGE_DEV), BF16),
        pltpu.VMEM((EDGE_DEV, PAD), BF16),
        pltpu.VMEM((PAD, EDGE_DEV), BF16),
        pltpu.VMEM((2 * HALF_PAIRS, PAD, 2 * C), BF16),
        pltpu.VMEM((PAD, C), BF16),
        pltpu.VMEM((LEVELS, EDGE_DEV, C), F32),
        pltpu.VMEM((LEVELS, EDGE_DEV, C), F32),
        pltpu.VMEM((LEVELS, EDGE_DEV, C), F32),
        pltpu.VMEM((LEVELS, EDGE_DEV, C), F32),
        pltpu.VMEM((LEVELS * LEVELS, NODE_DEV, C), F32),
        pltpu.VMEM((EDGE_DEV, 2 * C), BF16),
        pltpu.VMEM((EDGE_DEV, 2 * C), BF16),
        pltpu.VMEM((2, HALF_PAIRS, NODES, 2 * C), BF16),
        pltpu.VMEM((HALF_PAIRS, NODES, 2 * C), BF16),
        pltpu.VMEM((3, HALF_PAIRS, CHIP_ROWS, 2 * C), BF16),
        pltpu.VMEM((4, HALF_PAIRS, CHIP_ROWS, 2 * C), BF16),
        pltpu.VMEM((HALF_PAIRS, CHIP_ROWS, 2 * C), F32),
        pltpu.VMEM((HALF_PAIRS, NODE_DEV, 2 * C), F32),
        pltpu.VMEM((N_GRAPH, PAD, C), BF16),
        pltpu.VMEM((N_GRAPH, PAD, C), BF16),
        pltpu.VMEM((LATE_ROWS, C), BF16),
        pltpu.VMEM((N_GRAPH, LATE_PIECE, C), BF16),
        pltpu.VMEM((N_DP, LATE_PIECE, C), BF16),
        pltpu.VMEM((LATE_ROWS, C), BF16),
        pltpu.VMEM((2 * EARLY_HALF, C), BF16),
        pltpu.VMEM((EARLY_HALF, C), BF16),
        pltpu.VMEM((N_DP, EARLY_PIECE, C), BF16),
        pltpu.VMEM((EARLY_PAD, C), BF16),
        pltpu.VMEM((N_CHIP, EARLY_SUB, C), BF16),
        pltpu.VMEM((EARLY_PAD, C), BF16),
        pltpu.VMEM((2 * EARLY_HALF, C), BF16),
        pltpu.VMEM((EDGE_DEV, C), F32),
        pltpu.VMEM((EDGE_DEV, C), F32),
        pltpu.VMEM((EDGE_DEV, C), F32),
        pltpu.VMEM((EDGE_DEV, C), BF16),
        pltpu.VMEM((EDGE_DEV, C), F32),
        pltpu.VMEM((C, EDGE_DEV), BF16),
        dma((2,)),
        dma((1,)),
        dma((1,)),
        dma((2,)),
        dma((CHUNKS, 3)),
        dma((3,)),
        dma((CHUNKS, 4)),
        dma((1,)),
        dma((1,)),
        dma((1,)),
        dma((1,)),
        dma((1,)),
        dma((1,)),
        dma((1,)),
        dma((1,)),
        dma((6,)),
        dma((6,)),
    ]
    updated, grad_node, early, late = pl.pallas_call(
        kernel,
        out_shape=(
            jax.ShapeDtypeStruct((NODE_DEV, width), BF16),
            jax.ShapeDtypeStruct((NODE_DEV, width), BF16),
            jax.ShapeDtypeStruct((2 * EARLY * C, C), BF16),
            jax.ShapeDtypeStruct((LATE_ROWS, C), BF16),
        ),
        in_specs=[vmem] * 9,
        out_specs=(vmem,) * 4,
        scratch_shapes=scratch,
        compiler_params=pltpu.CompilerParams(
            collective_id=0, has_side_effects=True, vmem_limit_bytes=60 << 20
        ),
    )(node_feat[0], radial[0], src_node, dst_node, w_query, w_key, w_radial, w_degree, cotangent[0])
    updated, grad_node, grad_query, grad_key, grad_radial, grad_degree = pl.pallas_call(
        write_kernel,
        out_shape=(
            jax.ShapeDtypeStruct((NODE_DEV, width), BF16),
            jax.ShapeDtypeStruct((NODE_DEV, width), BF16),
            jax.ShapeDtypeStruct((C, C), F32),
            jax.ShapeDtypeStruct((C, C), F32),
            jax.ShapeDtypeStruct((C, LEVELS * C), F32),
            jax.ShapeDtypeStruct((LEVELS, C, C), F32),
        ),
        in_specs=[vmem] * 4,
        out_specs=(vmem,) * 6,
        compiler_params=pltpu.CompilerParams(vmem_limit_bytes=60 << 20),
    )(updated, grad_node, early, late)
    return (updated[None], grad_node[None], grad_query, grad_key, grad_radial, grad_degree)


def solution(mesh):
    return jax.shard_map(
        on_device,
        mesh=mesh,
        in_specs=(
            P("dp", "graph", None),
            P("dp", "graph", None),
            P("dp", "graph"),
            P("dp", "graph"),
            P(),
            P(),
            P(),
            P(),
            P("dp", "graph", None),
        ),
        out_specs=(P("dp", "graph", None), P("dp", "graph", None), P(), P(), P(), P()),
        check_vma=False,
    )
```
